32 devices in a mesh: dp: 8 (over y, x, core), fsdp: 4 (over z).
Axes of the slice: x: 2, y: 2, z: 4, core: 2. Of those that a mesh axis runs over, the one named last changes fastest.
Arguments:
- hidden: bfloat16 [20480, 768], P(('dp', 'fsdp')), may hold values from -6 to 6
- encoded: bfloat16 [65536, 768], P(('dp', 'fsdp')), may hold values from -6 to 6
- out_grad: bfloat16 [20480, 768], P(('dp', 'fsdp')), may hold values from -6 to 6
- lengths: int32 [128], P(('dp', 'fsdp')), may hold values from 64 to 256, as said below
- group_ids: int32 [128], P(('dp', 'fsdp')), may hold values from 0 to 2
- id_tags: int32 [20480], P(('dp', 'fsdp')), may hold values 0 or 1
- loss_mask: int32 [20480], P(('dp', 'fsdp')), may hold values from 0 to 1
- group_steps: int32 [3], replicated, may hold values from 0 to 9999
- group_weights: int32 [3], replicated, may hold values from 1 to 4
- gain_self: bfloat16 [768], P('fsdp'), may hold values from 0.5 to 1.5
- gain_cross: bfloat16 [768], P('fsdp'), may hold values from 0.5 to 1.5
- gain_ffn: bfloat16 [768], P('fsdp'), may hold values from 0.5 to 1.5
- rel_bias: bfloat16 [12, 32], P('fsdp'), may hold values from -4 to 4
- query_weight: bfloat16 [768, 768], P('fsdp'), may hold values from -0.109375 to 0.109375
- key_weight: bfloat16 [768, 768], P('fsdp'), may hold values from -0.109375 to 0.109375
- value_weight: bfloat16 [768, 768], P('fsdp'), may hold values from -0.21875 to 0.21875
- output_weight: bfloat16 [768, 768], P('fsdp'), may hold values from -0.625 to 0.625
- cross_query: bfloat16 [768, 768], P('fsdp'), may hold values from -0.109375 to 0.109375
- cross_key: bfloat16 [768, 768], P('fsdp'), may hold values from -0.109375 to 0.109375
- cross_value: bfloat16 [768, 768], P('fsdp'), may hold values from -0.21875 to 0.21875
- cross_output: bfloat16 [768, 768], P('fsdp'), may hold values from -0.875 to 0.875
- expand_weight: bfloat16 [768, 3072], P('fsdp'), may hold values from -0.21875 to 0.21875
- reduce_weight: bfloat16 [3072, 768], P('fsdp'), may hold values from -0.15625 to 0.15625
Outputs:
- layer_output: bfloat16 [20480, 768], P(('dp', 'fsdp'))
- grad_hidden: float32 [20480, 768], P(('dp', 'fsdp'))
- grad_encoded: float32 [65536, 768], P(('dp', 'fsdp'))
- grad_gain_self: float32 [768], P('fsdp')
- grad_gain_cross: float32 [768], P('fsdp')
- grad_gain_ffn: float32 [768], P('fsdp')
- grad_rel_bias: float32 [12, 32], P('fsdp')
- grad_query_weight: float32 [768, 768], P('fsdp')
- grad_key_weight: float32 [768, 768], P('fsdp')
- grad_value_weight: float32 [768, 768], P('fsdp')
- grad_output_weight: float32 [768, 768], P('fsdp')
- grad_cross_query: float32 [768, 768], P('fsdp')
- grad_cross_key: float32 [768, 768], P('fsdp')
- grad_cross_value: float32 [768, 768], P('fsdp')
- grad_cross_output: float32 [768, 768], P('fsdp')
- grad_expand_weight: float32 [768, 3072], P('fsdp')
- grad_reduce_weight: float32 [3072, 768], P('fsdp')
The draws below stay inside these ranges and needn't reach their ends.
Inputs may be any that keep to these rules, and one draw needn't show every extreme that they name: `lengths`: entries b * 4 to (b + 1) * 4 - 1 are the sequences of device b of dp+fsdp and sum to 640; in each such block exactly one length is 256.
All inputs are finite; a program needn't handle non-finite values. No bound on the sum of `id_tags` on one device may be relied on, other than what follows from the above.
Results may differ from the reference program's by a relative error of at most 0.022.
The reference program's roundings to bfloat16 on the way count: a program that leaves them out, or rounds other values in their place, can miss the bound.
Values may be sent and summed in bfloat16 or wider, within the bound.
No kernel may reach another device: no remote copies, remote signals or barrier semaphores. Data moves between devices by JAX's collectives and lax.ppermute only.
A program may use at most 256 MiB of HBM per device.

```python
import math
import jax
import jax.numpy as jnp
from jax import lax

D = 768
HEADS = 12
HEAD = 64
FF = 3072
BUCKETS = 32
MAX_DIST = 128
ENC_LEN = 512
MAX_LEN = 256
GROUPS = 3
HORIZON = 10000
SEQ_DEV = 4
MIN_LEN = 64
TOK_DEV = 640
SHARDS = 32
SEQS = 128
TOKENS = 20480
ENC_ROWS = 65536


def draw_lengths(key, part):
    key = jax.random.fold_in(key, 11)
    half = MAX_LEN // 2
    spare = half - MIN_LEN
    others = SEQ_DEV - 1
    row_keys = jax.random.split(key, SHARDS)

    def one_device(row_key):
        first, second = jax.random.split(row_key)
        longest = jnp.full((1,), MAX_LEN, jnp.int32)
        if others > 0:
            moves = jax.random.randint(first, (others,), 0, spare + 1).astype(jnp.int32)
            if others > 1:
                moves = moves.at[0].set(0).at[1].set(spare)
            rest = (half + moves - jnp.roll(moves, -1)).astype(jnp.int32)
            lined = jnp.concatenate([rest, longest])
        else:
            lined = longest
        return jax.random.permutation(second, lined)
    return jax.vmap(one_device)(row_keys).reshape(SEQS).astype(jnp.int32)


def draw_loss_mask(key, part):
    key = jax.random.fold_in(key, 23)
    first, second = jax.random.split(key)
    span = MAX_LEN // 8
    levels = jax.random.randint(first, (TOKENS // span,), 0, 5).astype(jnp.int32)
    spread = jnp.repeat(jnp.left_shift(jnp.ones_like(levels), levels), span)
    picks = jax.random.randint(second, (TOKENS,), 0, spread)
    return (picks == 0).astype(jnp.int32)


def touch_ends(values, rng, smallest, top_value):
    spot = [jax.random.randint(jax.random.fold_in(rng, axis), (), 0, length) for axis, length in enumerate(values.shape)]
    widest = values.shape.index(max(values.shape))
    next_to = spot[:widest] + [(spot[widest] + 1) % values.shape[widest]] + spot[widest + 1:]
    return values.at[tuple(spot)].set(smallest).at[tuple(next_to)].set(top_value)


def shard_levels(stream_key, extent, cuts, least, largest):
    factor_of, own = 1.0, jax.random.fold_in(stream_key, 6)
    for dim, shards_of in cuts:
        heights = jnp.exp(jax.random.uniform(jax.random.fold_in(own, dim), (shards_of,), jnp.float32, least / len(cuts), largest / len(cuts)))
        factor_of = factor_of * jnp.repeat(heights, extent[dim] // shards_of).reshape([-1 if axis == dim else 1 for axis in range(len(extent))])
    return factor_of


def gaussian(key, shape, width, most, shards=(), kind=jnp.bfloat16):
    factor_of = shard_levels(key, shape, shards, -0.22, 0.18) if shards else 1.0
    values = jax.random.normal(key, shape, jnp.float32) * width * factor_of
    return jnp.minimum(jnp.maximum(values, -most), most).astype(kind)


def setup_inputs(seed: int = 0) -> dict:
    streams_of = jax.random.split(jax.random.key(seed), 24)
    return {
        "hidden": gaussian(streams_of[0], (TOKENS, D), 1.0, 6.0, ((0, 32),)),
        "encoded": gaussian(streams_of[1], (ENC_ROWS, D), 1.0, 6.0, ((0, 32),)),
        "out_grad": gaussian(streams_of[2], (TOKENS, D), 1.0, 6.0, ((0, 32),)),
        "lengths": draw_lengths(jax.random.fold_in(streams_of[23], 71), 0),
        "group_ids": touch_ends(jax.random.randint(streams_of[4], (SEQS,), 0, GROUPS), jax.random.fold_in(streams_of[4], 1), 0, GROUPS - 1).astype(jnp.int32),
        "id_tags": touch_ends((jax.random.randint(streams_of[5], (TOKENS,), 0, 4) < 1).astype(jnp.int32), jax.random.fold_in(streams_of[5], 1), 0, 1),
        "loss_mask": draw_loss_mask(jax.random.fold_in(streams_of[23], 71), 0),
        "group_steps": jax.random.randint(streams_of[7], (GROUPS,), 0, HORIZON).astype(jnp.int32),
        "group_weights": jax.random.randint(streams_of[8], (GROUPS,), 1, 5).astype(jnp.int32),
        "gain_self": jnp.clip(1.0 + 0.1 * jax.random.normal(streams_of[9], (D,), jnp.float32), 0.5, 1.5).astype(jnp.bfloat16),
        "gain_cross": jnp.clip(1.0 + 0.1 * jax.random.normal(streams_of[10], (D,), jnp.float32), 0.5, 1.5).astype(jnp.bfloat16),
        "gain_ffn": jnp.clip(1.0 + 0.1 * jax.random.normal(streams_of[11], (D,), jnp.float32), 0.5, 1.5).astype(jnp.bfloat16),
        "rel_bias": gaussian(streams_of[12], (HEADS, BUCKETS), 1.0, 4.0, ((0, 4),)),
        "query_weight": gaussian(streams_of[13], (D, D), (4 * D) ** -0.5, 0.109375, ((0, 4),)),
        "key_weight": gaussian(streams_of[14], (D, D), (4 * D) ** -0.5, 0.109375, ((0, 4),)),
        "value_weight": gaussian(streams_of[15], (D, D), D ** -0.5, 0.21875, ((0, 4),)),
        "output_weight": gaussian(streams_of[16], (D, D), (D // 8) ** -0.5, 0.625, ((0, 4),)),
        "cross_query": gaussian(streams_of[17], (D, D), (4 * D) ** -0.5, 0.109375, ((0, 4),)),
        "cross_key": gaussian(streams_of[18], (D, D), (4 * D) ** -0.5, 0.109375, ((0, 4),)),
        "cross_value": gaussian(streams_of[19], (D, D), D ** -0.5, 0.21875, ((0, 4),)),
        "cross_output": gaussian(streams_of[20], (D, D), (D // 16) ** -0.5, 0.875, ((0, 4),)),
        "expand_weight": gaussian(streams_of[21], (D, FF), D ** -0.5, 0.21875, ((0, 4),)),
        "reduce_weight": gaussian(streams_of[22], (FF, D), (FF // 2) ** -0.5, 0.15625, ((0, 4),)),
    }


epsilon = 1e-06
masked_score = -1000000000.0
highest = lax.Precision.HIGHEST

@jax.custom_vjp
def low(v):
    return lax.optimization_barrier(v.astype(jnp.bfloat16)).astype(jnp.float32)

@jax.custom_vjp
def low_back(v):
    return v

def low_keep(v):
    return (low(v), None)

def low_pass(kept, grad):
    return (grad,)

def back_keep(v):
    return (v, None)

def back_low(kept, grad):
    return (low(grad),)
low.defvjp(low_keep, low_pass)
low_back.defvjp(back_keep, back_low)

def bucket_of(distance):
    exact = BUCKETS // 2
    bucket = jnp.minimum(distance, exact)
    for step in range(1, exact):
        edge = math.ceil(exact * (MAX_DIST / exact) ** (step / exact))
        bucket = bucket + (distance >= edge).astype(jnp.int32)
    return bucket.astype(jnp.int32)

def segments_of(lengths, rows):
    positions = jnp.arange(rows, dtype=jnp.int32)
    starts = (jnp.cumsum(lengths) - lengths).astype(jnp.int32)
    segment = lax.optimization_barrier(jnp.sum((positions[:, None] >= starts[None, :]).astype(jnp.int32), axis=1)).astype(jnp.int32) - 1
    return (positions, starts, segment)

def token_weights(lengths, group_ids, id_tags, loss_mask, group_steps, group_weights):
    positions, starts, segment = segments_of(lengths, id_tags.shape[0])
    member = segment[:, None] == jnp.arange(lengths.shape[0], dtype=jnp.int32)[None, :]
    group_of = lax.optimization_barrier(jnp.sum(jnp.where(member, group_ids[None, :], 0), axis=1)).astype(jnp.int32)
    factor = group_weights.astype(jnp.float32) * 0.25 * (1.0 - group_steps.astype(jnp.float32) / (2.0 * HORIZON))
    chosen = group_of[:, None] == jnp.arange(GROUPS, dtype=jnp.int32)[None, :]
    scale = lax.optimization_barrier(jnp.sum(jnp.where(chosen, factor[None, :], 0.0), axis=1))
    counted = jnp.where(group_of == 1, id_tags, loss_mask).astype(jnp.float32)
    return scale * (0.25 + 0.75 * counted)

def norm_rows(rows, gain):
    scale = lax.rsqrt(lax.optimization_barrier(jnp.mean(rows * rows, axis=-1, keepdims=True)) + epsilon)
    return rows * scale * gain

def heads_of(matrix):
    return matrix.reshape(matrix.shape[0], HEADS, HEAD)

def attend(query, keys, values, extra, allowed):
    raw = low_back(jnp.einsum('qhd,khd->hqk', query, keys, precision=highest))
    scores = jnp.where(allowed, raw + extra, masked_score)
    top = lax.optimization_barrier(jnp.max(scores, axis=-1, keepdims=True))
    powers = jnp.exp(scores - top)
    probs = powers / lax.optimization_barrier(jnp.sum(powers, axis=-1, keepdims=True))
    mixed = jnp.einsum('hqk,khe->qhe', low(probs), values, precision=highest)
    return mixed.reshape(mixed.shape[0], HEADS * HEAD)

def layer(hidden, encoded, params, lengths):
    query_weight, key_weight, value_weight, output_weight, cross_query, cross_key, cross_value, cross_output, expand_weight, reduce_weight, gain_self, gain_cross, gain_ffn, rel_bias = params
    rows = hidden.shape[0]
    positions, starts, segment = segments_of(lengths, rows)
    lag = positions[:, None] - positions[None, :]
    allowed = ((segment[:, None] == segment[None, :]) & (lag >= 0))[None]
    extra = rel_bias[:, bucket_of(jnp.maximum(lag, 0))]
    normed = low(norm_rows(hidden, gain_self))
    query = low_back(low(jnp.dot(normed, query_weight, precision=highest)))
    keys = low_back(low(jnp.dot(normed, key_weight, precision=highest)))
    values = low_back(low(jnp.dot(normed, value_weight, precision=highest)))
    mixed = low_back(low(attend(heads_of(query), heads_of(keys), heads_of(values), extra, allowed)))
    hidden_one = hidden + low_back(jnp.dot(mixed, output_weight, precision=highest))
    normed = low(norm_rows(hidden_one, gain_cross))
    cross_q = low_back(low(jnp.dot(normed, cross_query, precision=highest)))
    cross_k = low_back(low(jnp.dot(encoded, cross_key, precision=highest)))
    cross_v = low_back(low(jnp.dot(encoded, cross_value, precision=highest)))
    source = (jnp.arange(encoded.shape[0], dtype=jnp.int32) // ENC_LEN).astype(jnp.int32)
    linked = (segment[:, None] == source[None, :])[None]
    mixed = low_back(low(attend(heads_of(cross_q), heads_of(cross_k), heads_of(cross_v), 0.0, linked)))
    hidden_two = hidden_one + low_back(jnp.dot(mixed, cross_output, precision=highest))
    normed = low(norm_rows(hidden_two, gain_ffn))
    expanded = low_back(jnp.dot(normed, expand_weight, precision=highest))
    activated = low(jax.nn.gelu(expanded, approximate=False))
    return hidden_two + low_back(jnp.dot(activated, reduce_weight, precision=highest))

def reference(hidden, encoded, out_grad, lengths, group_ids, id_tags, loss_mask, group_steps, group_weights, gain_self, gain_cross, gain_ffn, rel_bias, query_weight, key_weight, value_weight, output_weight, cross_query, cross_key, cross_value, cross_output, expand_weight, reduce_weight):
    params = tuple((item.astype(jnp.float32) for item in (query_weight, key_weight, value_weight, output_weight, cross_query, cross_key, cross_value, cross_output, expand_weight, reduce_weight, gain_self, gain_cross, gain_ffn, rel_bias)))
    blocks = (hidden.reshape(SHARDS, TOK_DEV, D), encoded.reshape(SHARDS, SEQ_DEV * ENC_LEN, D), out_grad.reshape(SHARDS, TOK_DEV, D), lengths.reshape(SHARDS, SEQ_DEV), group_ids.reshape(SHARDS, SEQ_DEV), id_tags.reshape(SHARDS, TOK_DEV), loss_mask.reshape(SHARDS, TOK_DEV))

    def block_step(totals, items):
        block_hidden, block_encoded, block_grad, block_lengths, block_groups, block_tags, block_mask = items

        def forward(inner_hidden, inner_encoded, inner_params):
            return layer(inner_hidden, inner_encoded, inner_params, block_lengths)
        result, pull = jax.vjp(forward, block_hidden.astype(jnp.float32), block_encoded.astype(jnp.float32), params)
        weight_rows = token_weights(block_lengths, block_groups, block_tags, block_mask, group_steps, group_weights)
        grad_rows, grad_source, grad_params = pull(block_grad.astype(jnp.float32) * weight_rows[:, None])
        totals = jax.tree.map(jnp.add, totals, grad_params)
        return (totals, (result.astype(jnp.bfloat16), grad_rows, grad_source))
    zeros = jax.tree.map(jnp.zeros_like, params)
    totals, (output, grad_rows, grad_source) = lax.scan(block_step, zeros, blocks)
    return (output.reshape(TOKENS, D), grad_rows.reshape(TOKENS, D), grad_source.reshape(ENC_ROWS, D), totals[10], totals[11], totals[12], totals[13], totals[0], totals[1], totals[2], totals[3], totals[4], totals[5], totals[6], totals[7], totals[8], totals[9])
```

```python
from functools import partial
import math

import jax
import jax.numpy as jnp
import numpy as np
from jax import lax
from jax.experimental import pallas as pl
from jax.experimental.pallas import tpu as pltpu
from jax.sharding import PartitionSpec as P

HEADS = 12
HEAD = 64
PAIRS = 6
BUCKETS = 32
MAX_DIST = 128
ENC_LEN = 512
MAX_LEN = 256
GROUPS = 3
HORIZON = 10000
D = 768
COLS = 256

f32 = jnp.float32
bf16 = jnp.bfloat16
epsilon = 1e-06
masked_score = -1000000000.0

VMEM = pl.BlockSpec(memory_space=pltpu.VMEM)
SMEM = pl.BlockSpec(memory_space=pltpu.SMEM)
LIMIT = 60 * 1024 * 1024


def dot(left, right):
    return jnp.dot(left, right, preferred_element_type=f32)


def dot_nt(left, right):
    return lax.dot_general(left, right, (((1,), (1,)), ((), ())), preferred_element_type=f32)


def dot_tn(left, right):
    return lax.dot_general(left, right, (((0,), (0,)), ((), ())), preferred_element_type=f32)


def rounded(value):
    return value.astype(bf16).astype(f32)


def row_scale(rows):
    return lax.rsqrt(jnp.mean(rows * rows, axis=-1, keepdims=True) + epsilon)


def row_blocks(rows):
    return [slice(r, r + 128) for r in range(0, rows, 128)]


def col_blocks(width=D):
    return [slice(c, c + COLS) for c in range(0, width, COLS)]


def starts_of(len_ref):
    starts = [0]
    for s in range(3):
        starts.append(starts[-1] + len_ref[s])
    return starts


def norm_back(grad, rows, gain):
    r = row_scale(rows)
    pulled = gain * grad
    inner = jnp.mean(pulled * rows, axis=-1, keepdims=True)
    return r * pulled - rows * (r * r * r * inner), grad * rows * r


def split_three(value):
    high = value.astype(bf16)
    rest = value - high.astype(f32)
    mid = rest.astype(bf16)
    return high, mid, (rest - mid.astype(f32)).astype(bf16)


def weight_of(ref, index):
    return ref[:, index].reshape(D, D)


def weight_cols(ref, index, cols):
    return ref[:, index, :, cols].reshape(D, COLS)


def put_pairs(dst, cb, value):
    first = cb.start // 128
    dst[first, 0:value.shape[0], :] = value[:, :128]
    dst[first + 1, 0:value.shape[0], :] = value[:, 128:]


def clear_tail(dst, rows):
    dst[:, rows:, :] = jnp.zeros((PAIRS, dst.shape[1] - rows, 128), f32)


def join_pairs(dst, src, rows):
    for hp in range(PAIRS):
        dst[:, hp * 128:hp * 128 + 128] = src[hp, 0:rows, :].astype(dst.dtype)


def lane_index(rows):
    return lax.broadcasted_iota(jnp.int32, (rows, 128), 1)


def self_forward(len_ref, hid_ref, gain1_ref, gain2_ref, lag_ref, u_ref,
                 n1_ref, q_ref, k_ref, v_ref, lse_ref, mixed_ref, h1_ref, n2_ref,
                 q_s, k_s, v_s, m_s, bias_s):
    rows = hid_ref.shape[0]
    count = q_ref.shape[0]
    for rb in row_blocks(rows):
        x = hid_ref[rb, :].astype(f32)
        n1_ref[rb, :] = (x * row_scale(x) * gain1_ref[...]).astype(bf16)
    for w, dst in enumerate((q_s, k_s, v_s)):
        for cb in col_blocks():
            put_pairs(dst, cb, rounded(dot(n1_ref[...], weight_cols(u_ref, w, cb))))
        clear_tail(dst, rows)
    starts = starts_of(len_ref)
    row = lax.broadcasted_iota(jnp.int32, (MAX_LEN, MAX_LEN), 0)
    col = lax.broadcasted_iota(jnp.int32, (MAX_LEN, MAX_LEN), 1)
    lane = lane_index(MAX_LEN)
    even = lane < HEAD

    def pair(hp, carry):
        cols = pl.ds(pl.multiple_of(hp * 128, 128), 128)
        for e in range(2):
            w = jnp.broadcast_to(lag_ref[pl.ds(2 * hp + e, 1), :], (MAX_LEN, MAX_LEN))
            table = pltpu.roll(w, 0, 1, stride=1, stride_axis=0)
            bias_s[e] = jnp.where(row >= col, table, masked_score)
        for s in range(count):
            window = pl.ds(starts[s], MAX_LEN)
            q = q_s[hp, window, :].astype(bf16)
            k = k_s[hp, window, :].astype(bf16)
            v = v_s[hp, window, :].astype(bf16)
            q_ref[s, :, cols] = q
            k_ref[s, :, cols] = k
            v_ref[s, :, cols] = v
            res, tops = [], []
            for e in range(2):
                mine = even if e == 0 else ~even
                score = dot_nt(jnp.where(mine, q, 0), k) + bias_s[e]
                top = jnp.max(score, axis=-1, keepdims=True)
                p = jnp.exp(score - top).astype(bf16)
                res.append(dot(p, jnp.where(mine, v, 1)))
                tops.append(top)
            num = jnp.where(even, res[0], res[1])
            den = jnp.where(even, pltpu.roll(res[0], HEAD, 1), pltpu.roll(res[1], HEAD, 1))
            lse_ref[s, :, cols] = jnp.where(even, tops[0], tops[1]) + jnp.log(den)
            m_s[hp, window, :] = num / den
        return carry

    lax.fori_loop(0, PAIRS, pair, 0)
    join_pairs(mixed_ref, m_s, rows)
    for cb in col_blocks():
        h1_ref[:, cb] = hid_ref[:, cb].astype(f32) + dot(mixed_ref[...], weight_cols(u_ref, 3, cb))
    for rb in row_blocks(rows):
        x = h1_ref[rb, :]
        n2_ref[rb, :] = (x * row_scale(x) * gain2_ref[...]).astype(bf16)


def cross_forward(len_ref, n2_ref, h1_ref, gain3_ref, enc_ref, u_ref,
                  ck_ref, cv_ref, cq_ref, lse_ref, crossed_ref, h2_ref, n3_ref,
                  q_s, m_s):
    s = pl.program_id(0)
    rows = n2_ref.shape[0]
    count = pl.num_programs(0)

    @pl.when(s == 0)
    def _():
        for cb in col_blocks():
            put_pairs(q_s, cb, rounded(dot(n2_ref[...], weight_cols(u_ref, 0, cb))))
        clear_tail(q_s, rows)

    for cb in col_blocks():
        ck_ref[:, cb] = dot(enc_ref[...], weight_cols(u_ref, 1, cb)).astype(bf16)
        cv_ref[:, cb] = dot(enc_ref[...], weight_cols(u_ref, 2, cb)).astype(bf16)
    start = 0
    for t in range(3):
        start = start + jnp.where(s > t, len_ref[t], 0)
    window = pl.ds(start, MAX_LEN)
    even = lane_index(MAX_LEN) < HEAD
    even_v = lane_index(ENC_LEN) < HEAD

    def pair(hp, carry):
        cols = pl.ds(pl.multiple_of(hp * 128, 128), 128)
        q = q_s[hp, window, :].astype(bf16)
        cq_ref[0, :, cols] = q
        k = ck_ref[:, cols]
        v = cv_ref[:, cols]
        res, tops = [], []
        for e in range(2):
            mine = even if e == 0 else ~even
            mine_v = even_v if e == 0 else ~even_v
            score = dot_nt(jnp.where(mine, q, 0), k)
            top = jnp.max(score, axis=-1, keepdims=True)
            p = jnp.exp(score - top).astype(bf16)
            res.append(dot(p, jnp.where(mine_v, v, 1)))
            tops.append(top)
        num = jnp.where(even, res[0], res[1])
        den = jnp.where(even, pltpu.roll(res[0], HEAD, 1), pltpu.roll(res[1], HEAD, 1))
        lse_ref[0, :, cols] = jnp.where(even, tops[0], tops[1]) + jnp.log(den)
        m_s[hp, window, :] = num / den
        return carry

    lax.fori_loop(0, PAIRS, pair, 0)

    @pl.when(s == count - 1)
    def _():
        join_pairs(crossed_ref, m_s, rows)
        for cb in col_blocks():
            h2_ref[:, cb] = h1_ref[:, cb] + dot(crossed_ref[...], weight_cols(u_ref, 3, cb))
        for rb in row_blocks(rows):
            x = h2_ref[rb, :]
            n3_ref[rb, :] = (x * row_scale(x) * gain3_ref[...]).astype(bf16)


def gelu_parts(x):
    decay = jnp.exp(-0.5 * (x * x))
    t = 1.0 / (1.0 + jnp.abs(x) * (0.3275911 / math.sqrt(2.0)))
    poly = t * (0.5 * 0.254829592 + t * (-0.5 * 0.284496736 + t * (
        0.5 * 1.421413741 + t * (-0.5 * 1.453152027 + t * (0.5 * 1.061405429)))))
    tail = poly * decay
    below = jnp.where(x >= 0, 1.0 - tail, tail)
    return x * below, below + x * decay * (1.0 / math.sqrt(2.0 * math.pi))


def feed_forward(len_ref, group_ref, step_ref, weight_ref, tags_ref, mask_ref, og_ref, n3_ref,
                 h2_ref, gain3_ref, x_ref, r_ref,
                 out_ref, gx_ref, gr_ref, g2_ref, gg_ref,
                 scaled_s, out_s, dn_s, act_s, de_s):
    g = pl.program_id(0)
    rows = n3_ref.shape[0]

    def token_weight(rb):
        index = lax.broadcasted_iota(jnp.int32, (128, 1), 0) + rb.start
        scale = jnp.zeros((128, 1), f32)
        tagged = jnp.zeros((128, 1), jnp.int32)
        start = 0
        for s in range(4):
            group = group_ref[s]
            factor = jnp.float32(0.0)
            for k in range(GROUPS):
                value = weight_ref[k].astype(f32) * 0.25 * (
                    1.0 - step_ref[k].astype(f32) * (1.0 / (2.0 * HORIZON)))
                factor = jnp.where(group == k, value, factor)
            inside = index >= start
            scale = jnp.where(inside, factor, scale)
            tagged = jnp.where(inside, jnp.where(group == 1, 1, 0), tagged)
            start = start + len_ref[s]
        counted = jnp.where(tagged == 1, tags_ref[rb, :], mask_ref[rb, :]).astype(f32)
        return scale * (0.25 + 0.75 * counted)

    @pl.when(g == 0)
    def _():
        for rb in row_blocks(rows):
            scaled = og_ref[rb, :].astype(f32) * token_weight(rb)
            g2_ref[rb, :] = scaled
            scaled_s[rb, :] = scaled.astype(bf16)
        out_s[...] = h2_ref[...]
        dn_s[...] = jnp.zeros(dn_s.shape, f32)

    for cb in col_blocks():
        expanded = dot(n3_ref[...], x_ref[:, 0, :, cb].reshape(D, COLS))
        act, slope = gelu_parts(expanded)
        act_s[:, cb] = act.astype(bf16)
        back = dot_nt(scaled_s[...], r_ref[0, cb, :])
        de_s[:, cb] = (back * slope).astype(bf16)
    for cb in col_blocks():
        out_s[:, cb] += dot(act_s[...], r_ref[0, :, cb])
        gx_ref[:, 0, :, cb] = dot_tn(n3_ref[...], de_s[:, cb]).astype(bf16).reshape(4, D // 4, COLS)
        gr_ref[0, :, cb] = dot_tn(act_s[...], scaled_s[:, cb]).astype(bf16)
    full = x_ref[:, 0].reshape(D, D)
    for cb in col_blocks():
        dn_s[:, cb] += dot_nt(de_s[...], full[cb, :])

    @pl.when(g == pl.num_programs(0) - 1)
    def _():
        total = jnp.zeros((1, D), f32)
        for rb in row_blocks(rows):
            out_ref[rb, :] = out_s[rb, :].astype(bf16)
            part, pulled = norm_back(dn_s[rb, :], h2_ref[rb, :], gain3_ref[...])
            g2_ref[rb, :] += part
            total = total + jnp.sum(pulled, axis=0, keepdims=True)
        gg_ref[...] = total


def head_sums(product):
    a = lax.broadcasted_iota(jnp.int32, (128, 128), 0) < HEAD
    b = lax.broadcasted_iota(jnp.int32, (128, 128), 1) < HEAD
    ones = (a == b).astype(bf16)
    high, mid, rest = split_three(product)
    return dot(high, ones) + dot(mid, ones) + dot(rest, ones)


def augment(base, minus, lane, e):
    mine = (lane < HEAD) if e == 0 else (lane >= HEAD)
    spot = HEAD if e == 0 else 0
    high, mid, rest = split_three(-minus)
    extra = jnp.where(lane == spot, high, jnp.where(lane == spot + 1, mid, jnp.where(
        lane == spot + 2, rest, jnp.zeros_like(high))))
    return jnp.where(mine, base, extra)


def ones_beside(base, lane, e):
    mine = (lane < HEAD) if e == 0 else (lane >= HEAD)
    return jnp.where(mine, base, 1)


def other_half(value):
    return pltpu.roll(value, HEAD, 1)


def cross_backward(len_ref, g2_ref, crossed_ref, cq_ref, lse_ref, ck_ref, cv_ref, enc_ref, n2_ref,
                   h1_ref, gain2_ref, u_ref,
                   ge_ref, gu_ref, g1_ref, gg_ref,
                   dm_s, dd_s, dq_s, dk_s, dv_s, gk_s, gv_s, b2_s, dml_s, dn_s):
    s = pl.program_id(0)
    rows = g2_ref.shape[0]

    @pl.when(s == 0)
    def _():
        b2_s[...] = g2_ref[...].astype(bf16)
        full = weight_of(u_ref, 3)
        for cb in col_blocks():
            put_pairs(dm_s, cb, rounded(dot_nt(b2_s[...], full[cb, :])))
            gu_ref[:, 3, :, cb] = dot_tn(crossed_ref[...], b2_s[:, cb]).astype(bf16).reshape(
                4, D // 4, COLS)
        clear_tail(dm_s, rows)
        clear_tail(dd_s, rows)
        for hp in range(PAIRS):
            cols = slice(hp * 128, hp * 128 + 128)
            dd_s[hp, 0:rows, :] = head_sums(dm_s[hp, 0:rows, :] * crossed_ref[:, cols].astype(f32))
        gk_s[...] = jnp.zeros(gk_s.shape, f32)
        gv_s[...] = jnp.zeros(gv_s.shape, f32)

    start = 0
    length = len_ref[0]
    for t in range(3):
        start = start + jnp.where(s > t, len_ref[t], 0)
        length = jnp.where(s == t + 1, len_ref[t + 1], length)
    lane = lane_index(MAX_LEN)
    lane_k = lane_index(ENC_LEN)
    valid = lax.broadcasted_iota(jnp.int32, (MAX_LEN, 128), 0) < length
    window = pl.ds(start, MAX_LEN)

    def pair(hp, carry):
        cols = pl.ds(pl.multiple_of(hp * 128, 128), 128)
        q = cq_ref[0, :, cols]
        k = ck_ref[:, cols]
        v = cv_ref[:, cols]
        lse = other_half(lse_ref[0, :, cols])
        dm = jnp.where(valid, dm_s[hp, window, :], 0.0).astype(bf16)
        dd = other_half(jnp.where(valid, dd_s[hp, window, :], 0.0))
        dq = dk = dv = None
        for e in range(2):
            score = dot_nt(ones_beside(k, lane_k, e), augment(q, lse, lane, e))
            p = jnp.exp(score)
            back = dot_nt(ones_beside(v, lane_k, e), augment(dm, dd, lane, e))
            ds = (p * back).astype(bf16)
            mine = (lane < HEAD) if e == 0 else (lane >= HEAD)
            mine_k = (lane_k < HEAD) if e == 0 else (lane_k >= HEAD)
            dv_e = dot(p.astype(bf16), jnp.where(mine, dm, 0))
            dk_e = dot(ds, jnp.where(mine, q, 0))
            dq_e = dot_tn(ds, jnp.where(mine_k, k, 0))
            dq, dk, dv = (dq_e, dk_e, dv_e) if e == 0 else (dq + dq_e, dk + dk_e, dv + dv_e)
        dq_s[hp, window, :] = dq
        dk_s[:, cols] = dk.astype(bf16)
        dv_s[:, cols] = dv.astype(bf16)
        return carry

    lax.fori_loop(0, PAIRS, pair, 0)
    full_k = weight_of(u_ref, 1)
    full_v = weight_of(u_ref, 2)
    for cb in col_blocks():
        gk_s[:, cb] += dot_tn(enc_ref[...], dk_s[:, cb])
        gv_s[:, cb] += dot_tn(enc_ref[...], dv_s[:, cb])
        ge_ref[:, cb] = dot_nt(dk_s[...], full_k[cb, :]) + dot_nt(dv_s[...], full_v[cb, :])

    @pl.when(s == pl.num_programs(0) - 1)
    def _():
        join_pairs(dml_s, dq_s, rows)
        full_q = weight_of(u_ref, 0)
        for cb in col_blocks():
            gu_ref[:, 0, :, cb] = dot_tn(n2_ref[...], dml_s[:, cb]).astype(bf16).reshape(
                4, D // 4, COLS)
            gu_ref[:, 1, :, cb] = gk_s[:, cb].astype(bf16).reshape(4, D // 4, COLS)
            gu_ref[:, 2, :, cb] = gv_s[:, cb].astype(bf16).reshape(4, D // 4, COLS)
            dn_s[:, cb] = dot_nt(dml_s[...], full_q[cb, :])
        total = jnp.zeros((1, D), f32)
        for rb in row_blocks(rows):
            part, pulled = norm_back(dn_s[rb, :], h1_ref[rb, :], gain2_ref[...])
            g1_ref[rb, :] = g2_ref[rb, :] + part
            total = total + jnp.sum(pulled, axis=0, keepdims=True)
        gg_ref[...] = total


def diagonal_sums(ref):
    total = ref[0:8, :]
    for r in range(8, MAX_LEN, 8):
        total = total + pltpu.roll(ref[r:r + 8, :], MAX_LEN - r, 1)
    row = lax.broadcasted_iota(jnp.int32, (8, MAX_LEN), 0)
    for bit in (1, 2, 4):
        total = jnp.where((row & bit) != 0, pltpu.roll(total, MAX_LEN - bit, 1), total)
    return jnp.sum(total, axis=0, keepdims=True)


def self_backward(len_ref, g1_ref, mixed_ref, q_ref, k_ref, v_ref, lse_ref, n1_ref, hid_ref,
                  gain1_ref, lag_ref, u_ref,
                  gh_ref, gu_ref, gg_ref, gl_ref,
                  dm_s, dd_s, dq_s, dk_s, dv_s, b1_s, low_s, bias_s, acc_s, dn_s):
    rows = g1_ref.shape[0]
    count = q_ref.shape[0]
    b1_s[...] = g1_ref[...].astype(bf16)
    full = weight_of(u_ref, 3)
    for cb in col_blocks():
        put_pairs(dm_s, cb, rounded(dot_nt(b1_s[...], full[cb, :])))
        gu_ref[:, 3, :, cb] = dot_tn(mixed_ref[...], b1_s[:, cb]).astype(bf16).reshape(
            4, D // 4, COLS)
    clear_tail(dm_s, rows)
    clear_tail(dd_s, rows)
    for hp in range(PAIRS):
        cols = slice(hp * 128, hp * 128 + 128)
        dd_s[hp, 0:rows, :] = head_sums(dm_s[hp, 0:rows, :] * mixed_ref[:, cols].astype(f32))
    starts = starts_of(len_ref)
    row = lax.broadcasted_iota(jnp.int32, (MAX_LEN, MAX_LEN), 0)
    col = lax.broadcasted_iota(jnp.int32, (MAX_LEN, MAX_LEN), 1)
    lane = lane_index(MAX_LEN)
    index = lax.broadcasted_iota(jnp.int32, (MAX_LEN, 128), 0)

    def pair(hp, carry):
        cols = pl.ds(pl.multiple_of(hp * 128, 128), 128)
        for e in range(2):
            w = jnp.broadcast_to(lag_ref[pl.ds(2 * hp + e, 1), :], (MAX_LEN, MAX_LEN))
            table = pltpu.roll(w, 0, 1, stride=1, stride_axis=0)
            bias_s[e] = jnp.where(col >= row, table, masked_score)
        for s in range(count):
            valid = index < len_ref[s]
            window = pl.ds(starts[s], MAX_LEN)
            q = q_ref[s, :, cols]
            k = k_ref[s, :, cols]
            v = v_ref[s, :, cols]
            lse = other_half(lse_ref[s, :, cols])
            dm = jnp.where(valid, dm_s[hp, window, :], 0.0).astype(bf16)
            dd = other_half(jnp.where(valid, dd_s[hp, window, :], 0.0))
            dq = dk = dv = None
            for e in range(2):
                score = dot_nt(ones_beside(k, lane, e), augment(q, lse, lane, e)) + bias_s[e]
                p = jnp.exp(score)
                back = dot_nt(ones_beside(v, lane, e), augment(dm, dd, lane, e))
                grad = p * back
                if s == 0:
                    acc_s[e] = grad
                else:
                    acc_s[e] += grad
                ds = grad.astype(bf16)
                mine = (lane < HEAD) if e == 0 else (lane >= HEAD)
                dv_e = dot(p.astype(bf16), jnp.where(mine, dm, 0))
                dk_e = dot(ds, jnp.where(mine, q, 0))
                dq_e = dot_tn(ds, jnp.where(mine, k, 0))
                dq, dk, dv = (dq_e, dk_e, dv_e) if e == 0 else (dq + dq_e, dk + dk_e, dv + dv_e)
            dq_s[hp, window, :] = dq
            dk_s[hp, window, :] = dk
            dv_s[hp, window, :] = dv
        for e in range(2):
            gl_ref[pl.ds(2 * hp + e, 1), :] = diagonal_sums(acc_s.at[e])
        return carry

    lax.fori_loop(0, PAIRS, pair, 0)
    for w, src in enumerate((dq_s, dk_s, dv_s)):
        join_pairs(low_s, src, rows)
        full = weight_of(u_ref, w)
        for cb in col_blocks():
            gu_ref[:, w, :, cb] = dot_tn(n1_ref[...], low_s[:, cb]).astype(bf16).reshape(
                4, D // 4, COLS)
            part = dot_nt(low_s[...], full[cb, :])
            dn_s[:, cb] = part if w == 0 else dn_s[:, cb] + part
    total = jnp.zeros((1, D), f32)
    for rb in row_blocks(rows):
        part, pulled = norm_back(dn_s[rb, :], hid_ref[rb, :].astype(f32), gain1_ref[...])
        gh_ref[rb, :] = g1_ref[rb, :] + part
        total = total + jnp.sum(pulled, axis=0, keepdims=True)
    gg_ref[...] = total


def bucket_table():
    lags = np.arange(MAX_LEN)
    exact = BUCKETS // 2
    bucket = np.minimum(lags, exact)
    for step in range(1, exact):
        edge = math.ceil(exact * (MAX_DIST / exact) ** (step / exact))
        bucket = bucket + (lags >= edge)
    return (bucket[None, :] == np.arange(BUCKETS)[:, None]).astype(np.float32)


def shape(dims, kind):
    return jax.ShapeDtypeStruct(dims, kind)


def call(kernel, name, outs, ins, scratch, **extra):
    return pl.pallas_call(
        kernel,
        out_shape=list(outs),
        name=name,
        scratch_shapes=scratch,
        compiler_params=pltpu.CompilerParams(vmem_limit_bytes=LIMIT),
        **extra,
    )(*ins)


def whole(array_shape):
    zeros = (0,) * len(array_shape)
    return pl.BlockSpec(array_shape, lambda s: zeros)


def gather_unit(unit):
    parts = lax.axis_size("dp")
    size = D // parts
    piece = lax.dynamic_slice_in_dim(unit, lax.axis_index("dp") * size, size, 0)
    return lax.all_gather(piece, ("fsdp", "dp"), axis=0, tiled=True).reshape(4, 4, D // 4, D)


def reduce_unit(grads):
    return lax.psum_scatter(
        grads.reshape(4 * D, D), ("fsdp", "dp"), scatter_dimension=0, tiled=True)


def per_device(
    hidden, encoded, out_grad, lengths, group_ids, id_tags, loss_mask, group_steps, group_weights,
    gain_self, gain_cross, gain_ffn, rel_bias,
    query_weight, key_weight, value_weight, output_weight,
    cross_query, cross_key, cross_value, cross_output, expand_weight, reduce_weight,
):
    rows = hidden.shape[0]
    count = lengths.shape[0]
    quarter = D // 4
    u_self = gather_unit(jnp.concatenate([query_weight, key_weight, value_weight, output_weight], 0))
    small = jnp.concatenate([gain_self, gain_cross, gain_ffn, rel_bias.reshape(-1)])
    small = lax.all_gather(small[None], "fsdp", axis=0, tiled=True).astype(f32)
    u_cross = gather_unit(jnp.concatenate([cross_query, cross_key, cross_value, cross_output], 0))
    u_x = gather_unit(
        jnp.concatenate([expand_weight[:, g * D:(g + 1) * D] for g in range(4)], 0))
    u_r = gather_unit(reduce_weight)

    gain1 = small[:, 0:quarter].reshape(1, D)
    gain2 = small[:, quarter:2 * quarter].reshape(1, D)
    gain3 = small[:, 2 * quarter:3 * quarter].reshape(1, D)
    rel = small[:, 3 * quarter:].reshape(HEADS, BUCKETS)
    table = bucket_table()
    by_lag = jnp.dot(rel, jnp.asarray(table), precision=lax.Precision.HIGHEST)
    turned = jnp.dot(
        rel, jnp.asarray(table[:, (-np.arange(MAX_LEN)) % MAX_LEN]), precision=lax.Precision.HIGHEST)

    pad = rows + MAX_LEN
    wide = pltpu.VMEM((PAIRS, pad, 128), f32)
    heads = (count, MAX_LEN, D)
    n1, q, k, v, lse, mixed, h1, n2 = call(
        self_forward, "self_forward",
        (shape((rows, D), bf16), shape(heads, bf16), shape(heads, bf16), shape(heads, bf16),
         shape(heads, f32), shape((rows, D), bf16), shape((rows, D), f32), shape((rows, D), bf16)),
        (lengths, hidden, gain1, gain2, turned, u_self),
        [wide, wide, wide, wide, pltpu.VMEM((2, MAX_LEN, MAX_LEN), f32)],
        in_specs=[SMEM] + [VMEM] * 5, out_specs=[VMEM] * 8)

    enc_block = pl.BlockSpec((ENC_LEN, D), lambda s: (s, 0))
    seq_block = pl.BlockSpec((1, MAX_LEN, D), lambda s: (s, 0, 0))
    unit = whole((4, 4, quarter, D))
    full = whole((rows, D))
    line = whole((1, D))
    ck, cv, cq, cross_lse, crossed, h2, n3 = call(
        cross_forward, "cross_forward",
        (shape(encoded.shape, bf16), shape(encoded.shape, bf16), shape(heads, bf16),
         shape(heads, f32), shape((rows, D), bf16), shape((rows, D), f32), shape((rows, D), bf16)),
        (lengths, n2, h1, gain3, encoded, u_cross),
        [wide, wide],
        grid=(count,),
        in_specs=[SMEM, full, full, line, enc_block, unit],
        out_specs=[enc_block, enc_block, seq_block, seq_block, full, full, full])

    column = whole((rows, 1))
    x_block = pl.BlockSpec((4, 1, quarter, D), lambda g: (0, g, 0, 0))
    r_block = pl.BlockSpec((1, D, D), lambda g: (g, 0, 0))
    low = pltpu.VMEM((rows, D), bf16)
    flat = pltpu.VMEM((rows, D), f32)
    layer_output, grad_x, grad_r, g2, gg3 = call(
        feed_forward, "feed_forward",
        (shape((rows, D), bf16), shape((4, 4, quarter, D), bf16), shape((4, D, D), bf16),
         shape((rows, D), f32), shape((1, D), f32)),
        (lengths, group_ids, group_steps, group_weights, id_tags[:, None], loss_mask[:, None],
         out_grad, n3, h2, gain3, u_x, u_r.reshape(4, D, D)),
        [low, flat, flat, low, low],
        grid=(4,),
        in_specs=[SMEM] * 4 + [column, column, full, full, full, line, x_block, r_block],
        out_specs=[full, x_block, r_block, full, line])
    piece_x = reduce_unit(grad_x)
    piece_r = reduce_unit(grad_r)

    grad_encoded, grad_cross, g1, gg2 = call(
        cross_backward, "cross_backward",
        (shape(encoded.shape, f32), shape((4, 4, quarter, D), bf16), shape((rows, D), f32),
         shape((1, D), f32)),
        (lengths, g2, crossed, cq, cross_lse, ck, cv, encoded, n2, h1, gain2, u_cross),
        [wide, wide, wide, pltpu.VMEM((ENC_LEN, D), bf16), pltpu.VMEM((ENC_LEN, D), bf16),
         pltpu.VMEM((D, D), f32), pltpu.VMEM((D, D), f32), low, low, flat],
        grid=(count,),
        in_specs=[SMEM, full, full, seq_block, seq_block, enc_block, enc_block, enc_block, full,
                  full, line, unit],
        out_specs=[enc_block, unit, full, line])
    piece_cross = reduce_unit(grad_cross)

    grad_hidden, grad_self, gg1, grad_lag = call(
        self_backward, "self_backward",
        (shape((rows, D), f32), shape((4, 4, quarter, D), bf16), shape((1, D), f32),
         shape((HEADS, MAX_LEN), f32)),
        (lengths, g1, mixed, q, k, v, lse, n1, hidden, gain1, by_lag, u_self),
        [wide, wide, wide, wide, wide, low, low,
         pltpu.VMEM((2, MAX_LEN, MAX_LEN), f32), pltpu.VMEM((2, MAX_LEN, MAX_LEN), f32), flat],
        in_specs=[SMEM] + [VMEM] * 11, out_specs=[VMEM] * 4)
    piece_self = reduce_unit(grad_self)

    grad_rel = lax.dot_general(
        grad_lag, jnp.asarray(table), (((1,), (1,)), ((), ())), precision=lax.Precision.HIGHEST)
    small_grads = jnp.concatenate(
        [gg1.reshape(4, quarter), gg2.reshape(4, quarter), gg3.reshape(4, quarter),
         grad_rel.reshape(4, -1)], axis=1)
    small_total = lax.psum(small_grads, ("dp", "fsdp"))
    small_mine = lax.dynamic_slice_in_dim(small_total, lax.axis_index("fsdp"), 1, 0)[0]

    pieces = jnp.stack([piece_self, piece_cross, piece_x, piece_r])
    shards = lax.all_gather(pieces, "dp", axis=1, tiled=True).astype(f32)
    blocks = shards.reshape(4, 4, quarter, D)
    return (
        layer_output,
        grad_hidden,
        grad_encoded,
        small_mine[0:quarter],
        small_mine[quarter:2 * quarter],
        small_mine[2 * quarter:3 * quarter],
        small_mine[3 * quarter:].reshape(HEADS // 4, BUCKETS),
        blocks[0, 0],
        blocks[0, 1],
        blocks[0, 2],
        blocks[0, 3],
        blocks[1, 0],
        blocks[1, 1],
        blocks[1, 2],
        blocks[1, 3],
        jnp.concatenate([blocks[2, g] for g in range(4)], axis=1),
        shards[3],
    )


def solution(mesh):
    rows = P(("dp", "fsdp"), None)
    flat = P(("dp", "fsdp"))
    shard = P("fsdp", None)
    line = P("fsdp")
    return jax.shard_map(
        per_device,
        mesh=mesh,
        in_specs=(rows, rows, rows, flat, flat, flat, flat, P(), P(), line, line, line) + (shard,) * 11,
        out_specs=(rows, rows, rows, line, line, line) + (shard,) * 11,
        check_vma=False,
    )
```

```python
from functools import partial
import math

import jax
import jax.numpy as jnp
import numpy as np
from jax import lax
from jax.experimental import pallas as pl
from jax.experimental.pallas import tpu as pltpu
from jax.sharding import PartitionSpec as P

HEADS = 12
HEAD = 64
PAIRS = 6
BUCKETS = 32
MAX_DIST = 128
ENC_LEN = 512
MAX_LEN = 256
GROUPS = 3
HORIZON = 10000
D = 768
COLS = 256

f32 = jnp.float32
bf16 = jnp.bfloat16
epsilon = 1e-06
masked_score = -1000000000.0

VMEM = pl.BlockSpec(memory_space=pltpu.VMEM)
SMEM = pl.BlockSpec(memory_space=pltpu.SMEM)
ANY = pl.BlockSpec(memory_space=pl.ANY)
LIMIT = 60 * 1024 * 1024


def dot(left, right):
    return jnp.dot(left, right, preferred_element_type=f32)


def dot_nt(left, right):
    return lax.dot_general(left, right, (((1,), (1,)), ((), ())), preferred_element_type=f32)


def dot_tn(left, right):
    return lax.dot_general(left, right, (((0,), (0,)), ((), ())), preferred_element_type=f32)


def rounded(value):
    return value.astype(bf16).astype(f32)


def row_scale(rows):
    return lax.rsqrt(jnp.mean(rows * rows, axis=-1, keepdims=True) + epsilon)


def row_blocks(rows):
    return [slice(r, r + 128) for r in range(0, rows, 128)]


def col_blocks(width=D):
    return [slice(c, c + COLS) for c in range(0, width, COLS)]


def starts_of(len_ref):
    starts = [0]
    for s in range(3):
        starts.append(starts[-1] + len_ref[s])
    return starts


def norm_back(grad, rows, gain):
    r = row_scale(rows)
    pulled = gain * grad
    inner = jnp.mean(pulled * rows, axis=-1, keepdims=True)
    return r * pulled - rows * (r * r * r * inner), grad * rows * r


def split_three(value):
    high = value.astype(bf16)
    rest = value - high.astype(f32)
    mid = rest.astype(bf16)
    return high, mid, (rest - mid.astype(f32)).astype(bf16)


def weight_copies(core_ref, mine_ref, other_ref, w_s, sem):
    core = core_ref[0]
    quarter = D // 4
    copies = []
    for h, ref in enumerate((mine_ref, other_ref)):
        first = 2 * core if h == 0 else 2 * (1 - core)
        for z in range(4):
            copies.append(pltpu.make_async_copy(
                ref.at[z], w_s.at[pl.ds(first, 2), pl.ds(z * quarter, quarter), :],
                sem.at[4 * h + z]))
    return copies


def put_gradient(keep_ref, send_ref, core_ref, index, cb, value):
    value = value.astype(bf16).reshape(4, D // 4, COLS)
    stays = core_ref[0] == index // 2

    @pl.when(stays)
    def _():
        keep_ref[:, index % 2, :, cb] = value

    @pl.when(jnp.logical_not(stays))
    def _():
        send_ref[:, index % 2, :, cb] = value


def put_pairs(dst, cb, value):
    first = cb.start // 128
    dst[first, 0:value.shape[0], :] = value[:, :128]
    dst[first + 1, 0:value.shape[0], :] = value[:, 128:]


def clear_tail(dst, rows):
    dst[:, rows:, :] = jnp.zeros((PAIRS, dst.shape[1] - rows, 128), f32)


def join_pairs(dst, src, rows):
    for hp in range(PAIRS):
        dst[:, hp * 128:hp * 128 + 128] = src[hp, 0:rows, :].astype(dst.dtype)


def lane_index(rows):
    return lax.broadcasted_iota(jnp.int32, (rows, 128), 1)


def self_forward(len_ref, core_ref, hid_ref, gain1_ref, gain2_ref, lag_ref, um_ref, uo_ref,
                 n1_ref, q_ref, k_ref, v_ref, lse_ref, mixed_ref, h1_ref, n2_ref,
                 q_s, k_s, v_s, m_s, bias_s, w_s, sem):
    copies = weight_copies(core_ref, um_ref, uo_ref, w_s, sem)
    for copy in copies:
        copy.start()
    rows = hid_ref.shape[0]
    count = q_ref.shape[0]
    for rb in row_blocks(rows):
        x = hid_ref[rb, :].astype(f32)
        n1_ref[rb, :] = (x * row_scale(x) * gain1_ref[...]).astype(bf16)
    for copy in copies:
        copy.wait()
    for w, dst in enumerate((q_s, k_s, v_s)):
        for cb in col_blocks():
            put_pairs(dst, cb, rounded(dot(n1_ref[...], w_s[w, :, cb])))
        clear_tail(dst, rows)
    starts = starts_of(len_ref)
    row = lax.broadcasted_iota(jnp.int32, (MAX_LEN, MAX_LEN), 0)
    col = lax.broadcasted_iota(jnp.int32, (MAX_LEN, MAX_LEN), 1)
    lane = lane_index(MAX_LEN)
    even = lane < HEAD

    def pair(hp, carry):
        cols = pl.ds(pl.multiple_of(hp * 128, 128), 128)
        for e in range(2):
            w = jnp.broadcast_to(lag_ref[pl.ds(2 * hp + e, 1), :], (MAX_LEN, MAX_LEN))
            table = pltpu.roll(w, 0, 1, stride=1, stride_axis=0)
            bias_s[e] = jnp.where(row >= col, table, masked_score)
        for s in range(count):
            window = pl.ds(starts[s], MAX_LEN)
            q = q_s[hp, window, :].astype(bf16)
            k = k_s[hp, window, :].astype(bf16)
            v = v_s[hp, window, :].astype(bf16)
            q_ref[s, :, cols] = q
            k_ref[s, :, cols] = k
            v_ref[s, :, cols] = v
            res, tops = [], []
            for e in range(2):
                mine = even if e == 0 else ~even
                score = dot_nt(jnp.where(mine, q, 0), k) + bias_s[e]
                top = jnp.max(score, axis=-1, keepdims=True)
                p = jnp.exp(score - top).astype(bf16)
                res.append(dot(p, jnp.where(mine, v, 1)))
                tops.append(top)
            num = jnp.where(even, res[0], res[1])
            den = jnp.where(even, pltpu.roll(res[0], HEAD, 1), pltpu.roll(res[1], HEAD, 1))
            lse_ref[s, :, cols] = jnp.where(even, tops[0], tops[1]) + jnp.log(den)
            m_s[hp, window, :] = num / den
        return carry

    lax.fori_loop(0, PAIRS, pair, 0)
    join_pairs(mixed_ref, m_s, rows)
    for cb in col_blocks():
        h1_ref[:, cb] = hid_ref[:, cb].astype(f32) + dot(mixed_ref[...], w_s[3, :, cb])
    for rb in row_blocks(rows):
        x = h1_ref[rb, :]
        n2_ref[rb, :] = (x * row_scale(x) * gain2_ref[...]).astype(bf16)


def cross_forward(len_ref, core_ref, n2_ref, h1_ref, gain3_ref, enc_ref, um_ref, uo_ref,
                  ck_ref, cv_ref, cq_ref, lse_ref, crossed_ref, h2_ref, n3_ref,
                  q_s, m_s, w_s, sem):
    s = pl.program_id(0)
    rows = n2_ref.shape[0]
    count = pl.num_programs(0)

    @pl.when(s == 0)
    def _():
        copies = weight_copies(core_ref, um_ref, uo_ref, w_s, sem)
        for copy in copies:
            copy.start()
        for copy in copies:
            copy.wait()
        for cb in col_blocks():
            put_pairs(q_s, cb, rounded(dot(n2_ref[...], w_s[0, :, cb])))
        clear_tail(q_s, rows)

    for cb in col_blocks():
        ck_ref[:, cb] = dot(enc_ref[...], w_s[1, :, cb]).astype(bf16)
        cv_ref[:, cb] = dot(enc_ref[...], w_s[2, :, cb]).astype(bf16)
    start = 0
    for t in range(3):
        start = start + jnp.where(s > t, len_ref[t], 0)
    window = pl.ds(start, MAX_LEN)
    even = lane_index(MAX_LEN) < HEAD
    even_v = lane_index(ENC_LEN) < HEAD

    def pair(hp, carry):
        cols = pl.ds(pl.multiple_of(hp * 128, 128), 128)
        q = q_s[hp, window, :].astype(bf16)
        cq_ref[0, :, cols] = q
        k = ck_ref[:, cols]
        v = cv_ref[:, cols]
        res, tops = [], []
        for e in range(2):
            mine = even if e == 0 else ~even
            mine_v = even_v if e == 0 else ~even_v
            score = dot_nt(jnp.where(mine, q, 0), k)
            top = jnp.max(score, axis=-1, keepdims=True)
            p = jnp.exp(score - top).astype(bf16)
            res.append(dot(p, jnp.where(mine_v, v, 1)))
            tops.append(top)
        num = jnp.where(even, res[0], res[1])
        den = jnp.where(even, pltpu.roll(res[0], HEAD, 1), pltpu.roll(res[1], HEAD, 1))
        lse_ref[0, :, cols] = jnp.where(even, tops[0], tops[1]) + jnp.log(den)
        m_s[hp, window, :] = num / den
        return carry

    lax.fori_loop(0, PAIRS, pair, 0)

    @pl.when(s == count - 1)
    def _():
        join_pairs(crossed_ref, m_s, rows)
        for cb in col_blocks():
            h2_ref[:, cb] = h1_ref[:, cb] + dot(crossed_ref[...], w_s[3, :, cb])
        for rb in row_blocks(rows):
            x = h2_ref[rb, :]
            n3_ref[rb, :] = (x * row_scale(x) * gain3_ref[...]).astype(bf16)


def gelu_parts(x):
    decay = jnp.exp(-0.5 * (x * x))
    t = 1.0 / (1.0 + jnp.abs(x) * (0.3275911 / math.sqrt(2.0)))
    poly = t * (0.5 * 0.254829592 + t * (-0.5 * 0.284496736 + t * (
        0.5 * 1.421413741 + t * (-0.5 * 1.453152027 + t * (0.5 * 1.061405429)))))
    tail = poly * decay
    below = jnp.where(x >= 0, 1.0 - tail, tail)
    return x * below, below + x * decay * (1.0 / math.sqrt(2.0 * math.pi))


def feed_forward(len_ref, group_ref, step_ref, weight_ref, tags_ref, mask_ref, og_ref, n3_ref,
                 h2_ref, gain3_ref, x_ref, r_ref,
                 out_ref, gu_ref, g2_ref, gg_ref,
                 scaled_s, out_s, dn_s, act_s, de_s):
    g = pl.program_id(0)
    rows = n3_ref.shape[0]

    def token_weight(rb):
        index = lax.broadcasted_iota(jnp.int32, (128, 1), 0) + rb.start
        scale = jnp.zeros((128, 1), f32)
        tagged = jnp.zeros((128, 1), jnp.int32)
        start = 0
        for s in range(4):
            group = group_ref[s]
            factor = jnp.float32(0.0)
            for k in range(GROUPS):
                value = weight_ref[k].astype(f32) * 0.25 * (
                    1.0 - step_ref[k].astype(f32) * (1.0 / (2.0 * HORIZON)))
                factor = jnp.where(group == k, value, factor)
            inside = index >= start
            scale = jnp.where(inside, factor, scale)
            tagged = jnp.where(inside, jnp.where(group == 1, 1, 0), tagged)
            start = start + len_ref[s]
        counted = jnp.where(tagged == 1, tags_ref[rb, :], mask_ref[rb, :]).astype(f32)
        return scale * (0.25 + 0.75 * counted)

    @pl.when(g == 0)
    def _():
        for rb in row_blocks(rows):
            scaled = og_ref[rb, :].astype(f32) * token_weight(rb)
            g2_ref[rb, :] = scaled
            scaled_s[rb, :] = scaled.astype(bf16)
        out_s[...] = h2_ref[...]
        dn_s[...] = jnp.zeros(dn_s.shape, f32)

    for cb in col_blocks():
        expanded = dot(n3_ref[...], x_ref[:, 0, :, cb].reshape(D, COLS))
        act, slope = gelu_parts(expanded)
        act_s[:, cb] = act.astype(bf16)
        back = dot_nt(scaled_s[...], r_ref[0].reshape(D, D)[cb, :])
        de_s[:, cb] = (back * slope).astype(bf16)
    for cb in col_blocks():
        out_s[:, cb] += dot(act_s[...], r_ref[0, :, :, cb].reshape(D, COLS))
        gx = dot_tn(n3_ref[...], de_s[:, cb]).astype(bf16)
        gr = dot_tn(act_s[...], scaled_s[:, cb]).astype(bf16)
        gu_ref[g, :, :, cb] = gx.reshape(4, D // 4, COLS)
        for part in range(4):
            gu_ref[4 + part, g, :, cb] = gr[part * (D // 4):(part + 1) * (D // 4), :]
    full = x_ref[:, 0].reshape(D, D)
    for cb in col_blocks():
        dn_s[:, cb] += dot_nt(de_s[...], full[cb, :])

    @pl.when(g == pl.num_programs(0) - 1)
    def _():
        total = jnp.zeros((1, D), f32)
        for rb in row_blocks(rows):
            out_ref[rb, :] = out_s[rb, :].astype(bf16)
            part, pulled = norm_back(dn_s[rb, :], h2_ref[rb, :], gain3_ref[...])
            g2_ref[rb, :] += part
            total = total + jnp.sum(pulled, axis=0, keepdims=True)
        gg_ref[...] = total


def head_sums(product):
    a = lax.broadcasted_iota(jnp.int32, (128, 128), 0) < HEAD
    b = lax.broadcasted_iota(jnp.int32, (128, 128), 1) < HEAD
    ones = (a == b).astype(bf16)
    high, mid, rest = split_three(product)
    return dot(high, ones) + dot(mid, ones) + dot(rest, ones)


def augment(base, minus, lane, e):
    mine = (lane < HEAD) if e == 0 else (lane >= HEAD)
    spot = HEAD if e == 0 else 0
    high, mid, rest = split_three(-minus)
    extra = jnp.where(lane == spot, high, jnp.where(lane == spot + 1, mid, jnp.where(
        lane == spot + 2, rest, jnp.zeros_like(high))))
    return jnp.where(mine, base, extra)


def ones_beside(base, lane, e):
    mine = (lane < HEAD) if e == 0 else (lane >= HEAD)
    return jnp.where(mine, base, 1)


def other_half(value):
    return pltpu.roll(value, HEAD, 1)


def cross_backward(len_ref, g2_ref, crossed_ref, cq_ref, lse_ref, ck_ref, cv_ref, enc_ref, n2_ref,
                   h1_ref, gain2_ref, core_ref, um_ref, uo_ref,
                   dk_ref, dv_ref, keep_ref, send_ref, g1_ref, gg_ref,
                   dm_s, dd_s, dq_s, gk_s, gv_s, b2_s, dml_s, dn_s, w_s, sem):
    s = pl.program_id(0)
    rows = g2_ref.shape[0]

    @pl.when(s == 0)
    def _():
        copies = weight_copies(core_ref, um_ref, uo_ref, w_s, sem)
        for copy in copies:
            copy.start()
        b2_s[...] = g2_ref[...].astype(bf16)
        for cb in col_blocks():
            put_gradient(keep_ref, send_ref, core_ref, 3, cb,
                         dot_tn(crossed_ref[...], b2_s[:, cb]))
        for copy in copies:
            copy.wait()
        for cb in col_blocks():
            put_pairs(dm_s, cb, rounded(dot_nt(b2_s[...], w_s[3, cb, :])))
        clear_tail(dm_s, rows)
        clear_tail(dd_s, rows)
        for hp in range(PAIRS):
            cols = slice(hp * 128, hp * 128 + 128)
            dd_s[hp, 0:rows, :] = head_sums(dm_s[hp, 0:rows, :] * crossed_ref[:, cols].astype(f32))
        gk_s[...] = jnp.zeros(gk_s.shape, f32)
        gv_s[...] = jnp.zeros(gv_s.shape, f32)

    start = 0
    length = len_ref[0]
    for t in range(3):
        start = start + jnp.where(s > t, len_ref[t], 0)
        length = jnp.where(s == t + 1, len_ref[t + 1], length)
    lane = lane_index(MAX_LEN)
    lane_k = lane_index(ENC_LEN)
    valid = lax.broadcasted_iota(jnp.int32, (MAX_LEN, 128), 0) < length
    window = pl.ds(start, MAX_LEN)

    def pair(hp, carry):
        cols = pl.ds(pl.multiple_of(hp * 128, 128), 128)
        q = cq_ref[0, :, cols]
        k = ck_ref[:, cols]
        v = cv_ref[:, cols]
        lse = other_half(lse_ref[0, :, cols])
        dm = jnp.where(valid, dm_s[hp, window, :], 0.0).astype(bf16)
        dd = other_half(jnp.where(valid, dd_s[hp, window, :], 0.0))
        dq = dk = dv = None
        for e in range(2):
            score = dot_nt(ones_beside(k, lane_k, e), augment(q, lse, lane, e))
            p = jnp.exp(score)
            back = dot_nt(ones_beside(v, lane_k, e), augment(dm, dd, lane, e))
            ds = (p * back).astype(bf16)
            mine = (lane < HEAD) if e == 0 else (lane >= HEAD)
            mine_k = (lane_k < HEAD) if e == 0 else (lane_k >= HEAD)
            dv_e = dot(p.astype(bf16), jnp.where(mine, dm, 0))
            dk_e = dot(ds, jnp.where(mine, q, 0))
            dq_e = dot_tn(ds, jnp.where(mine_k, k, 0))
            dq, dk, dv = (dq_e, dk_e, dv_e) if e == 0 else (dq + dq_e, dk + dk_e, dv + dv_e)
        dq_s[hp, window, :] = dq
        dk_ref[:, cols] = dk.astype(bf16)
        dv_ref[:, cols] = dv.astype(bf16)
        return carry

    lax.fori_loop(0, PAIRS, pair, 0)
    for cb in col_blocks():
        gk_s[:, cb] += dot_tn(enc_ref[...], dk_ref[:, cb])
        gv_s[:, cb] += dot_tn(enc_ref[...], dv_ref[:, cb])

    @pl.when(s == pl.num_programs(0) - 1)
    def _():
        join_pairs(dml_s, dq_s, rows)
        for cb in col_blocks():
            put_gradient(keep_ref, send_ref, core_ref, 0, cb, dot_tn(n2_ref[...], dml_s[:, cb]))
            put_gradient(keep_ref, send_ref, core_ref, 1, cb, gk_s[:, cb])
            put_gradient(keep_ref, send_ref, core_ref, 2, cb, gv_s[:, cb])
            dn_s[:, cb] = dot_nt(dml_s[...], w_s[0, cb, :])
        total = jnp.zeros((1, D), f32)
        for rb in row_blocks(rows):
            part, pulled = norm_back(dn_s[rb, :], h1_ref[rb, :], gain2_ref[...])
            g1_ref[rb, :] = g2_ref[rb, :] + part
            total = total + jnp.sum(pulled, axis=0, keepdims=True)
        gg_ref[...] = total


def encoded_back(core_ref, dk_ref, dv_ref, um_ref, uo_ref, ge_ref, w_s, sem):
    @pl.when(pl.program_id(0) == 0)
    def _():
        copies = weight_copies(core_ref, um_ref, uo_ref, w_s, sem)
        for copy in copies:
            copy.start()
        for copy in copies:
            copy.wait()

    for cb in col_blocks():
        ge_ref[:, cb] = dot_nt(dk_ref[...], w_s[1, cb, :]) + dot_nt(dv_ref[...], w_s[2, cb, :])


def diagonal_sums(ref):
    total = ref[0:8, :]
    for r in range(8, MAX_LEN, 8):
        total = total + pltpu.roll(ref[r:r + 8, :], MAX_LEN - r, 1)
    row = lax.broadcasted_iota(jnp.int32, (8, MAX_LEN), 0)
    for bit in (1, 2, 4):
        total = jnp.where((row & bit) != 0, pltpu.roll(total, MAX_LEN - bit, 1), total)
    return jnp.sum(total, axis=0, keepdims=True)


def self_backward(len_ref, g1_ref, mixed_ref, q_ref, k_ref, v_ref, lse_ref, n1_ref,
                  lag_ref, core_ref, um_ref, uo_ref,
                  dq_ref, dk_ref, dv_ref, keep_ref, send_ref, gl_ref,
                  dm_s, dd_s, dq_s, dk_s, dv_s, b1_s, bias_s, acc_s, w_s, sem):
    copies = weight_copies(core_ref, um_ref, uo_ref, w_s, sem)
    for copy in copies:
        copy.start()
    rows = g1_ref.shape[0]
    count = q_ref.shape[0]
    b1_s[...] = g1_ref[...].astype(bf16)
    for cb in col_blocks():
        put_gradient(keep_ref, send_ref, core_ref, 3, cb, dot_tn(mixed_ref[...], b1_s[:, cb]))
    for copy in copies:
        copy.wait()
    for cb in col_blocks():
        put_pairs(dm_s, cb, rounded(dot_nt(b1_s[...], w_s[3, cb, :])))
    clear_tail(dm_s, rows)
    clear_tail(dd_s, rows)
    for hp in range(PAIRS):
        cols = slice(hp * 128, hp * 128 + 128)
        dd_s[hp, 0:rows, :] = head_sums(dm_s[hp, 0:rows, :] * mixed_ref[:, cols].astype(f32))
    starts = starts_of(len_ref)
    row = lax.broadcasted_iota(jnp.int32, (MAX_LEN, MAX_LEN), 0)
    col = lax.broadcasted_iota(jnp.int32, (MAX_LEN, MAX_LEN), 1)
    lane = lane_index(MAX_LEN)
    index = lax.broadcasted_iota(jnp.int32, (MAX_LEN, 128), 0)

    def pair(hp, carry):
        cols = pl.ds(pl.multiple_of(hp * 128, 128), 128)
        for e in range(2):
            w = jnp.broadcast_to(lag_ref[pl.ds(2 * hp + e, 1), :], (MAX_LEN, MAX_LEN))
            table = pltpu.roll(w, 0, 1, stride=1, stride_axis=0)
            bias_s[e] = jnp.where(col >= row, table, masked_score)
        for s in range(count):
            valid = index < len_ref[s]
            window = pl.ds(starts[s], MAX_LEN)
            q = q_ref[s, :, cols]
            k = k_ref[s, :, cols]
            v = v_ref[s, :, cols]
            lse = other_half(lse_ref[s, :, cols])
            dm = jnp.where(valid, dm_s[hp, window, :], 0.0).astype(bf16)
            dd = other_half(jnp.where(valid, dd_s[hp, window, :], 0.0))
            dq = dk = dv = None
            for e in range(2):
                score = dot_nt(ones_beside(k, lane, e), augment(q, lse, lane, e)) + bias_s[e]
                p = jnp.exp(score)
                back = dot_nt(ones_beside(v, lane, e), augment(dm, dd, lane, e))
                grad = p * back
                if s == 0:
                    acc_s[e] = grad
                else:
                    acc_s[e] += grad
                ds = grad.astype(bf16)
                mine = (lane < HEAD) if e == 0 else (lane >= HEAD)
                dv_e = dot(p.astype(bf16), jnp.where(mine, dm, 0))
                dk_e = dot(ds, jnp.where(mine, q, 0))
                dq_e = dot_tn(ds, jnp.where(mine, k, 0))
                dq, dk, dv = (dq_e, dk_e, dv_e) if e == 0 else (dq + dq_e, dk + dk_e, dv + dv_e)
            dq_s[hp, window, :] = dq
            dk_s[hp, window, :] = dk
            dv_s[hp, window, :] = dv
        for e in range(2):
            gl_ref[pl.ds(2 * hp + e, 1), :] = diagonal_sums(acc_s.at[e])
        return carry

    lax.fori_loop(0, PAIRS, pair, 0)
    for w, (src, out) in enumerate(((dq_s, dq_ref), (dk_s, dk_ref), (dv_s, dv_ref))):
        join_pairs(out, src, rows)
        for cb in col_blocks():
            put_gradient(keep_ref, send_ref, core_ref, w, cb, dot_tn(n1_ref[...], out[:, cb]))


def hidden_back(core_ref, g1_ref, hid_ref, gain1_ref, dq_ref, dk_ref, dv_ref, um_ref, uo_ref,
                gh_ref, gg_ref, dn_s, w_s, sem):
    copies = weight_copies(core_ref, um_ref, uo_ref, w_s, sem)
    for copy in copies:
        copy.start()
    for copy in copies:
        copy.wait()
    rows = g1_ref.shape[0]
    for cb in col_blocks():
        dn_s[:, cb] = (dot_nt(dq_ref[...], w_s[0, cb, :]) + dot_nt(dk_ref[...], w_s[1, cb, :])
                       + dot_nt(dv_ref[...], w_s[2, cb, :]))
    total = jnp.zeros((1, D), f32)
    for rb in row_blocks(rows):
        part, pulled = norm_back(dn_s[rb, :], hid_ref[rb, :].astype(f32), gain1_ref[...])
        gh_ref[rb, :] = g1_ref[rb, :] + part
        total = total + jnp.sum(pulled, axis=0, keepdims=True)
    gg_ref[...] = total


def bucket_table():
    lags = np.arange(MAX_LEN)
    exact = BUCKETS // 2
    bucket = np.minimum(lags, exact)
    for step in range(1, exact):
        edge = math.ceil(exact * (MAX_DIST / exact) ** (step / exact))
        bucket = bucket + (lags >= edge)
    return (bucket[None, :] == np.arange(BUCKETS)[:, None]).astype(np.float32)


def shape(dims, kind):
    return jax.ShapeDtypeStruct(dims, kind)


def call(kernel, name, micros, outs, ins, scratch, **extra):
    return pl.pallas_call(
        kernel,
        out_shape=list(outs),
        name=name,
        scratch_shapes=scratch,
        cost_estimate=pl.CostEstimate(
            flops=int(micros * 1e9), bytes_accessed=1 << 20, transcendentals=0),
        compiler_params=pltpu.CompilerParams(vmem_limit_bytes=LIMIT),
        **extra,
    )(*ins)


def whole(array_shape):
    zeros = (0,) * len(array_shape)
    return pl.BlockSpec(array_shape, lambda s: zeros)


class Routes:
    def __init__(self):
        self.parts = lax.axis_size("dp")
        self.shards = lax.axis_size("fsdp")
        self.dp = lax.axis_index("dp")
        self.z = lax.axis_index("fsdp")
        self.core = self.dp & 1
        bits = list(range(1, self.parts.bit_length() - 1))
        self.steps = list(zip(bits, bits[::-1]))

    def permute(self, value, partner):
        pairs = []
        for dp in range(self.parts):
            for z in range(self.shards):
                to_dp, to_z = partner(dp, z)
                pairs.append((dp * self.shards + z, to_dp * self.shards + to_z))
        return lax.ppermute(value, ("dp", "fsdp"), pairs)

    def swap_core(self, value):
        return self.permute(value, lambda dp, z: (dp ^ 1, z))

    def swap(self, value, step):
        return self.permute(value, lambda dp, z: (dp ^ (1 << step[dp & 1]), z))

    def shift(self, value, by):
        return self.permute(value, lambda dp, z: (dp, (z + by) % self.shards))

    def bit(self, step):
        return jnp.where(self.core == 0, (self.dp >> step[0]) & 1, (self.dp >> step[1]) & 1)

    def piece_index(self):
        index = self.core
        for step in self.steps:
            index = 2 * index + self.bit(step)
        return index

    def gather_shards(self, own):
        got = [own] + [self.shift(own, by) for by in range(1, self.shards)]
        return jnp.stack([
            lax.select_n((self.z - z) % self.shards, *got) for z in range(self.shards)])

    def collect(self, piece):
        for step in reversed(self.steps):
            piece = self.join(piece, self.swap(piece, step), step)
        return piece, self.swap_core(piece)

    def join(self, piece, got, step):
        return jnp.where(self.bit(step) == 0, jnp.concatenate([piece, got], 1),
                         jnp.concatenate([got, piece], 1))

    def reduce(self, total, after):
        for step in self.steps:
            size = total.shape[2] // 2
            bit = self.bit(step)
            send = lax.dynamic_slice_in_dim(total, (1 - bit) * size, size, 2)
            keep = lax.dynamic_slice_in_dim(total, bit * size, size, 2)
            got = self.swap(send, step)
            total = add(keep, tie(got, *after))
            after = ()
        return total

    def reduce_shards(self, total):
        mine = lax.dynamic_index_in_dim(total, self.z, 1, keepdims=False).astype(f32)
        got = []
        for by in range(1, self.shards):
            chunk = lax.dynamic_index_in_dim(
                total, (self.z + by) % self.shards, 1, keepdims=False)
            got.append(self.shift(chunk, by))
        for chunk in got:
            mine = mine + chunk.astype(f32)
        return mine.astype(bf16)


def add(left, right):
    return (left.astype(f32) + right.astype(f32)).astype(bf16)


def tie(value, *after):
    return lax.optimization_barrier((value, *after))[0]


def per_device(
    hidden, encoded, out_grad, lengths, group_ids, id_tags, loss_mask, group_steps, group_weights,
    gain_self, gain_cross, gain_ffn, rel_bias,
    query_weight, key_weight, value_weight, output_weight,
    cross_query, cross_key, cross_value, cross_output, expand_weight, reduce_weight,
):
    rows = hidden.shape[0]
    count = lengths.shape[0]
    quarter = D // 4
    routes = Routes()
    core = routes.core.reshape(1)
    size = D // routes.parts

    def piece_of(parts, index, extent):
        return lax.dynamic_slice_in_dim(jnp.concatenate(parts, 0), index * extent, extent, 0)

    small = jnp.concatenate([gain_self, gain_cross, gain_ffn, rel_bias.reshape(-1)])
    small_row = jnp.pad(small[None], ((0, 15), (0, D - small.shape[0])))
    own = piece_of([query_weight, key_weight, value_weight, output_weight],
                   routes.piece_index(), size)
    first = lax.all_gather(jnp.concatenate([own, small_row], 0)[None], "fsdp", axis=0, tiled=True)
    u_self = [half.reshape(4, 2, quarter, D) for half in routes.collect(first[:, :size])]
    small = first[:, size, :small.shape[0]].astype(f32)
    own = piece_of([cross_query, cross_key, cross_value, cross_output],
                   routes.piece_index(), size)
    cross_piece = routes.gather_shards(tie(own, first))
    for step in routes.steps[:0:-1]:
        cross_piece = routes.join(cross_piece, routes.swap(cross_piece, step), step)
    cross_last = routes.swap(cross_piece, routes.steps[0])
    ratio = routes.parts // 8
    slot, offset = routes.dp // ratio, (routes.dp % ratio) * (quarter // ratio)
    own = jnp.where(
        slot < 4,
        lax.dynamic_slice(expand_weight, (offset, jnp.minimum(slot, 3) * D), (quarter // ratio, D)),
        lax.dynamic_slice_in_dim(
            reduce_weight, jnp.maximum(slot - 4, 0) * quarter + offset, quarter // ratio, 0))
    u_ffn = lax.all_gather(tie(own, first), ("fsdp", "dp"), axis=0, tiled=True)
    u_ffn = u_ffn.reshape(4, 8, quarter, D)

    gain1 = small[:, 0:quarter].reshape(1, D)
    gain2 = small[:, quarter:2 * quarter].reshape(1, D)
    gain3 = small[:, 2 * quarter:3 * quarter].reshape(1, D)
    rel = small[:, 3 * quarter:].reshape(HEADS, BUCKETS)
    table = bucket_table()
    by_lag = jnp.dot(rel, jnp.asarray(table), precision=lax.Precision.HIGHEST)
    turned = jnp.dot(
        rel, jnp.asarray(table[:, (-np.arange(MAX_LEN)) % MAX_LEN]), precision=lax.Precision.HIGHEST)

    pad = rows + MAX_LEN
    wide = pltpu.VMEM((PAIRS, pad, 128), f32)
    low = pltpu.VMEM((rows, D), bf16)
    flat = pltpu.VMEM((rows, D), f32)
    square = pltpu.VMEM((2, MAX_LEN, MAX_LEN), f32)
    weights = [pltpu.VMEM((4, D, D), bf16), pltpu.SemaphoreType.DMA((8,))]
    heads = (count, MAX_LEN, D)
    halves = (4, 2, quarter, D)
    n1, q, k, v, lse, mixed, h1, n2 = call(
        self_forward, "self_forward", 21,
        (shape((rows, D), bf16), shape(heads, bf16), shape(heads, bf16), shape(heads, bf16),
         shape(heads, f32), shape((rows, D), bf16), shape((rows, D), f32), shape((rows, D), bf16)),
        (lengths, core, hidden, gain1, gain2, turned, *u_self),
        [wide, wide, wide, wide, square] + weights,
        in_specs=[SMEM] * 2 + [VMEM] * 4 + [ANY] * 2, out_specs=[VMEM] * 8)

    cross_piece = routes.join(cross_piece, tie(cross_last, n2), routes.steps[0])
    u_cross = [half.reshape(4, 2, quarter, D)
               for half in (cross_piece, routes.swap_core(cross_piece))]
    enc_block = pl.BlockSpec((ENC_LEN, D), lambda s: (s, 0))
    seq_block = pl.BlockSpec((1, MAX_LEN, D), lambda s: (s, 0, 0))
    full = whole((rows, D))
    line = whole((1, D))
    ck, cv, cq, cross_lse, crossed, h2, n3 = call(
        cross_forward, "cross_forward", 34,
        (shape(encoded.shape, bf16), shape(encoded.shape, bf16), shape(heads, bf16),
         shape(heads, f32), shape((rows, D), bf16), shape((rows, D), f32), shape((rows, D), bf16)),
        (lengths, core, n2, h1, gain3, encoded, *u_cross),
        [wide, wide] + weights,
        grid=(count,),
        in_specs=[SMEM] * 2 + [full, full, line, enc_block, ANY, ANY],
        out_specs=[enc_block, enc_block, seq_block, seq_block, full, full, full])

    column = whole((rows, 1))
    x_block = pl.BlockSpec((4, 1, quarter, D), lambda g: (0, g, 0, 0))
    r_block = pl.BlockSpec((1, 4, quarter, D), lambda g: (g, 1, 0, 0))
    layer_output, grad_ffn, g2, gg3 = call(
        feed_forward, "feed_forward", 32,
        (shape((rows, D), bf16), shape((8, 4, quarter, D), bf16),
         shape((rows, D), f32), shape((1, D), f32)),
        (lengths, group_ids, group_steps, group_weights, id_tags[:, None], loss_mask[:, None],
         out_grad, n3, h2, gain3, u_ffn, u_ffn),
        [low, flat, flat, low, low],
        grid=(4,),
        in_specs=[SMEM] * 4 + [column, column, full, full, full, line, x_block, r_block],
        out_specs=[full, whole((8, 4, quarter, D)), full, line])
    if routes.parts > 8:
        grad_ffn = grad_ffn.reshape(8, 4, routes.parts // 8, -1, D).swapaxes(1, 2)
    ffn_piece = lax.psum_scatter(
        grad_ffn.reshape(-1, D), "dp", scatter_dimension=0, tiled=True)

    dck, dcv, keep, send, g1, gg2 = call(
        cross_backward, "cross_backward", 42,
        (shape(encoded.shape, bf16), shape(encoded.shape, bf16), shape(halves, bf16),
         shape(halves, bf16), shape((rows, D), f32), shape((1, D), f32)),
        (lengths, g2, crossed, cq, cross_lse, ck, cv, encoded, n2, h1, gain2, core, *u_cross),
        [wide, wide, wide, pltpu.VMEM((D, D), f32), pltpu.VMEM((D, D), f32), low, low, flat]
        + weights,
        grid=(count,),
        in_specs=[SMEM, full, full, seq_block, seq_block, enc_block, enc_block, enc_block, full,
                  full, line, SMEM, ANY, ANY],
        out_specs=[enc_block, enc_block, whole(halves), whole(halves), full, line])
    cross_keep = keep
    cross_got = routes.swap_core(send)

    dq, dk, dv, keep, send, grad_lag = call(
        self_backward, "self_backward", 28,
        (shape((rows, D), bf16), shape((rows, D), bf16), shape((rows, D), bf16),
         shape(halves, bf16), shape(halves, bf16), shape((HEADS, MAX_LEN), f32)),
        (lengths, g1, mixed, q, k, v, lse, n1, by_lag, core, *u_self),
        [wide, wide, wide, wide, wide, low, square, square] + weights,
        in_specs=[SMEM] + [VMEM] * 8 + [SMEM, ANY, ANY], out_specs=[VMEM] * 6)
    self_got = routes.swap_core(send)

    grad_hidden, gg1 = call(
        hidden_back, "hidden_back", 8,
        (shape((rows, D), f32), shape((1, D), f32)),
        (core, g1, hidden, gain1, dq, dk, dv, *u_self),
        [flat] + weights,
        in_specs=[SMEM] + [VMEM] * 6 + [ANY] * 2, out_specs=[VMEM] * 2)
    total = jnp.stack([add(keep, tie(self_got, grad_hidden)), add(cross_keep, cross_got)])
    total = total.reshape(2, 4, D // 2, D)

    (grad_encoded,) = call(
        encoded_back, "encoded_back", 10,
        (shape(encoded.shape, f32),),
        (core, tie(dck, total), dcv, *u_cross),
        weights,
        grid=(count,),
        in_specs=[SMEM, enc_block, enc_block, ANY, ANY], out_specs=[enc_block])
    grad_rel = lax.dot_general(
        grad_lag, jnp.asarray(table), (((1,), (1,)), ((), ())), precision=lax.Precision.HIGHEST)
    small_grads = jnp.concatenate(
        [gg1.reshape(4, quarter), gg2.reshape(4, quarter), gg3.reshape(4, quarter),
         grad_rel.reshape(4, -1)], axis=1)
    extent = ffn_piece.shape[0] // 4
    small_rows = jnp.pad(small_grads.astype(bf16)[:, None, :],
                         ((0, 0), (0, 15), (0, D - small_grads.shape[1])))
    ffn_piece = jnp.concatenate(
        [tie(ffn_piece, total).reshape(4, extent, D), small_rows], axis=1)
    ffn_piece = lax.psum_scatter(ffn_piece.reshape(-1, D), "fsdp", scatter_dimension=0, tiled=True)
    ffn_shard = lax.all_gather(ffn_piece[None], "dp", axis=0, tiled=True).astype(f32)
    small_mine = jnp.sum(ffn_shard[:, extent], axis=0)
    ffn = ffn_shard[:, :extent].reshape(2 * D, D)

    piece = routes.reduce_shards(routes.reduce(total, (grad_encoded,)))
    mine, other = routes.collect(piece)
    low_half = jnp.where(routes.core == 0, mine, other).astype(f32).reshape(2, 2, quarter, D)
    high_half = jnp.where(routes.core == 0, other, mine).astype(f32).reshape(2, 2, quarter, D)
    return (
        layer_output,
        grad_hidden,
        grad_encoded,
        small_mine[0:quarter],
        small_mine[quarter:2 * quarter],
        small_mine[2 * quarter:3 * quarter],
        small_mine[3 * quarter:small_grads.shape[1]].reshape(HEADS // 4, BUCKETS),
        low_half[0, 0],
        low_half[0, 1],
        high_half[0, 0],
        high_half[0, 1],
        low_half[1, 0],
        low_half[1, 1],
        high_half[1, 0],
        high_half[1, 1],
        jnp.concatenate([ffn[g * quarter:(g + 1) * quarter] for g in range(4)], axis=1),
        ffn[D:],
    )


def solution(mesh):
    rows = P(("dp", "fsdp"), None)
    flat = P(("dp", "fsdp"))
    shard = P("fsdp", None)
    line = P("fsdp")
    return jax.shard_map(
        per_device,
        mesh=mesh,
        in_specs=(rows, rows, rows, flat, flat, flat, flat, P(), P(), line, line, line) + (shard,) * 11,
        out_specs=(rows, rows, rows, line, line, line) + (shard,) * 11,
        check_vma=False,
    )
```

```python
from functools import partial
import math

import jax
import jax.numpy as jnp
import numpy as np
from jax import lax
from jax.experimental import pallas as pl
from jax.experimental.pallas import tpu as pltpu
from jax.sharding import PartitionSpec as P

HEADS = 12
HEAD = 64
PAIRS = 6
BUCKETS = 32
MAX_DIST = 128
ENC_LEN = 512
MAX_LEN = 256
GROUPS = 3
HORIZON = 10000
D = 768
COLS = 768
SMALL = 16

f32 = jnp.float32
bf16 = jnp.bfloat16
epsilon = 1e-06
masked_score = -1000000000.0

VMEM = pl.BlockSpec(memory_space=pltpu.VMEM)
SMEM = pl.BlockSpec(memory_space=pltpu.SMEM)
ANY = pl.BlockSpec(memory_space=pl.ANY)
LIMIT = 60 * 1024 * 1024


def dot(left, right):
    return jnp.dot(left, right, preferred_element_type=f32)


def dot_nt(left, right):
    return lax.dot_general(left, right, (((1,), (1,)), ((), ())), preferred_element_type=f32)


def dot_tn(left, right):
    return lax.dot_general(left, right, (((0,), (0,)), ((), ())), preferred_element_type=f32)


def rounded(value):
    return value.astype(bf16).astype(f32)


def row_scale(rows):
    return lax.rsqrt(jnp.mean(rows * rows, axis=-1, keepdims=True) + epsilon)


def row_blocks(rows):
    return [slice(r, r + 128) for r in range(0, rows, 128)]


def col_blocks(width=D):
    return [slice(c, c + COLS) for c in range(0, width, COLS)]


def starts_of(len_ref):
    starts = [0]
    for s in range(3):
        starts.append(starts[-1] + len_ref[s])
    return starts


def norm_back(grad, rows, gain):
    r = row_scale(rows)
    pulled = gain * grad
    inner = jnp.mean(pulled * rows, axis=-1, keepdims=True)
    return r * pulled - rows * (r * r * r * inner), grad * rows * r


def split_three(value):
    high = value.astype(bf16)
    rest = value - high.astype(f32)
    mid = rest.astype(bf16)
    return high, mid, (rest - mid.astype(f32)).astype(bf16)


def weight_copies(core_ref, mine_ref, other_ref, w_s, sem):
    core = core_ref[0]
    quarter = D // 4
    copies = []
    for h, ref in enumerate((mine_ref, other_ref)):
        first = 2 * core if h == 0 else 2 * (1 - core)
        for z in range(4):
            copies.append(pltpu.make_async_copy(
                ref.at[z], w_s.at[pl.ds(first, 2), pl.ds(z * quarter, quarter), :],
                sem.at[4 * h + z]))
    return copies


def put_gradient(keep_ref, send_ref, core_ref, index, cb, value):
    value = value.astype(bf16).reshape(4, D // 4, COLS)
    stays = core_ref[0] == index // 2

    @pl.when(stays)
    def _():
        keep_ref[:, index % 2, :, cb] = value

    @pl.when(jnp.logical_not(stays))
    def _():
        send_ref[:, index % 2, :, cb] = value


def put_pairs(dst, cb, value):
    first = cb.start // 128
    for part in range(COLS // 128):
        dst[first + part, 0:value.shape[0], :] = value[:, part * 128:part * 128 + 128]


def clear_tail(dst, rows):
    dst[:, rows:, :] = jnp.zeros((PAIRS, dst.shape[1] - rows, 128), f32)


def join_pairs(dst, src, rows):
    for hp in range(PAIRS):
        dst[:, hp * 128:hp * 128 + 128] = src[hp, 0:rows, :].astype(dst.dtype)


def lane_index(rows):
    return lax.broadcasted_iota(jnp.int32, (rows, 128), 1)


def self_forward(len_ref, core_ref, hid_ref, gain1_ref, gain2_ref, lag_ref, um_ref, uo_ref,
                 n1_ref, q_ref, k_ref, v_ref, lse_ref, mixed_ref, h1_ref, n2_ref,
                 q_s, k_s, v_s, m_s, bias_s, w_s, sem):
    copies = weight_copies(core_ref, um_ref, uo_ref, w_s, sem)
    for copy in copies:
        copy.start()
    rows = hid_ref.shape[0]
    count = q_ref.shape[0]
    for rb in row_blocks(rows):
        x = hid_ref[rb, :].astype(f32)
        n1_ref[rb, :] = (x * row_scale(x) * gain1_ref[...]).astype(bf16)
    for copy in copies:
        copy.wait()
    for w, dst in enumerate((q_s, k_s, v_s)):
        for cb in col_blocks():
            put_pairs(dst, cb, rounded(dot(n1_ref[...], w_s[w, :, cb])))
        clear_tail(dst, rows)
    starts = starts_of(len_ref)
    row = lax.broadcasted_iota(jnp.int32, (MAX_LEN, MAX_LEN), 0)
    col = lax.broadcasted_iota(jnp.int32, (MAX_LEN, MAX_LEN), 1)
    lane = lane_index(MAX_LEN)
    even = lane < HEAD

    def pair(hp, carry):
        cols = pl.ds(pl.multiple_of(hp * 128, 128), 128)
        for e in range(2):
            w = jnp.broadcast_to(lag_ref[pl.ds(2 * hp + e, 1), :], (MAX_LEN, MAX_LEN))
            table = pltpu.roll(w, 0, 1, stride=1, stride_axis=0)
            bias_s[e] = jnp.where(row >= col, table, masked_score)
        for s in range(count):
            window = pl.ds(starts[s], MAX_LEN)
            q = q_s[hp, window, :].astype(bf16)
            k = k_s[hp, window, :].astype(bf16)
            v = v_s[hp, window, :].astype(bf16)
            q_ref[s, :, cols] = q
            k_ref[s, :, cols] = k
            v_ref[s, :, cols] = v
            res, tops = [], []
            for e in range(2):
                mine = even if e == 0 else ~even
                score = dot_nt(jnp.where(mine, q, 0), k) + bias_s[e]
                top = jnp.max(score, axis=-1, keepdims=True)
                p = jnp.exp(score - top).astype(bf16)
                res.append(dot(p, jnp.where(mine, v, 1)))
                tops.append(top)
            num = jnp.where(even, res[0], res[1])
            den = jnp.where(even, pltpu.roll(res[0], HEAD, 1), pltpu.roll(res[1], HEAD, 1))
            lse_ref[s, :, cols] = jnp.where(even, tops[0], tops[1]) + jnp.log(den)
            m_s[hp, window, :] = num / den
        return carry

    lax.fori_loop(0, PAIRS, pair, 0, unroll=2)
    join_pairs(mixed_ref, m_s, rows)
    for cb in col_blocks():
        h1_ref[:, cb] = hid_ref[:, cb].astype(f32) + dot(mixed_ref[...], w_s[3, :, cb])
    for rb in row_blocks(rows):
        x = h1_ref[rb, :]
        n2_ref[rb, :] = (x * row_scale(x) * gain2_ref[...]).astype(bf16)


def cross_forward(len_ref, core_ref, n2_ref, h1_ref, gain3_ref, enc_ref, um_ref, uo_ref,
                  ck_ref, cv_ref, cq_ref, lse_ref, crossed_ref, h2_ref, n3_ref,
                  q_s, m_s, w_s, sem):
    s = pl.program_id(0)
    rows = n2_ref.shape[0]
    count = pl.num_programs(0)

    @pl.when(s == 0)
    def _():
        copies = weight_copies(core_ref, um_ref, uo_ref, w_s, sem)
        for copy in copies:
            copy.start()
        for copy in copies:
            copy.wait()
        for cb in col_blocks():
            put_pairs(q_s, cb, rounded(dot(n2_ref[...], w_s[0, :, cb])))
        clear_tail(q_s, rows)

    for cb in col_blocks():
        ck_ref[:, cb] = dot(enc_ref[...], w_s[1, :, cb]).astype(bf16)
        cv_ref[:, cb] = dot(enc_ref[...], w_s[2, :, cb]).astype(bf16)
    start = 0
    for t in range(3):
        start = start + jnp.where(s > t, len_ref[t], 0)
    window = pl.ds(start, MAX_LEN)
    even = lane_index(MAX_LEN) < HEAD
    even_v = lane_index(ENC_LEN) < HEAD

    def pair(hp, carry):
        cols = pl.ds(pl.multiple_of(hp * 128, 128), 128)
        q = q_s[hp, window, :].astype(bf16)
        cq_ref[0, :, cols] = q
        k = ck_ref[:, cols]
        v = cv_ref[:, cols]
        res, tops = [], []
        for e in range(2):
            mine = even if e == 0 else ~even
            mine_v = even_v if e == 0 else ~even_v
            score = dot_nt(jnp.where(mine, q, 0), k)
            top = jnp.max(score, axis=-1, keepdims=True)
            p = jnp.exp(score - top).astype(bf16)
            res.append(dot(p, jnp.where(mine_v, v, 1)))
            tops.append(top)
        num = jnp.where(even, res[0], res[1])
        den = jnp.where(even, pltpu.roll(res[0], HEAD, 1), pltpu.roll(res[1], HEAD, 1))
        lse_ref[0, :, cols] = jnp.where(even, tops[0], tops[1]) + jnp.log(den)
        m_s[hp, window, :] = num / den
        return carry

    lax.fori_loop(0, PAIRS, pair, 0, unroll=2)

    @pl.when(s == count - 1)
    def _():
        join_pairs(crossed_ref, m_s, rows)
        for cb in col_blocks():
            h2_ref[:, cb] = h1_ref[:, cb] + dot(crossed_ref[...], w_s[3, :, cb])
        for rb in row_blocks(rows):
            x = h2_ref[rb, :]
            n3_ref[rb, :] = (x * row_scale(x) * gain3_ref[...]).astype(bf16)


def gelu_parts(x):
    decay = jnp.exp(-0.5 * (x * x))
    t = 1.0 / (1.0 + jnp.abs(x) * (0.3275911 / math.sqrt(2.0)))
    poly = t * (0.5 * 0.254829592 + t * (-0.5 * 0.284496736 + t * (
        0.5 * 1.421413741 + t * (-0.5 * 1.453152027 + t * (0.5 * 1.061405429)))))
    tail = poly * decay
    below = jnp.where(x >= 0, 1.0 - tail, tail)
    return x * below, below + x * decay * (1.0 / math.sqrt(2.0 * math.pi))


def feed_forward(len_ref, group_ref, step_ref, weight_ref, tags_ref, mask_ref, og_ref, n3_ref,
                 h2_ref, gain3_ref, x_ref, r_ref,
                 out_ref, gu_ref, g2_ref, gg_ref,
                 scaled_s, out_s, dn_s, act_s, de_s):
    g = pl.program_id(0)
    rows = n3_ref.shape[0]

    def token_weight(rb):
        index = lax.broadcasted_iota(jnp.int32, (128, 1), 0) + rb.start
        scale = jnp.zeros((128, 1), f32)
        tagged = jnp.zeros((128, 1), jnp.int32)
        start = 0
        for s in range(4):
            group = group_ref[s]
            factor = jnp.float32(0.0)
            for k in range(GROUPS):
                value = weight_ref[k].astype(f32) * 0.25 * (
                    1.0 - step_ref[k].astype(f32) * (1.0 / (2.0 * HORIZON)))
                factor = jnp.where(group == k, value, factor)
            inside = index >= start
            scale = jnp.where(inside, factor, scale)
            tagged = jnp.where(inside, jnp.where(group == 1, 1, 0), tagged)
            start = start + len_ref[s]
        counted = jnp.where(tagged == 1, tags_ref[rb, :], mask_ref[rb, :]).astype(f32)
        return scale * (0.25 + 0.75 * counted)

    @pl.when(g == 0)
    def _():
        for rb in row_blocks(rows):
            scaled = og_ref[rb, :].astype(f32) * token_weight(rb)
            g2_ref[rb, :] = scaled
            scaled_s[rb, :] = scaled.astype(bf16)
        out_s[...] = h2_ref[...]
        dn_s[...] = jnp.zeros(dn_s.shape, f32)

    for cb in col_blocks():
        expanded = dot(n3_ref[...], x_ref[:, 0, :, cb].reshape(D, COLS))
        act, slope = gelu_parts(expanded)
        act_s[:, cb] = act.astype(bf16)
        back = dot_nt(scaled_s[...], r_ref[0].reshape(D, D)[cb, :])
        de_s[:, cb] = (back * slope).astype(bf16)
    for cb in col_blocks():
        out_s[:, cb] += dot(act_s[...], r_ref[0, :, :, cb].reshape(D, COLS))
        gx = dot_tn(n3_ref[...], de_s[:, cb]).astype(bf16)
        gr = dot_tn(act_s[...], scaled_s[:, cb]).astype(bf16)
        gu_ref[g, :, :, cb] = gx.reshape(4, D // 4, COLS)
        for part in range(4):
            gu_ref[4 + part, g, :, cb] = gr[part * (D // 4):(part + 1) * (D // 4), :]
    full = x_ref[:, 0].reshape(D, D)
    for cb in col_blocks():
        dn_s[:, cb] += dot_nt(de_s[...], full[cb, :])

    @pl.when(g == pl.num_programs(0) - 1)
    def _():
        total = jnp.zeros((1, D), f32)
        for rb in row_blocks(rows):
            out_ref[rb, :] = out_s[rb, :].astype(bf16)
            part, pulled = norm_back(dn_s[rb, :], h2_ref[rb, :], gain3_ref[...])
            g2_ref[rb, :] += part
            total = total + jnp.sum(pulled, axis=0, keepdims=True)
        gg_ref[...] = total


def head_sums(product):
    a = lax.broadcasted_iota(jnp.int32, (128, 128), 0) < HEAD
    b = lax.broadcasted_iota(jnp.int32, (128, 128), 1) < HEAD
    ones = (a == b).astype(bf16)
    high, mid, rest = split_three(product)
    return dot(high, ones) + dot(mid, ones) + dot(rest, ones)


def augment(base, minus, lane, e):
    mine = (lane < HEAD) if e == 0 else (lane >= HEAD)
    spot = HEAD if e == 0 else 0
    high, mid, rest = split_three(-minus)
    extra = jnp.where(lane == spot, high, jnp.where(lane == spot + 1, mid, jnp.where(
        lane == spot + 2, rest, jnp.zeros_like(high))))
    return jnp.where(mine, base, extra)


def ones_beside(base, lane, e):
    mine = (lane < HEAD) if e == 0 else (lane >= HEAD)
    return jnp.where(mine, base, 1)


def other_half(value):
    return pltpu.roll(value, HEAD, 1)


def cross_backward(len_ref, g2_ref, crossed_ref, cq_ref, lse_ref, ck_ref, cv_ref, enc_ref, n2_ref,
                   h1_ref, gain2_ref, core_ref, um_ref, uo_ref,
                   dk_ref, dv_ref, keep_ref, send_ref, g1_ref, gg_ref,
                   dm_s, dd_s, dq_s, gk_s, gv_s, b2_s, dml_s, dn_s, w_s, sem):
    s = pl.program_id(0)
    rows = g2_ref.shape[0]

    @pl.when(s == 0)
    def _():
        copies = weight_copies(core_ref, um_ref, uo_ref, w_s, sem)
        for copy in copies:
            copy.start()
        b2_s[...] = g2_ref[...].astype(bf16)
        for cb in col_blocks():
            put_gradient(keep_ref, send_ref, core_ref, 3, cb,
                         dot_tn(crossed_ref[...], b2_s[:, cb]))
        for copy in copies:
            copy.wait()
        for cb in col_blocks():
            put_pairs(dm_s, cb, rounded(dot_nt(b2_s[...], w_s[3, cb, :])))
        clear_tail(dm_s, rows)
        clear_tail(dd_s, rows)
        for hp in range(PAIRS):
            cols = slice(hp * 128, hp * 128 + 128)
            dd_s[hp, 0:rows, :] = head_sums(dm_s[hp, 0:rows, :] * crossed_ref[:, cols].astype(f32))
        gk_s[...] = jnp.zeros(gk_s.shape, f32)
        gv_s[...] = jnp.zeros(gv_s.shape, f32)

    start = 0
    length = len_ref[0]
    for t in range(3):
        start = start + jnp.where(s > t, len_ref[t], 0)
        length = jnp.where(s == t + 1, len_ref[t + 1], length)
    lane = lane_index(MAX_LEN)
    lane_k = lane_index(ENC_LEN)
    valid = lax.broadcasted_iota(jnp.int32, (MAX_LEN, 128), 0) < length
    window = pl.ds(start, MAX_LEN)

    def pair(hp, carry):
        cols = pl.ds(pl.multiple_of(hp * 128, 128), 128)
        q = cq_ref[0, :, cols]
        k = ck_ref[:, cols]
        v = cv_ref[:, cols]
        lse = other_half(lse_ref[0, :, cols])
        dm = jnp.where(valid, dm_s[hp, window, :], 0.0).astype(bf16)
        dd = other_half(jnp.where(valid, dd_s[hp, window, :], 0.0))
        dq = dk = dv = None
        for e in range(2):
            score = dot_nt(ones_beside(k, lane_k, e), augment(q, lse, lane, e))
            p = jnp.exp(score)
            back = dot_nt(ones_beside(v, lane_k, e), augment(dm, dd, lane, e))
            ds = (p * back).astype(bf16)
            mine = (lane < HEAD) if e == 0 else (lane >= HEAD)
            mine_k = (lane_k < HEAD) if e == 0 else (lane_k >= HEAD)
            dv_e = dot(p.astype(bf16), jnp.where(mine, dm, 0))
            dk_e = dot(ds, jnp.where(mine, q, 0))
            dq_e = dot_tn(ds, jnp.where(mine_k, k, 0))
            dq, dk, dv = (dq_e, dk_e, dv_e) if e == 0 else (dq + dq_e, dk + dk_e, dv + dv_e)
        dq_s[hp, window, :] = dq
        dk_ref[:, cols] = dk.astype(bf16)
        dv_ref[:, cols] = dv.astype(bf16)
        return carry

    lax.fori_loop(0, PAIRS, pair, 0, unroll=2)
    for cb in col_blocks():
        gk_s[:, cb] += dot_tn(enc_ref[...], dk_ref[:, cb])
        gv_s[:, cb] += dot_tn(enc_ref[...], dv_ref[:, cb])

    @pl.when(s == pl.num_programs(0) - 1)
    def _():
        join_pairs(dml_s, dq_s, rows)
        for cb in col_blocks():
            put_gradient(keep_ref, send_ref, core_ref, 0, cb, dot_tn(n2_ref[...], dml_s[:, cb]))
            put_gradient(keep_ref, send_ref, core_ref, 1, cb, gk_s[:, cb])
            put_gradient(keep_ref, send_ref, core_ref, 2, cb, gv_s[:, cb])
            dn_s[:, cb] = dot_nt(dml_s[...], w_s[0, cb, :])
        total = jnp.zeros((1, D), f32)
        for rb in row_blocks(rows):
            part, pulled = norm_back(dn_s[rb, :], h1_ref[rb, :], gain2_ref[...])
            g1_ref[rb, :] = g2_ref[rb, :] + part
            total = total + jnp.sum(pulled, axis=0, keepdims=True)
        gg_ref[...] = total


def encoded_back(core_ref, dk_ref, dv_ref, um_ref, uo_ref, ge_ref, w_s, sem):
    @pl.when(pl.program_id(0) == 0)
    def _():
        copies = weight_copies(core_ref, um_ref, uo_ref, w_s, sem)
        for copy in copies:
            copy.start()
        for copy in copies:
            copy.wait()

    for cb in col_blocks():
        ge_ref[:, cb] = dot_nt(dk_ref[...], w_s[1, cb, :]) + dot_nt(dv_ref[...], w_s[2, cb, :])


def diagonal_sums(ref):
    total = ref[0:8, :]
    for r in range(8, MAX_LEN, 8):
        total = total + pltpu.roll(ref[r:r + 8, :], MAX_LEN - r, 1)
    row = lax.broadcasted_iota(jnp.int32, (8, MAX_LEN), 0)
    for bit in (1, 2, 4):
        total = jnp.where((row & bit) != 0, pltpu.roll(total, MAX_LEN - bit, 1), total)
    return jnp.sum(total, axis=0, keepdims=True)


def self_backward(len_ref, g1_ref, mixed_ref, q_ref, k_ref, v_ref, lse_ref, n1_ref,
                  lag_ref, core_ref, um_ref, uo_ref,
                  dq_ref, dk_ref, dv_ref, keep_ref, send_ref, gl_ref,
                  dm_s, dd_s, dq_s, dk_s, dv_s, b1_s, bias_s, acc_s, w_s, sem):
    copies = weight_copies(core_ref, um_ref, uo_ref, w_s, sem)
    for copy in copies:
        copy.start()
    rows = g1_ref.shape[0]
    count = q_ref.shape[0]
    b1_s[...] = g1_ref[...].astype(bf16)
    for cb in col_blocks():
        put_gradient(keep_ref, send_ref, core_ref, 3, cb, dot_tn(mixed_ref[...], b1_s[:, cb]))
    for copy in copies:
        copy.wait()
    for cb in col_blocks():
        put_pairs(dm_s, cb, rounded(dot_nt(b1_s[...], w_s[3, cb, :])))
    clear_tail(dm_s, rows)
    clear_tail(dd_s, rows)
    for hp in range(PAIRS):
        cols = slice(hp * 128, hp * 128 + 128)
        dd_s[hp, 0:rows, :] = head_sums(dm_s[hp, 0:rows, :] * mixed_ref[:, cols].astype(f32))
    starts = starts_of(len_ref)
    row = lax.broadcasted_iota(jnp.int32, (MAX_LEN, MAX_LEN), 0)
    col = lax.broadcasted_iota(jnp.int32, (MAX_LEN, MAX_LEN), 1)
    lane = lane_index(MAX_LEN)
    index = lax.broadcasted_iota(jnp.int32, (MAX_LEN, 128), 0)

    def pair(hp, carry):
        cols = pl.ds(pl.multiple_of(hp * 128, 128), 128)
        for e in range(2):
            w = jnp.broadcast_to(lag_ref[pl.ds(2 * hp + e, 1), :], (MAX_LEN, MAX_LEN))
            table = pltpu.roll(w, 0, 1, stride=1, stride_axis=0)
            bias_s[e] = jnp.where(col >= row, table, masked_score)
        for s in range(count):
            valid = index < len_ref[s]
            window = pl.ds(starts[s], MAX_LEN)
            q = q_ref[s, :, cols]
            k = k_ref[s, :, cols]
            v = v_ref[s, :, cols]
            lse = other_half(lse_ref[s, :, cols])
            dm = jnp.where(valid, dm_s[hp, window, :], 0.0).astype(bf16)
            dd = other_half(jnp.where(valid, dd_s[hp, window, :], 0.0))
            dq = dk = dv = None
            for e in range(2):
                score = dot_nt(ones_beside(k, lane, e), augment(q, lse, lane, e)) + bias_s[e]
                p = jnp.exp(score)
                back = dot_nt(ones_beside(v, lane, e), augment(dm, dd, lane, e))
                grad = p * back
                if s == 0:
                    acc_s[e] = grad
                else:
                    acc_s[e] += grad
                ds = grad.astype(bf16)
                mine = (lane < HEAD) if e == 0 else (lane >= HEAD)
                dv_e = dot(p.astype(bf16), jnp.where(mine, dm, 0))
                dk_e = dot(ds, jnp.where(mine, q, 0))
                dq_e = dot_tn(ds, jnp.where(mine, k, 0))
                dq, dk, dv = (dq_e, dk_e, dv_e) if e == 0 else (dq + dq_e, dk + dk_e, dv + dv_e)
            dq_s[hp, window, :] = dq
            dk_s[hp, window, :] = dk
            dv_s[hp, window, :] = dv
        for e in range(2):
            gl_ref[pl.ds(2 * hp + e, 1), :] = diagonal_sums(acc_s.at[e])
        return carry

    lax.fori_loop(0, PAIRS, pair, 0, unroll=2)
    for w, (src, out) in enumerate(((dq_s, dq_ref), (dk_s, dk_ref), (dv_s, dv_ref))):
        join_pairs(out, src, rows)
        for cb in col_blocks():
            put_gradient(keep_ref, send_ref, core_ref, w, cb, dot_tn(n1_ref[...], out[:, cb]))


def hidden_back(core_ref, g1_ref, hid_ref, gain1_ref, dq_ref, dk_ref, dv_ref, gg2_ref, gg3_ref,
                gl_ref, um_ref, uo_ref, gh_ref, small_ref, dn_s, small_s, w_s, sem):
    copies = weight_copies(core_ref, um_ref, uo_ref, w_s, sem)
    for copy in copies:
        copy.start()
    for copy in copies:
        copy.wait()
    rows = g1_ref.shape[0]
    for cb in col_blocks():
        dn_s[:, cb] = (dot_nt(dq_ref[...], w_s[0, cb, :]) + dot_nt(dk_ref[...], w_s[1, cb, :])
                       + dot_nt(dv_ref[...], w_s[2, cb, :]))
    total = jnp.zeros((1, D), f32)
    for rb in row_blocks(rows):
        part, pulled = norm_back(dn_s[rb, :], hid_ref[rb, :].astype(f32), gain1_ref[...])
        gh_ref[rb, :] = g1_ref[rb, :] + part
        total = total + jnp.sum(pulled, axis=0, keepdims=True)
    small_s[...] = jnp.zeros(small_s.shape, f32)
    small_s[0:1, :] = total
    small_s[1:2, :] = gg2_ref[...]
    small_s[2:3, :] = gg3_ref[...]
    small_s[3:3 + HEADS, 0:MAX_LEN] = gl_ref[...]
    small_ref[...] = small_s[...].astype(bf16)


def bucket_table():
    lags = np.arange(MAX_LEN)
    exact = BUCKETS // 2
    bucket = np.minimum(lags, exact)
    for step in range(1, exact):
        edge = math.ceil(exact * (MAX_DIST / exact) ** (step / exact))
        bucket = bucket + (lags >= edge)
    return (bucket[None, :] == np.arange(BUCKETS)[:, None]).astype(np.float32)


def shape(dims, kind):
    return jax.ShapeDtypeStruct(dims, kind)


def call(kernel, name, micros, outs, ins, scratch, **extra):
    return pl.pallas_call(
        kernel,
        out_shape=list(outs),
        name=name,
        scratch_shapes=scratch,
        cost_estimate=pl.CostEstimate(
            flops=int(micros * 1e9), bytes_accessed=1 << 20, transcendentals=0),
        compiler_params=pltpu.CompilerParams(vmem_limit_bytes=LIMIT),
        **extra,
    )(*ins)


def whole(array_shape):
    zeros = (0,) * len(array_shape)
    return pl.BlockSpec(array_shape, lambda s: zeros)


class Routes:
    def __init__(self):
        self.parts = lax.axis_size("dp")
        self.shards = lax.axis_size("fsdp")
        self.dp = lax.axis_index("dp")
        self.z = lax.axis_index("fsdp")
        self.core = self.dp & 1
        bits = list(range(1, self.parts.bit_length() - 1))
        self.steps = list(zip(bits, bits[::-1]))

    def permute(self, value, partner):
        pairs = []
        for dp in range(self.parts):
            for z in range(self.shards):
                to_dp, to_z = partner(dp, z)
                pairs.append((dp * self.shards + z, to_dp * self.shards + to_z))
        return lax.ppermute(value, ("dp", "fsdp"), pairs)

    def swap_core(self, value):
        return self.permute(value, lambda dp, z: (dp ^ 1, z))

    def swap(self, value, step):
        return self.permute(value, lambda dp, z: (dp ^ (1 << step[dp & 1]), z))

    def shift(self, value, by):
        return self.permute(value, lambda dp, z: (dp, (z + by) % self.shards))

    def bit(self, step):
        return jnp.where(self.core == 0, (self.dp >> step[0]) & 1, (self.dp >> step[1]) & 1)

    def piece_index(self):
        index = self.core
        for step in self.steps:
            index = 2 * index + self.bit(step)
        return index

    def gather_shards(self, own):
        got = [own] + [self.shift(own, by) for by in range(1, self.shards)]
        return jnp.stack([
            lax.select_n((self.z - z) % self.shards, *got) for z in range(self.shards)])

    def collect(self, piece):
        for step in reversed(self.steps):
            piece = self.join(piece, self.swap(piece, step), step)
        return piece, self.swap_core(piece)

    def join(self, piece, got, step):
        return jnp.where(self.bit(step) == 0, jnp.concatenate([piece, got], 1),
                         jnp.concatenate([got, piece], 1))

    def halve(self, total, step):
        size = total.shape[1] // 2
        bit = self.bit(step)
        send = lax.dynamic_slice_in_dim(total, (1 - bit) * size, size, 1)
        keep = lax.dynamic_slice_in_dim(total, bit * size, size, 1)
        return keep, self.swap(send, step)

    def send_shards(self, total):
        parts = [lax.dynamic_index_in_dim(total, self.z, 0, keepdims=False)]
        for by in range(1, self.shards):
            chunk = lax.dynamic_index_in_dim(total, (self.z + by) % self.shards, 0, keepdims=False)
            parts.append(self.shift(chunk, by))
        return parts


def add(left, right):
    return (left.astype(f32) + right.astype(f32)).astype(bf16)


HALVES = (4, 2, D // 4, D)
WEIGHTS = [pltpu.VMEM((4, D, D), bf16), pltpu.SemaphoreType.DMA((8,))]
SQUARE = pltpu.VMEM((2, MAX_LEN, MAX_LEN), f32)
LINE = whole((1, D))
ENC_BLOCK = pl.BlockSpec((ENC_LEN, D), lambda s: (s, 0))
SEQ_BLOCK = pl.BlockSpec((1, MAX_LEN, D), lambda s: (s, 0, 0))


def scratch_of(rows):
    wide = pltpu.VMEM((PAIRS, rows + MAX_LEN, 128), f32)
    return wide, pltpu.VMEM((rows, D), bf16), pltpu.VMEM((rows, D), f32)


def run_self_forward(lengths, core, hidden, gain1, gain2, turned, u_self):
    rows = hidden.shape[0]
    heads = (lengths.shape[0], MAX_LEN, D)
    wide, low, flat = scratch_of(rows)
    return call(
        self_forward, "self_forward", 21,
        (shape((rows, D), bf16), shape(heads, bf16), shape(heads, bf16), shape(heads, bf16),
         shape(heads, f32), shape((rows, D), bf16), shape((rows, D), f32), shape((rows, D), bf16)),
        (lengths, core, hidden, gain1, gain2, turned, *u_self),
        [wide, wide, wide, wide, SQUARE] + WEIGHTS,
        in_specs=[SMEM] * 2 + [VMEM] * 4 + [ANY] * 2, out_specs=[VMEM] * 8)


def run_cross_forward(lengths, core, n2, h1, gain3, encoded, u_cross):
    rows = n2.shape[0]
    count = lengths.shape[0]
    heads = (count, MAX_LEN, D)
    wide, low, flat = scratch_of(rows)
    full = whole((rows, D))
    return call(
        cross_forward, "cross_forward", 34,
        (shape(encoded.shape, bf16), shape(encoded.shape, bf16), shape(heads, bf16),
         shape(heads, f32), shape((rows, D), bf16), shape((rows, D), f32), shape((rows, D), bf16)),
        (lengths, core, n2, h1, gain3, encoded, *u_cross),
        [wide, wide] + WEIGHTS,
        grid=(count,),
        in_specs=[SMEM] * 2 + [full, full, LINE, ENC_BLOCK, ANY, ANY],
        out_specs=[ENC_BLOCK, ENC_BLOCK, SEQ_BLOCK, SEQ_BLOCK, full, full, full])


def run_feed_forward(lengths, group_ids, group_steps, group_weights, tags, mask, out_grad, n3, h2,
                     gain3, u_ffn):
    rows = n3.shape[0]
    quarter = D // 4
    wide, low, flat = scratch_of(rows)
    full = whole((rows, D))
    column = whole((rows, 1))
    x_block = pl.BlockSpec((4, 1, quarter, D), lambda g: (0, g, 0, 0))
    r_block = pl.BlockSpec((1, 4, quarter, D), lambda g: (g, 1, 0, 0))
    return call(
        feed_forward, "feed_forward", 32,
        (shape((rows, D), bf16), shape((8, 4, quarter, D), bf16),
         shape((rows, D), f32), shape((1, D), f32)),
        (lengths, group_ids, group_steps, group_weights, tags, mask, out_grad, n3, h2, gain3,
         u_ffn, u_ffn),
        [low, flat, flat, low, low],
        grid=(4,),
        in_specs=[SMEM] * 4 + [column, column, full, full, full, LINE, x_block, r_block],
        out_specs=[full, whole((8, 4, quarter, D)), full, LINE])


def run_cross_backward(lengths, g2, crossed, cq, lse, ck, cv, encoded, n2, h1, gain2, core,
                       u_cross):
    rows = g2.shape[0]
    count = lengths.shape[0]
    wide, low, flat = scratch_of(rows)
    full = whole((rows, D))
    return call(
        cross_backward, "cross_backward", 42,
        (shape(encoded.shape, bf16), shape(encoded.shape, bf16), shape(HALVES, bf16),
         shape(HALVES, bf16), shape((rows, D), f32), shape((1, D), f32)),
        (lengths, g2, crossed, cq, lse, ck, cv, encoded, n2, h1, gain2, core, *u_cross),
        [wide, wide, wide, pltpu.VMEM((D, D), f32), pltpu.VMEM((D, D), f32), low, low, flat]
        + WEIGHTS,
        grid=(count,),
        in_specs=[SMEM, full, full, SEQ_BLOCK, SEQ_BLOCK, ENC_BLOCK, ENC_BLOCK, ENC_BLOCK, full,
                  full, LINE, SMEM, ANY, ANY],
        out_specs=[ENC_BLOCK, ENC_BLOCK, whole(HALVES), whole(HALVES), full, LINE])


def run_self_backward(lengths, g1, mixed, q, k, v, lse, n1, by_lag, core, u_self):
    rows = g1.shape[0]
    wide, low, flat = scratch_of(rows)
    return call(
        self_backward, "self_backward", 28,
        (shape((rows, D), bf16), shape((rows, D), bf16), shape((rows, D), bf16),
         shape(HALVES, bf16), shape(HALVES, bf16), shape((HEADS, MAX_LEN), f32)),
        (lengths, g1, mixed, q, k, v, lse, n1, by_lag, core, *u_self),
        [wide, wide, wide, wide, wide, low, SQUARE, SQUARE] + WEIGHTS,
        in_specs=[SMEM] + [VMEM] * 8 + [SMEM, ANY, ANY], out_specs=[VMEM] * 6)


def run_hidden_back(core, g1, hidden, gain1, dq, dk, dv, gg2, gg3, grad_lag, u_self):
    rows = g1.shape[0]
    wide, low, flat = scratch_of(rows)
    return call(
        hidden_back, "hidden_back", 8,
        (shape((rows, D), f32), shape((SMALL, D), bf16)),
        (core, g1, hidden, gain1, dq, dk, dv, gg2, gg3, grad_lag, *u_self),
        [flat, pltpu.VMEM((SMALL, D), f32)] + WEIGHTS,
        in_specs=[SMEM] + [VMEM] * 9 + [ANY] * 2, out_specs=[VMEM] * 2)


def run_encoded_back(core, dck, dcv, u_cross):
    return call(
        encoded_back, "encoded_back", 10,
        (shape(dck.shape, f32),),
        (core, dck, dcv, *u_cross),
        WEIGHTS,
        grid=(dck.shape[0] // ENC_LEN,),
        in_specs=[SMEM, ENC_BLOCK, ENC_BLOCK, ANY, ANY], out_specs=[ENC_BLOCK])


def add_all(parts):
    total = parts[0].astype(f32)
    for part in parts[1:]:
        total = total + part.astype(f32)
    return total.astype(bf16)


def tie(value, *after):
    return lax.optimization_barrier((value, *after))[0]


def tie_all(values, *after):
    return lax.optimization_barrier((*values, *after))[:len(values)]


def per_device(
    hidden, encoded, out_grad, lengths, group_ids, id_tags, loss_mask, group_steps, group_weights,
    gain_self, gain_cross, gain_ffn, rel_bias,
    query_weight, key_weight, value_weight, output_weight,
    cross_query, cross_key, cross_value, cross_output, expand_weight, reduce_weight,
):
    rows = hidden.shape[0]
    count = lengths.shape[0]
    quarter = D // 4
    routes = Routes()
    core = routes.core.reshape(1)
    size = D // routes.parts

    def piece_of(parts, index, extent):
        return lax.dynamic_slice_in_dim(jnp.concatenate(parts, 0), index * extent, extent, 0)

    small = jnp.concatenate([gain_self, gain_cross, gain_ffn, rel_bias.reshape(-1)])
    small_row = jnp.pad(small[None], ((0, 15), (0, D - small.shape[0])))
    own = piece_of([query_weight, key_weight, value_weight, output_weight],
                   routes.piece_index(), size)
    first = lax.all_gather(jnp.concatenate([own, small_row], 0)[None], "fsdp", axis=0, tiled=True)
    small = first[:, size, :small.shape[0]].astype(f32)
    cross_own = piece_of([cross_query, cross_key, cross_value, cross_output],
                         routes.piece_index(), size)
    self_piece = first[:, :size]
    for step in routes.steps[:0:-1]:
        self_piece = routes.join(self_piece, routes.swap(self_piece, step), step)
    cross_piece = routes.gather_shards(tie(cross_own, self_piece))
    step = routes.steps[0]
    self_piece = routes.join(self_piece, tie(routes.swap(self_piece, step), cross_piece), step)
    for step in routes.steps[:0:-1]:
        got = routes.swap(tie(cross_piece, self_piece), step)
        cross_piece = routes.join(cross_piece, got, step)
    self_other = tie(routes.swap_core(self_piece), cross_piece)
    cross_last = routes.swap(cross_piece, routes.steps[0])
    u_self = [half.reshape(HALVES) for half in (self_piece, self_other)]
    ratio = routes.parts // 8
    slot, offset = routes.dp // ratio, (routes.dp % ratio) * (quarter // ratio)
    own = jnp.where(
        slot < 4,
        lax.dynamic_slice(expand_weight, (offset, jnp.minimum(slot, 3) * D), (quarter // ratio, D)),
        lax.dynamic_slice_in_dim(
            reduce_weight, jnp.maximum(slot - 4, 0) * quarter + offset, quarter // ratio, 0))
    u_ffn = lax.all_gather(tie(own, first), ("fsdp", "dp"), axis=0, tiled=True)
    u_ffn = u_ffn.reshape(4, 8, quarter, D)

    gain1 = small[:, 0:quarter].reshape(1, D)
    gain2 = small[:, quarter:2 * quarter].reshape(1, D)
    gain3 = small[:, 2 * quarter:3 * quarter].reshape(1, D)
    rel = small[:, 3 * quarter:].reshape(HEADS, BUCKETS)
    table = bucket_table()
    by_lag = jnp.dot(rel, jnp.asarray(table), precision=lax.Precision.HIGHEST)
    turned = jnp.dot(
        rel, jnp.asarray(table[:, (-np.arange(MAX_LEN)) % MAX_LEN]), precision=lax.Precision.HIGHEST)

    n1, q, k, v, lse, mixed, h1, n2 = run_self_forward(
        lengths, core, hidden, gain1, gain2, turned, u_self)
    cross_piece = routes.join(cross_piece, tie(cross_last, n2), routes.steps[0])
    u_cross = [half.reshape(HALVES) for half in (cross_piece, routes.swap_core(cross_piece))]
    ck, cv, cq, cross_lse, crossed, h2, n3 = run_cross_forward(
        lengths, core, n2, h1, gain3, encoded, u_cross)
    layer_output, grad_ffn, g2, gg3 = run_feed_forward(
        lengths, group_ids, group_steps, group_weights, id_tags[:, None], loss_mask[:, None],
        out_grad, n3, h2, gain3, u_ffn)
    if routes.parts > 8:
        grad_ffn = grad_ffn.reshape(8, 4, routes.parts // 8, -1, D).swapaxes(1, 2)
    ffn_piece = lax.psum_scatter(
        grad_ffn.reshape(-1, D), "dp", scatter_dimension=0, tiled=True)

    dck, dcv, keep, send, g1, gg2 = run_cross_backward(
        lengths, g2, crossed, cq, cross_lse, ck, cv, encoded, n2, h1, gain2, core, u_cross)
    first_step, later_steps = routes.steps[0], routes.steps[1:]
    half = (4, D // 2, D)
    got = routes.swap_core(send.reshape(half))
    (grad_encoded,) = run_encoded_back(core, tie(dck, g1), dcv, u_cross)
    cross_total = add(keep.reshape(half), tie(got, grad_encoded))
    cross_keep, cross_got = routes.halve(cross_total, first_step)

    dq, dk, dv, keep, send, grad_lag = run_self_backward(
        lengths, tie(g1, cross_total), mixed, q, k, v, lse, n1, by_lag, core, u_self)
    cross_total = add(cross_keep, tie(cross_got, dq))
    got = routes.swap_core(tie(send, cross_total).reshape(half))
    for step in later_steps:
        cross_keep, cross_got = routes.halve(cross_total, step)
        if step is not later_steps[-1]:
            cross_total = add(cross_keep, cross_got)
    self_total = add(keep.reshape(half), got)
    self_keep, self_got = routes.halve(self_total, first_step)

    grad_hidden, small = run_hidden_back(
        core, g1, hidden, gain1, tie(dq, self_total), dk, dv, gg2, gg3, grad_lag, u_self)
    cross_total = add(cross_keep, tie(cross_got, grad_hidden))
    self_total = add(self_keep, tie(self_got, grad_hidden, cross_total))
    cross_parts = routes.send_shards(tie(cross_total, self_total))
    for step in later_steps:
        self_keep, self_got = routes.halve(self_total, step)
        if step is not later_steps[-1]:
            self_total = add(self_keep, self_got)
    self_total = add(self_keep, self_got)
    self_parts = routes.send_shards(jnp.concatenate(
        [self_total, jnp.broadcast_to(small[None], (4, SMALL, D))], axis=1))
    piece = jnp.concatenate(
        [add_all(self_parts), add_all(tie_all(cross_parts, self_total))], axis=0)

    ffn_piece = lax.psum_scatter(ffn_piece, "fsdp", scatter_dimension=0, tiled=True)
    ffn = lax.all_gather(ffn_piece, "dp", axis=0, tiled=True).astype(f32)

    mine, other = routes.collect(piece[None])
    mine = mine.reshape(routes.parts // 2, 2 * size + SMALL, D)
    other = other.reshape(routes.parts // 2, 2 * size + SMALL, D)
    small = jnp.sum(mine[:, size:size + SMALL].astype(f32), 0) + jnp.sum(
        other[:, size:size + SMALL].astype(f32), 0)
    gains = lax.dynamic_slice_in_dim(small[0:3], routes.z * quarter, quarter, 1)
    lag = lax.dynamic_slice_in_dim(small[3:3 + HEADS, :MAX_LEN], routes.z * (HEADS // 4), HEADS // 4, 0)
    grad_rel = lax.dot_general(
        lag, jnp.asarray(table), (((1,), (1,)), ((), ())), precision=lax.Precision.HIGHEST)

    def weight_grads(first):
        own = [value[:, first:first + size].reshape(2, quarter, D) for value in (mine, other)]
        lows = jnp.where(routes.core == 0, own[0], own[1]).astype(f32)
        highs = jnp.where(routes.core == 0, own[1], own[0]).astype(f32)
        return lows[0], lows[1], highs[0], highs[1]

    return (
        layer_output,
        grad_hidden,
        grad_encoded,
        gains[0],
        gains[1],
        gains[2],
        grad_rel,
        *weight_grads(0),
        *weight_grads(size + SMALL),
        jnp.concatenate([ffn[g * quarter:(g + 1) * quarter] for g in range(4)], axis=1),
        ffn[D:],
    )


def solution(mesh):
    rows = P(("dp", "fsdp"), None)
    flat = P(("dp", "fsdp"))
    shard = P("fsdp", None)
    line = P("fsdp")
    return jax.shard_map(
        per_device,
        mesh=mesh,
        in_specs=(rows, rows, rows, flat, flat, flat, flat, P(), P(), line, line, line) + (shard,) * 11,
        out_specs=(rows, rows, rows, line, line, line) + (shard,) * 11,
        check_vma=False,
    )
```

```python
from functools import partial
import math

import jax
import jax.numpy as jnp
import numpy as np
from jax import lax
from jax.experimental import pallas as pl
from jax.experimental.pallas import tpu as pltpu
from jax.sharding import PartitionSpec as P

HEADS = 12
HEAD = 64
PAIRS = 6
BUCKETS = 32
MAX_DIST = 128
ENC_LEN = 512
MAX_LEN = 256
GROUPS = 3
HORIZON = 10000
D = 768
COLS = 768
SMALL = 16

f32 = jnp.float32
bf16 = jnp.bfloat16
epsilon = 1e-06
masked_score = -1000000000.0

VMEM = pl.BlockSpec(memory_space=pltpu.VMEM)
SMEM = pl.BlockSpec(memory_space=pltpu.SMEM)
ANY = pl.BlockSpec(memory_space=pl.ANY)


def dot(left, right):
    return jnp.dot(left, right, preferred_element_type=f32)


def dot_nt(left, right):
    return lax.dot_general(left, right, (((1,), (1,)), ((), ())), preferred_element_type=f32)


def dot_tn(left, right):
    return lax.dot_general(left, right, (((0,), (0,)), ((), ())), preferred_element_type=f32)


def rounded(value):
    return value.astype(bf16).astype(f32)


def row_scale(rows):
    return lax.rsqrt(jnp.mean(rows * rows, axis=-1, keepdims=True) + epsilon)


def row_blocks(rows):
    return [slice(r, r + 128) for r in range(0, rows, 128)]


def col_blocks(width=D):
    return [slice(c, c + COLS) for c in range(0, width, COLS)]


def starts_of(len_ref):
    starts = [0]
    for s in range(3):
        starts.append(starts[-1] + len_ref[s])
    return starts


def norm_back(grad, rows, gain):
    r = row_scale(rows)
    pulled = gain * grad
    inner = jnp.mean(pulled * rows, axis=-1, keepdims=True)
    return r * pulled - rows * (r * r * r * inner), grad * rows * r


def split_three(value):
    high = value.astype(bf16)
    rest = value - high.astype(f32)
    mid = rest.astype(bf16)
    return high, mid, (rest - mid.astype(f32)).astype(bf16)


def weight_copies(core_ref, mine_ref, other_ref, w_s, sem):
    core = core_ref[0]
    quarter = D // 4
    copies = []
    for h, ref in enumerate((mine_ref, other_ref)):
        first = 2 * core if h == 0 else 2 * (1 - core)
        for z in range(4):
            copies.append(pltpu.make_async_copy(
                ref.at[z], w_s.at[pl.ds(first, 2), pl.ds(z * quarter, quarter), :],
                sem.at[4 * h + z]))
    return copies


def put_gradient(keep_ref, send_ref, core_ref, index, cb, value):
    value = value.astype(bf16).reshape(4, D // 4, COLS)
    stays = core_ref[0] == index // 2

    @pl.when(stays)
    def _():
        keep_ref[:, index % 2, :, cb] = value

    @pl.when(jnp.logical_not(stays))
    def _():
        send_ref[:, index % 2, :, cb] = value


def put_pairs(dst, cb, value):
    first = cb.start // 128
    for part in range(COLS // 128):
        dst[first + part, 0:value.shape[0], :] = value[:, part * 128:part * 128 + 128]


def clear_tail(dst, rows):
    dst[:, rows:, :] = jnp.zeros((PAIRS, dst.shape[1] - rows, 128), f32)


def join_pairs(dst, src, rows):
    for hp in range(PAIRS):
        dst[:, hp * 128:hp * 128 + 128] = src[hp, 0:rows, :].astype(dst.dtype)


def by_length(length, sizes, body):
    below = 0
    for size in sizes:
        fits = length > below if size == sizes[-1] else (length > below) & (length <= size)
        pl.when(fits)(lambda size=size: body(size))
        below = size


def clear_rows(ref, s, first):
    if first < MAX_LEN:
        ref[s, first:, :] = jnp.zeros((MAX_LEN - first, D), ref.dtype)


def start_of(len_ref, s):
    start = 0
    for t in range(3):
        start = start + jnp.where(s > t, len_ref[t], 0)
    return start


def lane_index(rows):
    return lax.broadcasted_iota(jnp.int32, (rows, 128), 1)


def self_forward(len_ref, core_ref, hid_ref, gain1_ref, gain2_ref, lag_ref, um_ref, uo_ref,
                 n1_ref, q_ref, k_ref, v_ref, lse_ref, mixed_ref, h1_ref, n2_ref,
                 q_s, k_s, v_s, m_s, bias_s, w_s, sem):
    copies = weight_copies(core_ref, um_ref, uo_ref, w_s, sem)
    for copy in copies:
        copy.start()
    rows = hid_ref.shape[0]
    count = q_ref.shape[0]
    for rb in row_blocks(rows):
        x = hid_ref[rb, :].astype(f32)
        n1_ref[rb, :] = (x * row_scale(x) * gain1_ref[...]).astype(bf16)
    for copy in copies:
        copy.wait()
    for w, dst in enumerate((q_s, k_s, v_s)):
        for cb in col_blocks():
            put_pairs(dst, cb, rounded(dot(n1_ref[...], w_s[w, :, cb])))
        clear_tail(dst, rows)
    starts = starts_of(len_ref)
    row = lax.broadcasted_iota(jnp.int32, (MAX_LEN, MAX_LEN), 0)
    col = lax.broadcasted_iota(jnp.int32, (MAX_LEN, MAX_LEN), 1)
    lane = lane_index(MAX_LEN)
    even = lane < HEAD

    def pair(hp, carry):
        cols = pl.ds(pl.multiple_of(hp * 128, 128), 128)
        for e in range(2):
            w = jnp.broadcast_to(lag_ref[pl.ds(2 * hp + e, 1), :], (MAX_LEN, MAX_LEN))
            table = pltpu.roll(w, 0, 1, stride=1, stride_axis=0)
            bias_s[e] = jnp.where(row >= col, table, masked_score)
        for s in range(count):
            window = pl.ds(starts[s], MAX_LEN)
            q = q_s[hp, window, :].astype(bf16)
            k = k_s[hp, window, :].astype(bf16)
            v = v_s[hp, window, :].astype(bf16)
            q_ref[s, :, cols] = q
            k_ref[s, :, cols] = k
            v_ref[s, :, cols] = v
            res, tops = [], []
            for e in range(2):
                mine = even if e == 0 else ~even
                score = dot_nt(jnp.where(mine, q, 0), k) + bias_s[e]
                top = jnp.max(score, axis=-1, keepdims=True)
                p = jnp.exp(score - top).astype(bf16)
                res.append(dot(p, jnp.where(mine, v, 1)))
                tops.append(top)
            num = jnp.where(even, res[0], res[1])
            den = jnp.where(even, pltpu.roll(res[0], HEAD, 1), pltpu.roll(res[1], HEAD, 1))
            lse_ref[s, :, cols] = jnp.where(even, tops[0], tops[1]) + jnp.log(den)
            m_s[hp, window, :] = num / den
        return carry

    lax.fori_loop(0, PAIRS, pair, 0, unroll=2)
    join_pairs(mixed_ref, m_s, rows)
    for cb in col_blocks():
        h1_ref[:, cb] = hid_ref[:, cb].astype(f32) + dot(mixed_ref[...], w_s[3, :, cb])
    for rb in row_blocks(rows):
        x = h1_ref[rb, :]
        n2_ref[rb, :] = (x * row_scale(x) * gain2_ref[...]).astype(bf16)


def cross_forward(len_ref, core_ref, n2_ref, h1_ref, gain3_ref, enc_ref, um_ref, uo_ref,
                  ck_ref, cv_ref, cq_ref, lse_ref, crossed_ref, h2_ref, n3_ref,
                  q_s, m_s, w_s, sem):
    s = pl.program_id(0)
    rows = n2_ref.shape[0]
    count = pl.num_programs(0)

    @pl.when(s == 0)
    def _():
        copies = weight_copies(core_ref, um_ref, uo_ref, w_s, sem)
        for copy in copies:
            copy.start()
        for copy in copies:
            copy.wait()
        for cb in col_blocks():
            put_pairs(q_s, cb, rounded(dot(n2_ref[...], w_s[0, :, cb])))
        clear_tail(q_s, rows)

    for cb in col_blocks():
        ck_ref[:, cb] = dot(enc_ref[...], w_s[1, :, cb]).astype(bf16)
        cv_ref[:, cb] = dot(enc_ref[...], w_s[2, :, cb]).astype(bf16)
    start = start_of(len_ref, s)
    even_v = lane_index(ENC_LEN) < HEAD

    def attend(size):
        window = pl.ds(start, size)
        even = lane_index(size) < HEAD
        clear_rows(cq_ref, 0, size)
        clear_rows(lse_ref, 0, size)

        def pair(hp, carry):
            cols = pl.ds(pl.multiple_of(hp * 128, 128), 128)
            q = q_s[hp, window, :].astype(bf16)
            cq_ref[0, 0:size, cols] = q
            k = ck_ref[:, cols]
            v = cv_ref[:, cols]
            res, tops = [], []
            for e in range(2):
                mine = even if e == 0 else ~even
                mine_v = even_v if e == 0 else ~even_v
                score = dot_nt(jnp.where(mine, q, 0), k)
                top = jnp.max(score, axis=-1, keepdims=True)
                p = jnp.exp(score - top).astype(bf16)
                res.append(dot(p, jnp.where(mine_v, v, 1)))
                tops.append(top)
            num = jnp.where(even, res[0], res[1])
            den = jnp.where(even, pltpu.roll(res[0], HEAD, 1), pltpu.roll(res[1], HEAD, 1))
            lse_ref[0, 0:size, cols] = jnp.where(even, tops[0], tops[1]) + jnp.log(den)
            m_s[hp, window, :] = num / den
            return carry

        lax.fori_loop(0, PAIRS, pair, 0, unroll=3)

    by_length(len_ref[s], (64, 128, 192, 256), attend)

    @pl.when(s == count - 1)
    def _():
        join_pairs(crossed_ref, m_s, rows)
        for cb in col_blocks():
            h2_ref[:, cb] = h1_ref[:, cb] + dot(crossed_ref[...], w_s[3, :, cb])
        for rb in row_blocks(rows):
            x = h2_ref[rb, :]
            n3_ref[rb, :] = (x * row_scale(x) * gain3_ref[...]).astype(bf16)


def gelu_parts(x):
    decay = jnp.exp(-0.5 * (x * x))
    t = 1.0 / (1.0 + jnp.abs(x) * (0.3275911 / math.sqrt(2.0)))
    poly = t * (0.5 * 0.254829592 + t * (-0.5 * 0.284496736 + t * (
        0.5 * 1.421413741 + t * (-0.5 * 1.453152027 + t * (0.5 * 1.061405429)))))
    tail = poly * decay
    below = jnp.where(x >= 0, 1.0 - tail, tail)
    return x * below, below + x * decay * (1.0 / math.sqrt(2.0 * math.pi))


def feed_forward(len_ref, group_ref, step_ref, weight_ref, tags_ref, mask_ref, og_ref, n3_ref,
                 h2_ref, gain3_ref, x_ref, r_ref,
                 out_ref, gu_ref, g2_ref, gg_ref,
                 scaled_s, out_s, dn_s, act_s, de_s, gu_s, sem):
    g = pl.program_id(0)
    count = 4

    def copies(g):
        return (pltpu.make_async_copy(gu_s.at[g], gu_ref.at[g], sem.at[g]),
                pltpu.make_async_copy(
                    gu_s.at[pl.ds(4, 4), g], gu_ref.at[pl.ds(4, 4), g], sem.at[count + g]))

    rows = n3_ref.shape[0]

    def token_weight(rb):
        index = lax.broadcasted_iota(jnp.int32, (128, 1), 0) + rb.start
        scale = jnp.zeros((128, 1), f32)
        tagged = jnp.zeros((128, 1), jnp.int32)
        start = 0
        for s in range(4):
            group = group_ref[s]
            factor = jnp.float32(0.0)
            for k in range(GROUPS):
                value = weight_ref[k].astype(f32) * 0.25 * (
                    1.0 - step_ref[k].astype(f32) * (1.0 / (2.0 * HORIZON)))
                factor = jnp.where(group == k, value, factor)
            inside = index >= start
            scale = jnp.where(inside, factor, scale)
            tagged = jnp.where(inside, jnp.where(group == 1, 1, 0), tagged)
            start = start + len_ref[s]
        counted = jnp.where(tagged == 1, tags_ref[rb, :], mask_ref[rb, :]).astype(f32)
        return scale * (0.25 + 0.75 * counted)

    @pl.when(g == 0)
    def _():
        for rb in row_blocks(rows):
            scaled = og_ref[rb, :].astype(f32) * token_weight(rb)
            g2_ref[rb, :] = scaled
            scaled_s[rb, :] = scaled.astype(bf16)
        out_s[...] = h2_ref[...]
        dn_s[...] = jnp.zeros(dn_s.shape, f32)

    for cb in col_blocks():
        expanded = dot(n3_ref[...], x_ref[:, 0, :, cb].reshape(D, COLS))
        act, slope = gelu_parts(expanded)
        act_s[:, cb] = act.astype(bf16)
        back = dot_nt(scaled_s[...], r_ref[0].reshape(D, D)[cb, :])
        de_s[:, cb] = (back * slope).astype(bf16)
    for cb in col_blocks():
        out_s[:, cb] += dot(act_s[...], r_ref[0, :, :, cb].reshape(D, COLS))
        gx = dot_tn(n3_ref[...], de_s[:, cb]).astype(bf16)
        gr = dot_tn(act_s[...], scaled_s[:, cb]).astype(bf16)
        gu_s[g, :, :, cb] = gx.reshape(4, D // 4, COLS)
        for part in range(4):
            gu_s[4 + part, g, :, cb] = gr[part * (D // 4):(part + 1) * (D // 4), :]
    for copy in copies(g):
        copy.start()
    full = x_ref[:, 0].reshape(D, D)
    for cb in col_blocks():
        dn_s[:, cb] += dot_nt(de_s[...], full[cb, :])

    @pl.when(g == pl.num_programs(0) - 1)
    def _():
        total = jnp.zeros((1, D), f32)
        for rb in row_blocks(rows):
            out_ref[rb, :] = out_s[rb, :].astype(bf16)
            part, pulled = norm_back(dn_s[rb, :], h2_ref[rb, :], gain3_ref[...])
            g2_ref[rb, :] += part
            total = total + jnp.sum(pulled, axis=0, keepdims=True)
        gg_ref[...] = total
        for step in range(count):
            for copy in copies(step):
                copy.wait()


def head_sums(product):
    a = lax.broadcasted_iota(jnp.int32, (128, 128), 0) < HEAD
    b = lax.broadcasted_iota(jnp.int32, (128, 128), 1) < HEAD
    ones = (a == b).astype(bf16)
    high, mid, rest = split_three(product)
    return dot(high, ones) + dot(mid, ones) + dot(rest, ones)


def augment(base, minus, lane, e):
    mine = (lane < HEAD) if e == 0 else (lane >= HEAD)
    spot = HEAD if e == 0 else 0
    high, mid, rest = split_three(-minus)
    extra = jnp.where(lane == spot, high, jnp.where(lane == spot + 1, mid, jnp.where(
        lane == spot + 2, rest, jnp.zeros_like(high))))
    return jnp.where(mine, base, extra)


def ones_beside(base, lane, e):
    mine = (lane < HEAD) if e == 0 else (lane >= HEAD)
    return jnp.where(mine, base, 1)


def other_half(value):
    return pltpu.roll(value, HEAD, 1)


def cross_backward(len_ref, g2_ref, crossed_ref, cq_ref, lse_ref, ck_ref, cv_ref, enc_ref, n2_ref,
                   h1_ref, gain2_ref, core_ref, um_ref, uo_ref,
                   dk_ref, dv_ref, keep_ref, send_ref, g1_ref, gg_ref,
                   dm_s, dd_s, dq_s, dk_s, dv_s, b2_s, dml_s, dn_s, enc_s, n2_s, h1_s, late,
                   w_s, sem):
    s = pl.program_id(0)
    rows = g2_ref.shape[0]
    early = [pltpu.make_async_copy(src, dst, late.at[i])
             for i, (src, dst) in enumerate(((enc_ref, enc_s), (n2_ref, n2_s), (h1_ref, h1_s)))]

    def results(s):
        part = pl.ds(pl.multiple_of(s * ENC_LEN, ENC_LEN), ENC_LEN)
        return [pltpu.make_async_copy(src.at[part], dst.at[part], late.at[3 + 4 * i + s])
                for i, (src, dst) in enumerate(((dk_s, dk_ref), (dv_s, dv_ref)))]

    @pl.when(s == 0)
    def _():
        copies = weight_copies(core_ref, um_ref, uo_ref, w_s, sem)
        for copy in copies:
            copy.start()
        b2_s[...] = g2_ref[...].astype(bf16)
        for cb in col_blocks():
            put_gradient(keep_ref, send_ref, core_ref, 3, cb,
                         dot_tn(crossed_ref[...], b2_s[:, cb]))
        for copy in copies:
            copy.wait()
        for cb in col_blocks():
            put_pairs(dm_s, cb, rounded(dot_nt(b2_s[...], w_s[3, cb, :])))
        for copy in early:
            copy.start()
        clear_tail(dm_s, rows)
        clear_tail(dd_s, rows)
        for hp in range(PAIRS):
            cols = slice(hp * 128, hp * 128 + 128)
            dd_s[hp, 0:rows, :] = head_sums(dm_s[hp, 0:rows, :] * crossed_ref[:, cols].astype(f32))

    start = 0
    length = len_ref[0]
    for t in range(3):
        start = start + jnp.where(s > t, len_ref[t], 0)
        length = jnp.where(s == t + 1, len_ref[t + 1], length)
    lane = lane_index(MAX_LEN)
    lane_k = lane_index(ENC_LEN)
    valid = lax.broadcasted_iota(jnp.int32, (MAX_LEN, 128), 0) < length
    window = pl.ds(start, MAX_LEN)
    part = pl.ds(pl.multiple_of(s * ENC_LEN, ENC_LEN), ENC_LEN)

    def pair(hp, carry):
        cols = pl.ds(pl.multiple_of(hp * 128, 128), 128)
        q = cq_ref[0, :, cols]
        k = ck_ref[:, cols]
        v = cv_ref[:, cols]
        lse = other_half(lse_ref[0, :, cols])
        dm = jnp.where(valid, dm_s[hp, window, :], 0.0).astype(bf16)
        dd = other_half(jnp.where(valid, dd_s[hp, window, :], 0.0))
        dq = dk = dv = None
        for e in range(2):
            score = dot_nt(ones_beside(k, lane_k, e), augment(q, lse, lane, e))
            p = jnp.exp(score)
            back = dot_nt(ones_beside(v, lane_k, e), augment(dm, dd, lane, e))
            ds = (p * back).astype(bf16)
            mine = (lane < HEAD) if e == 0 else (lane >= HEAD)
            mine_k = (lane_k < HEAD) if e == 0 else (lane_k >= HEAD)
            dv_e = dot(p.astype(bf16), jnp.where(mine, dm, 0))
            dk_e = dot(ds, jnp.where(mine, q, 0))
            dq_e = dot_tn(ds, jnp.where(mine_k, k, 0))
            dq, dk, dv = (dq_e, dk_e, dv_e) if e == 0 else (dq + dq_e, dk + dk_e, dv + dv_e)
        dq_s[hp, window, :] = dq
        dk_s[part, cols] = dk.astype(bf16)
        dv_s[part, cols] = dv.astype(bf16)
        return carry

    lax.fori_loop(0, PAIRS, pair, 0, unroll=2)
    for copy in results(s):
        copy.start()

    @pl.when(s == pl.num_programs(0) - 1)
    def _():
        join_pairs(dml_s, dq_s, rows)
        for copy in early:
            copy.wait()
        for cb in col_blocks():
            put_gradient(keep_ref, send_ref, core_ref, 0, cb, dot_tn(n2_s[...], dml_s[:, cb]))
            put_gradient(keep_ref, send_ref, core_ref, 1, cb, dot_tn(enc_s[...], dk_s[:, cb]))
            put_gradient(keep_ref, send_ref, core_ref, 2, cb, dot_tn(enc_s[...], dv_s[:, cb]))
            dn_s[:, cb] = dot_nt(dml_s[...], w_s[0, cb, :])
        total = jnp.zeros((1, D), f32)
        for rb in row_blocks(rows):
            part, pulled = norm_back(dn_s[rb, :], h1_s[rb, :], gain2_ref[...])
            g1_ref[rb, :] = g2_ref[rb, :] + part
            total = total + jnp.sum(pulled, axis=0, keepdims=True)
        gg_ref[...] = total
        for step in range(4):
            for copy in results(step):
                copy.wait()


def encoded_back(core_ref, dk_ref, dv_ref, um_ref, uo_ref, ge_ref, w_s, sem):
    @pl.when(pl.program_id(0) == 0)
    def _():
        copies = weight_copies(core_ref, um_ref, uo_ref, w_s, sem)
        for copy in copies:
            copy.start()
        for copy in copies:
            copy.wait()

    for cb in col_blocks():
        ge_ref[:, cb] = dot_nt(dk_ref[...], w_s[1, cb, :]) + dot_nt(dv_ref[...], w_s[2, cb, :])


def diagonal_sums(ref):
    total = ref[0:8, :]
    for r in range(8, MAX_LEN, 8):
        total = total + pltpu.roll(ref[r:r + 8, :], MAX_LEN - r, 1)
    row = lax.broadcasted_iota(jnp.int32, (8, MAX_LEN), 0)
    for bit in (1, 2, 4):
        total = jnp.where((row & bit) != 0, pltpu.roll(total, MAX_LEN - bit, 1), total)
    return jnp.sum(total, axis=0, keepdims=True)


def self_backward(len_ref, g1_ref, mixed_ref, q_ref, k_ref, v_ref, lse_ref, n1_ref,
                  lag_ref, core_ref, um_ref, uo_ref,
                  dq_ref, dk_ref, dv_ref, keep_ref, send_ref, gl_ref,
                  dm_s, dd_s, dq_s, dk_s, dv_s, b1_s, bias_s, acc_s, qh_s, kh_s, vh_s, lh_s, late,
                  w_s, sem):
    early = [pltpu.make_async_copy(src, dst, late.at[i]) for i, (src, dst) in enumerate(
        ((q_ref, qh_s), (k_ref, kh_s), (v_ref, vh_s), (lse_ref, lh_s)))]
    copies = weight_copies(core_ref, um_ref, uo_ref, w_s, sem)
    for copy in copies:
        copy.start()
    for copy in early:
        copy.start()
    rows = g1_ref.shape[0]
    count = q_ref.shape[0]
    b1_s[...] = g1_ref[...].astype(bf16)
    for cb in col_blocks():
        put_gradient(keep_ref, send_ref, core_ref, 3, cb, dot_tn(mixed_ref[...], b1_s[:, cb]))
    for copy in copies:
        copy.wait()
    for cb in col_blocks():
        put_pairs(dm_s, cb, rounded(dot_nt(b1_s[...], w_s[3, cb, :])))
    clear_tail(dm_s, rows)
    clear_tail(dd_s, rows)
    for hp in range(PAIRS):
        cols = slice(hp * 128, hp * 128 + 128)
        dd_s[hp, 0:rows, :] = head_sums(dm_s[hp, 0:rows, :] * mixed_ref[:, cols].astype(f32))
    starts = starts_of(len_ref)
    row = lax.broadcasted_iota(jnp.int32, (MAX_LEN, MAX_LEN), 0)
    col = lax.broadcasted_iota(jnp.int32, (MAX_LEN, MAX_LEN), 1)
    lane = lane_index(MAX_LEN)
    index = lax.broadcasted_iota(jnp.int32, (MAX_LEN, 128), 0)

    for copy in early:
        copy.wait()

    def pair(hp, carry):
        cols = pl.ds(pl.multiple_of(hp * 128, 128), 128)
        for e in range(2):
            w = jnp.broadcast_to(lag_ref[pl.ds(2 * hp + e, 1), :], (MAX_LEN, MAX_LEN))
            table = pltpu.roll(w, 0, 1, stride=1, stride_axis=0)
            bias_s[e] = jnp.where(col >= row, table, masked_score)
        for s in range(count):
            valid = index < len_ref[s]
            window = pl.ds(starts[s], MAX_LEN)
            q = qh_s[s, :, cols]
            k = kh_s[s, :, cols]
            v = vh_s[s, :, cols]
            lse = other_half(lh_s[s, :, cols])
            dm = jnp.where(valid, dm_s[hp, window, :], 0.0).astype(bf16)
            dd = other_half(jnp.where(valid, dd_s[hp, window, :], 0.0))
            dq = dk = dv = None
            for e in range(2):
                score = dot_nt(ones_beside(k, lane, e), augment(q, lse, lane, e)) + bias_s[e]
                p = jnp.exp(score)
                back = dot_nt(ones_beside(v, lane, e), augment(dm, dd, lane, e))
                grad = p * back
                if s == 0:
                    acc_s[e] = grad
                else:
                    acc_s[e] += grad
                ds = grad.astype(bf16)
                mine = (lane < HEAD) if e == 0 else (lane >= HEAD)
                dv_e = dot(p.astype(bf16), jnp.where(mine, dm, 0))
                dk_e = dot(ds, jnp.where(mine, q, 0))
                dq_e = dot_tn(ds, jnp.where(mine, k, 0))
                dq, dk, dv = (dq_e, dk_e, dv_e) if e == 0 else (dq + dq_e, dk + dk_e, dv + dv_e)
            dq_s[hp, window, :] = dq
            dk_s[hp, window, :] = dk
            dv_s[hp, window, :] = dv
        for e in range(2):
            gl_ref[pl.ds(2 * hp + e, 1), :] = diagonal_sums(acc_s.at[e])
        return carry

    lax.fori_loop(0, PAIRS, pair, 0, unroll=2)
    for w, (src, out) in enumerate(((dq_s, dq_ref), (dk_s, dk_ref), (dv_s, dv_ref))):
        join_pairs(out, src, rows)
        for cb in col_blocks():
            put_gradient(keep_ref, send_ref, core_ref, w, cb, dot_tn(n1_ref[...], out[:, cb]))


def hidden_back(core_ref, g1_ref, hid_ref, gain1_ref, dq_ref, dk_ref, dv_ref, gg2_ref, gg3_ref,
                gl_ref, um_ref, uo_ref, gh_ref, small_ref, dn_s, small_s, w_s, sem):
    copies = weight_copies(core_ref, um_ref, uo_ref, w_s, sem)
    for copy in copies:
        copy.start()
    for copy in copies:
        copy.wait()
    rows = g1_ref.shape[0]
    for cb in col_blocks():
        dn_s[:, cb] = (dot_nt(dq_ref[...], w_s[0, cb, :]) + dot_nt(dk_ref[...], w_s[1, cb, :])
                       + dot_nt(dv_ref[...], w_s[2, cb, :]))
    total = jnp.zeros((1, D), f32)
    for rb in row_blocks(rows):
        part, pulled = norm_back(dn_s[rb, :], hid_ref[rb, :].astype(f32), gain1_ref[...])
        gh_ref[rb, :] = g1_ref[rb, :] + part
        total = total + jnp.sum(pulled, axis=0, keepdims=True)
    small_s[...] = jnp.zeros(small_s.shape, f32)
    small_s[0:1, :] = total
    small_s[1:2, :] = gg2_ref[...]
    small_s[2:3, :] = gg3_ref[...]
    small_s[3:3 + HEADS, 0:MAX_LEN] = gl_ref[...]
    small_ref[...] = small_s[...].astype(bf16)


def bucket_table():
    lags = np.arange(MAX_LEN)
    exact = BUCKETS // 2
    bucket = np.minimum(lags, exact)
    for step in range(1, exact):
        edge = math.ceil(exact * (MAX_DIST / exact) ** (step / exact))
        bucket = bucket + (lags >= edge)
    return (bucket[None, :] == np.arange(BUCKETS)[:, None]).astype(np.float32)


def shape(dims, kind):
    return jax.ShapeDtypeStruct(dims, kind)


def call(kernel, name, micros, grant, outs, ins, scratch, **extra):
    return pl.pallas_call(
        kernel,
        out_shape=list(outs),
        name=name,
        scratch_shapes=scratch,
        cost_estimate=pl.CostEstimate(
            flops=int(micros * 1e9), bytes_accessed=1 << 20, transcendentals=0),
        compiler_params=pltpu.CompilerParams(vmem_limit_bytes=grant << 20),
        **extra,
    )(*ins)


def whole(array_shape):
    zeros = (0,) * len(array_shape)
    return pl.BlockSpec(array_shape, lambda s: zeros)


class Routes:
    def __init__(self):
        self.parts = lax.axis_size("dp")
        self.shards = lax.axis_size("fsdp")
        self.dp = lax.axis_index("dp")
        self.z = lax.axis_index("fsdp")
        self.core = self.dp & 1
        bits = list(range(1, self.parts.bit_length() - 1))
        self.steps = list(zip(bits, bits[::-1]))

    def permute(self, value, partner):
        pairs = []
        for dp in range(self.parts):
            for z in range(self.shards):
                to_dp, to_z = partner(dp, z)
                pairs.append((dp * self.shards + z, to_dp * self.shards + to_z))
        return lax.ppermute(value, ("dp", "fsdp"), pairs)

    def swap_core(self, value):
        return self.permute(value, lambda dp, z: (dp ^ 1, z))

    def swap(self, value, step):
        return self.permute(value, lambda dp, z: (dp ^ (1 << step[dp & 1]), z))

    def shift(self, value, by):
        return self.permute(value, lambda dp, z: (dp, (z + by) % self.shards))

    def bit(self, step):
        return jnp.where(self.core == 0, (self.dp >> step[0]) & 1, (self.dp >> step[1]) & 1)

    def piece_index(self):
        index = self.core
        for step in self.steps:
            index = 2 * index + self.bit(step)
        return index

    def shift_all(self, own):
        return [own] + [self.shift(own, by) for by in range(1, self.shards)]

    def stack_shards(self, got):
        return jnp.stack([
            lax.select_n((self.z - z) % self.shards, *got) for z in range(self.shards)])

    def collect(self, piece):
        for step in reversed(self.steps):
            piece = self.join(piece, self.swap(piece, step), step)
        return piece, self.swap_core(piece)

    def join(self, piece, got, step):
        return jnp.where(self.bit(step) == 0, jnp.concatenate([piece, got], 1),
                         jnp.concatenate([got, piece], 1))

    def halve(self, total, step):
        size = total.shape[1] // 2
        bit = self.bit(step)
        send = lax.dynamic_slice_in_dim(total, (1 - bit) * size, size, 1)
        keep = lax.dynamic_slice_in_dim(total, bit * size, size, 1)
        return keep, self.swap(send, step)

    def send_shards(self, total):
        parts = [lax.dynamic_index_in_dim(total, self.z, 0, keepdims=False)]
        for by in range(1, self.shards):
            chunk = lax.dynamic_index_in_dim(total, (self.z + by) % self.shards, 0, keepdims=False)
            parts.append(self.shift(chunk, by))
        return parts


def add(left, right):
    return (left.astype(f32) + right.astype(f32)).astype(bf16)


HALVES = (4, 2, D // 4, D)
WEIGHTS = [pltpu.VMEM((4, D, D), bf16), pltpu.SemaphoreType.DMA((8,))]
SQUARE = pltpu.VMEM((2, MAX_LEN, MAX_LEN), f32)
LINE = whole((1, D))
ENC_BLOCK = pl.BlockSpec((ENC_LEN, D), lambda s: (s, 0))
SEQ_BLOCK = pl.BlockSpec((1, MAX_LEN, D), lambda s: (s, 0, 0))


def scratch_of(rows):
    wide = pltpu.VMEM((PAIRS, rows + MAX_LEN, 128), f32)
    return wide, pltpu.VMEM((rows, D), bf16), pltpu.VMEM((rows, D), f32)


def run_self_forward(lengths, core, hidden, gain1, gain2, turned, u_self):
    rows = hidden.shape[0]
    heads = (lengths.shape[0], MAX_LEN, D)
    wide, low, flat = scratch_of(rows)
    return call(
        self_forward, "self_forward", 21, 40,
        (shape((rows, D), bf16), shape(heads, bf16), shape(heads, bf16), shape(heads, bf16),
         shape(heads, f32), shape((rows, D), bf16), shape((rows, D), f32), shape((rows, D), bf16)),
        (lengths, core, hidden, gain1, gain2, turned, *u_self),
        [wide, wide, wide, wide, SQUARE] + WEIGHTS,
        in_specs=[SMEM] * 2 + [VMEM] * 4 + [ANY] * 2, out_specs=[VMEM] * 8)


def run_cross_forward(lengths, core, n2, h1, gain3, encoded, u_cross):
    rows = n2.shape[0]
    count = lengths.shape[0]
    heads = (count, MAX_LEN, D)
    wide, low, flat = scratch_of(rows)
    full = whole((rows, D))
    return call(
        cross_forward, "cross_forward", 34, 60,
        (shape(encoded.shape, bf16), shape(encoded.shape, bf16), shape(heads, bf16),
         shape(heads, f32), shape((rows, D), bf16), shape((rows, D), f32), shape((rows, D), bf16)),
        (lengths, core, n2, h1, gain3, encoded, *u_cross),
        [wide, wide] + WEIGHTS,
        grid=(count,),
        in_specs=[SMEM] * 2 + [full, full, LINE, ENC_BLOCK, ANY, ANY],
        out_specs=[ENC_BLOCK, ENC_BLOCK, SEQ_BLOCK, SEQ_BLOCK, full, full, full])


def run_feed_forward(lengths, group_ids, group_steps, group_weights, tags, mask, out_grad, n3, h2,
                     gain3, u_ffn):
    rows = n3.shape[0]
    quarter = D // 4
    wide, low, flat = scratch_of(rows)
    full = whole((rows, D))
    column = whole((rows, 1))
    x_block = pl.BlockSpec((4, 1, quarter, D), lambda g: (0, g, 0, 0))
    r_block = pl.BlockSpec((1, 4, quarter, D), lambda g: (g, 1, 0, 0))
    return call(
        feed_forward, "feed_forward", 32, 60,
        (shape((rows, D), bf16), shape((8, 4, quarter, D), bf16),
         shape((rows, D), f32), shape((1, D), f32)),
        (lengths, group_ids, group_steps, group_weights, tags, mask, out_grad, n3, h2, gain3,
         u_ffn, u_ffn),
        [low, flat, flat, low, low, pltpu.VMEM((8, 4, quarter, D), bf16),
         pltpu.SemaphoreType.DMA((8,))],
        grid=(4,),
        in_specs=[SMEM] * 4 + [column, column, full, full, full, LINE, x_block, r_block],
        out_specs=[full, ANY, full, LINE])


def run_cross_backward(lengths, g2, crossed, cq, lse, ck, cv, encoded, n2, h1, gain2, core,
                       u_cross):
    rows = g2.shape[0]
    count = lengths.shape[0]
    wide, low, flat = scratch_of(rows)
    full = whole((rows, D))
    return call(
        cross_backward, "cross_backward", 42, 60,
        (shape(encoded.shape, bf16), shape(encoded.shape, bf16), shape(HALVES, bf16),
         shape(HALVES, bf16), shape((rows, D), f32), shape((1, D), f32)),
        (lengths, g2, crossed, cq, lse, ck, cv, encoded, n2, h1, gain2, core, *u_cross),
        [wide, wide, wide, pltpu.VMEM(encoded.shape, bf16), pltpu.VMEM(encoded.shape, bf16),
         low, low, flat, pltpu.VMEM(encoded.shape, bf16), low, flat,
         pltpu.SemaphoreType.DMA((11,))] + WEIGHTS,
        grid=(count,),
        in_specs=[SMEM, full, full, SEQ_BLOCK, SEQ_BLOCK, ENC_BLOCK, ENC_BLOCK, ANY, ANY,
                  ANY, LINE, SMEM, ANY, ANY],
        out_specs=[ANY, ANY, whole(HALVES), whole(HALVES), full, LINE])


def run_self_backward(lengths, g1, mixed, q, k, v, lse, n1, by_lag, core, u_self):
    rows = g1.shape[0]
    wide, low, flat = scratch_of(rows)
    return call(
        self_backward, "self_backward", 28, 60,
        (shape((rows, D), bf16), shape((rows, D), bf16), shape((rows, D), bf16),
         shape(HALVES, bf16), shape(HALVES, bf16), shape((HEADS, MAX_LEN), f32)),
        (lengths, g1, mixed, q, k, v, lse, n1, by_lag, core, *u_self),
        [wide, wide, wide, wide, wide, low, SQUARE, SQUARE]
        + [pltpu.VMEM(value.shape, value.dtype) for value in (q, k, v, lse)]
        + [pltpu.SemaphoreType.DMA((4,))] + WEIGHTS,
        in_specs=[SMEM, VMEM, VMEM, ANY, ANY, ANY, ANY, VMEM, VMEM, SMEM, ANY, ANY], out_specs=[VMEM] * 6)


def run_hidden_back(core, g1, hidden, gain1, dq, dk, dv, gg2, gg3, grad_lag, u_self):
    rows = g1.shape[0]
    wide, low, flat = scratch_of(rows)
    return call(
        hidden_back, "hidden_back", 8, 24,
        (shape((rows, D), f32), shape((SMALL, D), bf16)),
        (core, g1, hidden, gain1, dq, dk, dv, gg2, gg3, grad_lag, *u_self),
        [flat, pltpu.VMEM((SMALL, D), f32)] + WEIGHTS,
        in_specs=[SMEM] + [VMEM] * 9 + [ANY] * 2, out_specs=[VMEM] * 2)


def run_encoded_back(core, dck, dcv, u_cross):
    return call(
        encoded_back, "encoded_back", 10, 20,
        (shape(dck.shape, f32),),
        (core, dck, dcv, *u_cross),
        WEIGHTS,
        grid=(dck.shape[0] // ENC_LEN,),
        in_specs=[SMEM, ENC_BLOCK, ENC_BLOCK, ANY, ANY], out_specs=[ENC_BLOCK])


def add_all(parts):
    total = parts[0].astype(f32)
    for part in parts[1:]:
        total = total + part.astype(f32)
    return total.astype(bf16)


def tie(value, *after):
    return lax.optimization_barrier((value, *after))[0]


def tie_all(values, *after):
    return lax.optimization_barrier((*values, *after))[:len(values)]


def per_device(
    hidden, encoded, out_grad, lengths, group_ids, id_tags, loss_mask, group_steps, group_weights,
    gain_self, gain_cross, gain_ffn, rel_bias,
    query_weight, key_weight, value_weight, output_weight,
    cross_query, cross_key, cross_value, cross_output, expand_weight, reduce_weight,
):
    rows = hidden.shape[0]
    count = lengths.shape[0]
    quarter = D // 4
    routes = Routes()
    core = routes.core.reshape(1)
    size = D // routes.parts

    def piece_of(parts, index, extent):
        return lax.dynamic_slice_in_dim(jnp.concatenate(parts, 0), index * extent, extent, 0)

    small = jnp.concatenate([gain_self, gain_cross, gain_ffn, rel_bias.reshape(-1)])
    small_row = jnp.pad(small[None], ((0, 15), (0, D - small.shape[0])))
    own = piece_of([query_weight, key_weight, value_weight, output_weight],
                   routes.piece_index(), size)
    first = lax.all_gather(jnp.concatenate([own, small_row], 0)[None], "fsdp", axis=0, tiled=True)
    small = first[:, size, :small.shape[0]].astype(f32)
    cross_own = piece_of([cross_query, cross_key, cross_value, cross_output],
                         routes.piece_index(), size)
    self_piece = first[:, :size]
    cross_got = routes.shift_all(tie(cross_own, first))
    for step in routes.steps[:0:-1]:
        self_piece = routes.join(self_piece, routes.swap(self_piece, step), step)
    start_ffn = self_piece
    cross_piece = routes.stack_shards(tie_all(cross_got, self_piece))
    for step in routes.steps[:0:-1]:
        cross_piece = routes.join(cross_piece, routes.swap(cross_piece, step), step)
    step = routes.steps[0]
    self_piece = routes.join(self_piece, tie(routes.swap(self_piece, step), cross_piece), step)
    self_other = routes.swap_core(self_piece)
    cross_last = routes.swap(cross_piece, routes.steps[0])
    u_self = [half.reshape(HALVES) for half in (self_piece, self_other)]
    ratio = routes.parts // 8
    slot, offset = routes.dp // ratio, (routes.dp % ratio) * (quarter // ratio)
    own = jnp.where(
        slot < 4,
        lax.dynamic_slice(expand_weight, (offset, jnp.minimum(slot, 3) * D), (quarter // ratio, D)),
        lax.dynamic_slice_in_dim(
            reduce_weight, jnp.maximum(slot - 4, 0) * quarter + offset, quarter // ratio, 0))
    u_ffn = lax.all_gather(tie(own, start_ffn), ("fsdp", "dp"), axis=0, tiled=True)
    u_ffn = u_ffn.reshape(4, 8, quarter, D)

    gain1 = small[:, 0:quarter].reshape(1, D)
    gain2 = small[:, quarter:2 * quarter].reshape(1, D)
    gain3 = small[:, 2 * quarter:3 * quarter].reshape(1, D)
    rel = small[:, 3 * quarter:].reshape(HEADS, BUCKETS)
    table = bucket_table()
    by_lag = jnp.dot(rel, jnp.asarray(table), precision=lax.Precision.HIGHEST)
    turned = jnp.dot(
        rel, jnp.asarray(table[:, (-np.arange(MAX_LEN)) % MAX_LEN]), precision=lax.Precision.HIGHEST)

    n1, q, k, v, lse, mixed, h1, n2 = run_self_forward(
        lengths, core, hidden, gain1, gain2, turned, u_self)
    cross_piece = routes.join(cross_piece, tie(cross_last, n2), routes.steps[0])
    u_cross = [half.reshape(HALVES) for half in (cross_piece, routes.swap_core(cross_piece))]
    ck, cv, cq, cross_lse, crossed, h2, n3 = run_cross_forward(
        lengths, core, n2, h1, gain3, encoded, u_cross)
    layer_output, grad_ffn, g2, gg3 = run_feed_forward(
        lengths, group_ids, group_steps, group_weights, id_tags[:, None], loss_mask[:, None],
        out_grad, n3, h2, gain3, u_ffn)
    if routes.parts > 8:
        grad_ffn = grad_ffn.reshape(8, 4, routes.parts // 8, -1, D).swapaxes(1, 2)
    ffn_piece = lax.psum_scatter(
        grad_ffn.reshape(-1, D), "dp", scatter_dimension=0, tiled=True)

    dck, dcv, keep, send, g1, gg2 = run_cross_backward(
        lengths, g2, crossed, cq, cross_lse, ck, cv, encoded, n2, h1, gain2, core, u_cross)
    first_step, later_steps = routes.steps[0], routes.steps[1:]
    half = (4, D // 2, D)
    got = routes.swap_core(send.reshape(half))
    (grad_encoded,) = run_encoded_back(core, tie(dck, g1), dcv, u_cross)
    cross_total = add(keep.reshape(half), tie(got, grad_encoded))
    cross_keep, cross_got = routes.halve(cross_total, first_step)

    ffn_half = ffn_piece
    ffn_piece = lax.psum_scatter(ffn_piece, "fsdp", scatter_dimension=0, tiled=True)
    ffn = lax.all_gather(ffn_piece, "dp", axis=0, tiled=True).astype(f32)

    dq, dk, dv, keep, send, grad_lag = run_self_backward(
        lengths, tie(g1, cross_total), mixed, q, k, v, lse, n1, by_lag, core, u_self)
    cross_total = add(cross_keep, tie(cross_got, dq))
    got = routes.swap_core(tie(send, cross_total).reshape(half))
    for step in later_steps:
        cross_keep, cross_got = routes.halve(cross_total, step)
        if step is not later_steps[-1]:
            cross_total = add(cross_keep, cross_got)
    self_total = add(keep.reshape(half), tie(got, ffn_half))
    self_keep, self_got = routes.halve(self_total, first_step)

    grad_hidden, small = run_hidden_back(
        core, g1, hidden, gain1, tie(dq, self_total), dk, dv, gg2, gg3, grad_lag, u_self)
    cross_total = add(cross_keep, tie(cross_got, grad_hidden))
    self_total = add(self_keep, tie(self_got, grad_hidden, cross_total))
    cross_parts = routes.send_shards(tie(cross_total, self_total))
    for step in later_steps:
        self_keep, self_got = routes.halve(self_total, step)
        if step is not later_steps[-1]:
            self_total = add(self_keep, self_got)
    self_total = add(self_keep, self_got)
    self_parts = routes.send_shards(jnp.concatenate(
        [tie(self_total, ffn_piece), jnp.broadcast_to(small[None], (4, SMALL, D))], axis=1))
    piece = jnp.concatenate(
        [add_all(self_parts), add_all(tie_all(cross_parts, self_total))], axis=0)

    mine, other = routes.collect(piece[None])
    mine = mine.reshape(routes.parts // 2, 2 * size + SMALL, D)
    other = other.reshape(routes.parts // 2, 2 * size + SMALL, D)
    small = jnp.sum(mine[:, size:size + SMALL].astype(f32), 0) + jnp.sum(
        other[:, size:size + SMALL].astype(f32), 0)
    gains = lax.dynamic_slice_in_dim(small[0:3], routes.z * quarter, quarter, 1)
    lag = lax.dynamic_slice_in_dim(small[3:3 + HEADS, :MAX_LEN], routes.z * (HEADS // 4), HEADS // 4, 0)
    grad_rel = lax.dot_general(
        lag, jnp.asarray(table), (((1,), (1,)), ((), ())), precision=lax.Precision.HIGHEST)

    def weight_grads(first):
        own = [value[:, first:first + size].reshape(2, quarter, D) for value in (mine, other)]
        lows = jnp.where(routes.core == 0, own[0], own[1]).astype(f32)
        highs = jnp.where(routes.core == 0, own[1], own[0]).astype(f32)
        return lows[0], lows[1], highs[0], highs[1]

    return (
        layer_output,
        grad_hidden,
        grad_encoded,
        gains[0],
        gains[1],
        gains[2],
        grad_rel,
        *weight_grads(0),
        *weight_grads(size + SMALL),
        jnp.concatenate([ffn[g * quarter:(g + 1) * quarter] for g in range(4)], axis=1),
        ffn[D:],
    )


def solution(mesh):
    rows = P(("dp", "fsdp"), None)
    flat = P(("dp", "fsdp"))
    shard = P("fsdp", None)
    line = P("fsdp")
    return jax.shard_map(
        per_device,
        mesh=mesh,
        in_specs=(rows, rows, rows, flat, flat, flat, flat, P(), P(), line, line, line) + (shard,) * 11,
        out_specs=(rows, rows, rows, line, line, line) + (shard,) * 11,
        check_vma=False,
    )
```

```python
from functools import partial
import math

import jax
import jax.numpy as jnp
import numpy as np
from jax import lax
from jax.experimental import pallas as pl
from jax.experimental.pallas import tpu as pltpu
from jax.sharding import PartitionSpec as P

HEADS = 12
HEAD = 64
PAIRS = 6
BUCKETS = 32
MAX_DIST = 128
ENC_LEN = 512
MAX_LEN = 256
GROUPS = 3
HORIZON = 10000
D = 768
COLS = 768
SMALL = 16

f32 = jnp.float32
bf16 = jnp.bfloat16
epsilon = 1e-06
masked_score = -1000000000.0

VMEM = pl.BlockSpec(memory_space=pltpu.VMEM)
SMEM = pl.BlockSpec(memory_space=pltpu.SMEM)
ANY = pl.BlockSpec(memory_space=pl.ANY)


def dot(left, right):
    return jnp.dot(left, right, preferred_element_type=f32)


def dot_nt(left, right):
    return lax.dot_general(left, right, (((1,), (1,)), ((), ())), preferred_element_type=f32)


def dot_tn(left, right):
    return lax.dot_general(left, right, (((0,), (0,)), ((), ())), preferred_element_type=f32)


def rounded(value):
    return value.astype(bf16).astype(f32)


def row_scale(rows):
    return lax.rsqrt(jnp.mean(rows * rows, axis=-1, keepdims=True) + epsilon)


def row_blocks(rows):
    return [slice(r, r + 128) for r in range(0, rows, 128)]


def col_blocks(width=D):
    return [slice(c, c + COLS) for c in range(0, width, COLS)]


def starts_of(len_ref):
    starts = [0]
    for s in range(3):
        starts.append(starts[-1] + len_ref[s])
    return starts


def norm_back(grad, rows, gain):
    r = row_scale(rows)
    pulled = gain * grad
    inner = jnp.mean(pulled * rows, axis=-1, keepdims=True)
    return r * pulled - rows * (r * r * r * inner), grad * rows * r


def split_three(value):
    high = value.astype(bf16)
    rest = value - high.astype(f32)
    mid = rest.astype(bf16)
    return high, mid, (rest - mid.astype(f32)).astype(bf16)


def weight_copies(core_ref, mine_ref, other_ref, w_s, sem):
    core = core_ref[0]
    quarter = D // 4
    copies = []
    for h, ref in enumerate((mine_ref, other_ref)):
        first = 2 * core if h == 0 else 2 * (1 - core)
        for z in range(4):
            copies.append(pltpu.make_async_copy(
                ref.at[z], w_s.at[pl.ds(first, 2), pl.ds(z * quarter, quarter), :],
                sem.at[4 * h + z]))
    return copies


def put_gradient(keep_ref, send_ref, core_ref, index, cb, value):
    value = value.astype(bf16).reshape(4, D // 4, COLS)
    stays = core_ref[0] == index // 2

    @pl.when(stays)
    def _():
        keep_ref[:, index % 2, :, cb] = value

    @pl.when(jnp.logical_not(stays))
    def _():
        send_ref[:, index % 2, :, cb] = value


def put_pairs(dst, cb, value):
    first = cb.start // 128
    for part in range(COLS // 128):
        dst[first + part, 0:value.shape[0], :] = value[:, part * 128:part * 128 + 128]


def clear_tail(dst, rows):
    dst[:, rows:, :] = jnp.zeros((PAIRS, dst.shape[1] - rows, 128), f32)


def join_pairs(dst, src, rows):
    for hp in range(PAIRS):
        dst[:, hp * 128:hp * 128 + 128] = src[hp, 0:rows, :].astype(dst.dtype)


def by_length(length, sizes, body):
    below = 0
    for size in sizes:
        fits = length > below if size == sizes[-1] else (length > below) & (length <= size)
        pl.when(fits)(lambda size=size: body(size))
        below = size


def clear_rows(ref, s, first):
    if first < MAX_LEN:
        ref[s, first:, :] = jnp.zeros((MAX_LEN - first, D), ref.dtype)


def start_of(len_ref, s):
    start = 0
    for t in range(3):
        start = start + jnp.where(s > t, len_ref[t], 0)
    return start


def lane_index(rows):
    return lax.broadcasted_iota(jnp.int32, (rows, 128), 1)


def self_forward(len_ref, core_ref, hid_ref, gain1_ref, gain2_ref, lag_ref, um_ref, uo_ref,
                 n1_ref, q_ref, k_ref, v_ref, lse_ref, mixed_ref, h1_ref, n2_ref,
                 q_s, k_s, v_s, m_s, bias_s, w_s, sem):
    copies = weight_copies(core_ref, um_ref, uo_ref, w_s, sem)
    for copy in copies:
        copy.start()
    rows = hid_ref.shape[0]
    count = q_ref.shape[0]
    for rb in row_blocks(rows):
        x = hid_ref[rb, :].astype(f32)
        n1_ref[rb, :] = (x * row_scale(x) * gain1_ref[...]).astype(bf16)
    for copy in copies:
        copy.wait()
    for w, dst in enumerate((q_s, k_s, v_s)):
        for cb in col_blocks():
            put_pairs(dst, cb, rounded(dot(n1_ref[...], w_s[w, :, cb])))
        clear_tail(dst, rows)
    starts = starts_of(len_ref)
    row = lax.broadcasted_iota(jnp.int32, (MAX_LEN, MAX_LEN), 0)
    col = lax.broadcasted_iota(jnp.int32, (MAX_LEN, MAX_LEN), 1)
    lane = lane_index(MAX_LEN)
    even = lane < HEAD

    def pair(hp, carry):
        cols = pl.ds(pl.multiple_of(hp * 128, 128), 128)
        for e in range(2):
            w = jnp.broadcast_to(lag_ref[pl.ds(2 * hp + e, 1), :], (MAX_LEN, MAX_LEN))
            table = pltpu.roll(w, 0, 1, stride=1, stride_axis=0)
            bias_s[e] = jnp.where(row >= col, table, masked_score)
        for s in range(count):
            window = pl.ds(starts[s], MAX_LEN)
            q = q_s[hp, window, :].astype(bf16)
            k = k_s[hp, window, :].astype(bf16)
            v = v_s[hp, window, :].astype(bf16)
            q_ref[s, :, cols] = q
            k_ref[s, :, cols] = k
            v_ref[s, :, cols] = v
            res, tops = [], []
            for e in range(2):
                mine = even if e == 0 else ~even
                score = dot_nt(jnp.where(mine, q, 0), k) + bias_s[e]
                top = jnp.max(score, axis=-1, keepdims=True)
                p = jnp.exp(score - top).astype(bf16)
                res.append(dot(p, jnp.where(mine, v, 1)))
                tops.append(top)
            num = jnp.where(even, res[0], res[1])
            den = jnp.where(even, pltpu.roll(res[0], HEAD, 1), pltpu.roll(res[1], HEAD, 1))
            lse_ref[s, :, cols] = jnp.where(even, tops[0], tops[1]) + jnp.log(den)
            m_s[hp, window, :] = num / den
        return carry

    lax.fori_loop(0, PAIRS, pair, 0, unroll=2)
    join_pairs(mixed_ref, m_s, rows)
    for cb in col_blocks():
        h1_ref[:, cb] = hid_ref[:, cb].astype(f32) + dot(mixed_ref[...], w_s[3, :, cb])
    for rb in row_blocks(rows):
        x = h1_ref[rb, :]
        n2_ref[rb, :] = (x * row_scale(x) * gain2_ref[...]).astype(bf16)


def cross_forward(len_ref, core_ref, n2_ref, h1_ref, gain3_ref, enc_ref, um_ref, uo_ref,
                  ck_ref, cv_ref, cq_ref, lse_ref, crossed_ref, h2_ref, n3_ref,
                  q_s, m_s, w_s, sem):
    s = pl.program_id(0)
    rows = n2_ref.shape[0]
    count = pl.num_programs(0)

    @pl.when(s == 0)
    def _():
        copies = weight_copies(core_ref, um_ref, uo_ref, w_s, sem)
        for copy in copies:
            copy.start()
        for copy in copies:
            copy.wait()
        for cb in col_blocks():
            put_pairs(q_s, cb, rounded(dot(n2_ref[...], w_s[0, :, cb])))
        clear_tail(q_s, rows)

    for cb in col_blocks():
        ck_ref[:, cb] = dot(enc_ref[...], w_s[1, :, cb]).astype(bf16)
        cv_ref[:, cb] = dot(enc_ref[...], w_s[2, :, cb]).astype(bf16)
    start = start_of(len_ref, s)
    even_v = lane_index(ENC_LEN) < HEAD

    def attend(size):
        window = pl.ds(start, size)
        even = lane_index(size) < HEAD
        clear_rows(cq_ref, 0, size)
        clear_rows(lse_ref, 0, size)

        def pair(hp, carry):
            cols = pl.ds(pl.multiple_of(hp * 128, 128), 128)
            q = q_s[hp, window, :].astype(bf16)
            cq_ref[0, 0:size, cols] = q
            k = ck_ref[:, cols]
            v = cv_ref[:, cols]
            res, tops = [], []
            for e in range(2):
                mine = even if e == 0 else ~even
                mine_v = even_v if e == 0 else ~even_v
                score = dot_nt(jnp.where(mine, q, 0), k)
                top = jnp.max(score, axis=-1, keepdims=True)
                p = jnp.exp(score - top).astype(bf16)
                res.append(dot(p, jnp.where(mine_v, v, 1)))
                tops.append(top)
            num = jnp.where(even, res[0], res[1])
            den = jnp.where(even, pltpu.roll(res[0], HEAD, 1), pltpu.roll(res[1], HEAD, 1))
            lse_ref[0, 0:size, cols] = jnp.where(even, tops[0], tops[1]) + jnp.log(den)
            m_s[hp, window, :] = num / den
            return carry

        lax.fori_loop(0, PAIRS, pair, 0, unroll=2)

    by_length(len_ref[s], (64, 128, 192, 256), attend)

    @pl.when(s == count - 1)
    def _():
        join_pairs(crossed_ref, m_s, rows)
        for cb in col_blocks():
            h2_ref[:, cb] = h1_ref[:, cb] + dot(crossed_ref[...], w_s[3, :, cb])
        for rb in row_blocks(rows):
            x = h2_ref[rb, :]
            n3_ref[rb, :] = (x * row_scale(x) * gain3_ref[...]).astype(bf16)


def gelu_parts(x):
    decay = jnp.exp(-0.5 * (x * x))
    t = 1.0 / (1.0 + jnp.abs(x) * (0.3275911 / math.sqrt(2.0)))
    poly = t * (0.5 * 0.254829592 + t * (-0.5 * 0.284496736 + t * (
        0.5 * 1.421413741 + t * (-0.5 * 1.453152027 + t * (0.5 * 1.061405429)))))
    tail = poly * decay
    below = jnp.where(x >= 0, 1.0 - tail, tail)
    return x * below, below + x * decay * (1.0 / math.sqrt(2.0 * math.pi))


def feed_forward(len_ref, group_ref, step_ref, weight_ref, tags_ref, mask_ref, og_ref, n3_ref,
                 h2_ref, gain3_ref, x_ref, r_ref,
                 out_ref, gu_ref, g2_ref, gg_ref,
                 scaled_s, out_s, dn_s, act_s, de_s, gu_s, sem):
    g = pl.program_id(0)
    count = 4

    def copies(g):
        return (pltpu.make_async_copy(gu_s.at[g], gu_ref.at[g], sem.at[g]),
                pltpu.make_async_copy(
                    gu_s.at[pl.ds(4, 4), g], gu_ref.at[pl.ds(4, 4), g], sem.at[count + g]))

    rows = n3_ref.shape[0]

    def token_weight(rb):
        index = lax.broadcasted_iota(jnp.int32, (128, 1), 0) + rb.start
        scale = jnp.zeros((128, 1), f32)
        tagged = jnp.zeros((128, 1), jnp.int32)
        start = 0
        for s in range(4):
            group = group_ref[s]
            factor = jnp.float32(0.0)
            for k in range(GROUPS):
                value = weight_ref[k].astype(f32) * 0.25 * (
                    1.0 - step_ref[k].astype(f32) * (1.0 / (2.0 * HORIZON)))
                factor = jnp.where(group == k, value, factor)
            inside = index >= start
            scale = jnp.where(inside, factor, scale)
            tagged = jnp.where(inside, jnp.where(group == 1, 1, 0), tagged)
            start = start + len_ref[s]
        counted = jnp.where(tagged == 1, tags_ref[rb, :], mask_ref[rb, :]).astype(f32)
        return scale * (0.25 + 0.75 * counted)

    @pl.when(g == 0)
    def _():
        for rb in row_blocks(rows):
            scaled = og_ref[rb, :].astype(f32) * token_weight(rb)
            g2_ref[rb, :] = scaled
            scaled_s[rb, :] = scaled.astype(bf16)
        out_s[...] = h2_ref[...]
        dn_s[...] = jnp.zeros(dn_s.shape, f32)

    for cb in col_blocks():
        expanded = dot(n3_ref[...], x_ref[:, 0, :, cb].reshape(D, COLS))
        act, slope = gelu_parts(expanded)
        act_s[:, cb] = act.astype(bf16)
        back = dot_nt(scaled_s[...], r_ref[0].reshape(D, D)[cb, :])
        de_s[:, cb] = (back * slope).astype(bf16)
    for cb in col_blocks():
        out_s[:, cb] += dot(act_s[...], r_ref[0, :, :, cb].reshape(D, COLS))
        gx = dot_tn(n3_ref[...], de_s[:, cb]).astype(bf16)
        gr = dot_tn(act_s[...], scaled_s[:, cb]).astype(bf16)
        gu_s[g, :, :, cb] = gx.reshape(4, D // 4, COLS)
        for part in range(4):
            gu_s[4 + part, g, :, cb] = gr[part * (D // 4):(part + 1) * (D // 4), :]
    for copy in copies(g):
        copy.start()
    full = x_ref[:, 0].reshape(D, D)
    for cb in col_blocks():
        dn_s[:, cb] += dot_nt(de_s[...], full[cb, :])

    @pl.when(g == pl.num_programs(0) - 1)
    def _():
        total = jnp.zeros((1, D), f32)
        for rb in row_blocks(rows):
            out_ref[rb, :] = out_s[rb, :].astype(bf16)
            part, pulled = norm_back(dn_s[rb, :], h2_ref[rb, :], gain3_ref[...])
            g2_ref[rb, :] += part
            total = total + jnp.sum(pulled, axis=0, keepdims=True)
        gg_ref[...] = total
        for step in range(count):
            for copy in copies(step):
                copy.wait()


def head_sums(product):
    a = lax.broadcasted_iota(jnp.int32, (128, 128), 0) < HEAD
    b = lax.broadcasted_iota(jnp.int32, (128, 128), 1) < HEAD
    ones = (a == b).astype(bf16)
    high, mid, rest = split_three(product)
    return dot(high, ones) + dot(mid, ones) + dot(rest, ones)


def augment(base, minus, lane, e):
    mine = (lane < HEAD) if e == 0 else (lane >= HEAD)
    spot = HEAD if e == 0 else 0
    high, mid, rest = split_three(-minus)
    extra = jnp.where(lane == spot, high, jnp.where(lane == spot + 1, mid, jnp.where(
        lane == spot + 2, rest, jnp.zeros_like(high))))
    return jnp.where(mine, base, extra)


def ones_beside(base, lane, e):
    mine = (lane < HEAD) if e == 0 else (lane >= HEAD)
    return jnp.where(mine, base, 1)


def other_half(value):
    return pltpu.roll(value, HEAD, 1)


def cross_backward(len_ref, g2_ref, crossed_ref, cq_ref, lse_ref, ck_ref, cv_ref, enc_ref, n2_ref,
                   h1_ref, gain2_ref, core_ref, um_ref, uo_ref,
                   dk_ref, dv_ref, keep_ref, send_ref, g1_ref, gg_ref,
                   dm_s, dd_s, dq_s, dk_s, dv_s, b2_s, dml_s, dn_s, enc_s, n2_s, h1_s, late,
                   w_s, sem):
    s = pl.program_id(0)
    rows = g2_ref.shape[0]
    early = [pltpu.make_async_copy(src, dst, late.at[i])
             for i, (src, dst) in enumerate(((enc_ref, enc_s), (n2_ref, n2_s), (h1_ref, h1_s)))]

    def results(s):
        part = pl.ds(pl.multiple_of(s * ENC_LEN, ENC_LEN), ENC_LEN)
        return [pltpu.make_async_copy(src.at[part], dst.at[part], late.at[3 + 4 * i + s])
                for i, (src, dst) in enumerate(((dk_s, dk_ref), (dv_s, dv_ref)))]

    @pl.when(s == 0)
    def _():
        copies = weight_copies(core_ref, um_ref, uo_ref, w_s, sem)
        for copy in copies:
            copy.start()
        b2_s[...] = g2_ref[...].astype(bf16)
        for cb in col_blocks():
            put_gradient(keep_ref, send_ref, core_ref, 3, cb,
                         dot_tn(crossed_ref[...], b2_s[:, cb]))
        for copy in copies:
            copy.wait()
        for cb in col_blocks():
            put_pairs(dm_s, cb, rounded(dot_nt(b2_s[...], w_s[3, cb, :])))
        for copy in early:
            copy.start()
        clear_tail(dm_s, rows)
        clear_tail(dd_s, rows)
        for hp in range(PAIRS):
            cols = slice(hp * 128, hp * 128 + 128)
            dd_s[hp, 0:rows, :] = head_sums(dm_s[hp, 0:rows, :] * crossed_ref[:, cols].astype(f32))

    start = 0
    length = len_ref[0]
    for t in range(3):
        start = start + jnp.where(s > t, len_ref[t], 0)
        length = jnp.where(s == t + 1, len_ref[t + 1], length)
    lane = lane_index(MAX_LEN)
    lane_k = lane_index(ENC_LEN)
    valid = lax.broadcasted_iota(jnp.int32, (MAX_LEN, 128), 0) < length
    window = pl.ds(start, MAX_LEN)
    part = pl.ds(pl.multiple_of(s * ENC_LEN, ENC_LEN), ENC_LEN)

    def pair(hp, carry):
        cols = pl.ds(pl.multiple_of(hp * 128, 128), 128)
        q = cq_ref[0, :, cols]
        k = ck_ref[:, cols]
        v = cv_ref[:, cols]
        lse = other_half(lse_ref[0, :, cols])
        dm = jnp.where(valid, dm_s[hp, window, :], 0.0).astype(bf16)
        dd = other_half(jnp.where(valid, dd_s[hp, window, :], 0.0))
        dq = dk = dv = None
        for e in range(2):
            score = dot_nt(ones_beside(k, lane_k, e), augment(q, lse, lane, e))
            p = jnp.exp(score)
            back = dot_nt(ones_beside(v, lane_k, e), augment(dm, dd, lane, e))
            ds = (p * back).astype(bf16)
            mine = (lane < HEAD) if e == 0 else (lane >= HEAD)
            mine_k = (lane_k < HEAD) if e == 0 else (lane_k >= HEAD)
            dv_e = dot(p.astype(bf16), jnp.where(mine, dm, 0))
            dk_e = dot(ds, jnp.where(mine, q, 0))
            dq_e = dot_tn(ds, jnp.where(mine_k, k, 0))
            dq, dk, dv = (dq_e, dk_e, dv_e) if e == 0 else (dq + dq_e, dk + dk_e, dv + dv_e)
        dq_s[hp, window, :] = dq
        dk_s[part, cols] = dk.astype(bf16)
        dv_s[part, cols] = dv.astype(bf16)
        return carry

    lax.fori_loop(0, PAIRS, pair, 0, unroll=2)
    for copy in results(s):
        copy.start()

    @pl.when(s == pl.num_programs(0) - 1)
    def _():
        join_pairs(dml_s, dq_s, rows)
        for copy in early:
            copy.wait()
        for cb in col_blocks():
            put_gradient(keep_ref, send_ref, core_ref, 0, cb, dot_tn(n2_s[...], dml_s[:, cb]))
            put_gradient(keep_ref, send_ref, core_ref, 1, cb, dot_tn(enc_s[...], dk_s[:, cb]))
            put_gradient(keep_ref, send_ref, core_ref, 2, cb, dot_tn(enc_s[...], dv_s[:, cb]))
            dn_s[:, cb] = dot_nt(dml_s[...], w_s[0, cb, :])
        total = jnp.zeros((1, D), f32)
        for rb in row_blocks(rows):
            part, pulled = norm_back(dn_s[rb, :], h1_s[rb, :], gain2_ref[...])
            g1_ref[rb, :] = g2_ref[rb, :] + part
            total = total + jnp.sum(pulled, axis=0, keepdims=True)
        gg_ref[...] = total
        for step in range(4):
            for copy in results(step):
                copy.wait()


def encoded_back(core_ref, dk_ref, dv_ref, um_ref, uo_ref, ge_ref, w_s, sem):
    @pl.when(pl.program_id(0) == 0)
    def _():
        copies = weight_copies(core_ref, um_ref, uo_ref, w_s, sem)
        for copy in copies:
            copy.start()
        for copy in copies:
            copy.wait()

    for cb in col_blocks():
        ge_ref[:, cb] = dot_nt(dk_ref[...], w_s[1, cb, :]) + dot_nt(dv_ref[...], w_s[2, cb, :])


def diagonal_sums(ref):
    total = ref[0:8, :]
    for r in range(8, MAX_LEN, 8):
        total = total + pltpu.roll(ref[r:r + 8, :], MAX_LEN - r, 1)
    row = lax.broadcasted_iota(jnp.int32, (8, MAX_LEN), 0)
    for bit in (1, 2, 4):
        total = jnp.where((row & bit) != 0, pltpu.roll(total, MAX_LEN - bit, 1), total)
    return jnp.sum(total, axis=0, keepdims=True)


def self_backward(len_ref, g1_ref, mixed_ref, q_ref, k_ref, v_ref, lse_ref, n1_ref,
                  lag_ref, core_ref, um_ref, uo_ref,
                  dq_ref, dk_ref, dv_ref, keep_ref, send_ref, gl_ref,
                  dm_s, dd_s, dq_s, dk_s, dv_s, b1_s, bias_s, acc_s, qh_s, kh_s, vh_s, lh_s, late,
                  w_s, sem):
    early = [pltpu.make_async_copy(src, dst, late.at[i]) for i, (src, dst) in enumerate(
        ((q_ref, qh_s), (k_ref, kh_s), (v_ref, vh_s), (lse_ref, lh_s)))]
    copies = weight_copies(core_ref, um_ref, uo_ref, w_s, sem)
    for copy in copies:
        copy.start()
    for copy in early:
        copy.start()
    rows = g1_ref.shape[0]
    count = q_ref.shape[0]
    b1_s[...] = g1_ref[...].astype(bf16)
    for cb in col_blocks():
        put_gradient(keep_ref, send_ref, core_ref, 3, cb, dot_tn(mixed_ref[...], b1_s[:, cb]))
    for copy in copies:
        copy.wait()
    for cb in col_blocks():
        put_pairs(dm_s, cb, rounded(dot_nt(b1_s[...], w_s[3, cb, :])))
    clear_tail(dm_s, rows)
    clear_tail(dd_s, rows)
    for hp in range(PAIRS):
        cols = slice(hp * 128, hp * 128 + 128)
        dd_s[hp, 0:rows, :] = head_sums(dm_s[hp, 0:rows, :] * mixed_ref[:, cols].astype(f32))
    starts = starts_of(len_ref)
    row = lax.broadcasted_iota(jnp.int32, (MAX_LEN, MAX_LEN), 0)
    col = lax.broadcasted_iota(jnp.int32, (MAX_LEN, MAX_LEN), 1)
    lane = lane_index(MAX_LEN)
    index = lax.broadcasted_iota(jnp.int32, (MAX_LEN, 128), 0)

    for copy in early:
        copy.wait()

    def pair(hp, carry):
        cols = pl.ds(pl.multiple_of(hp * 128, 128), 128)
        for e in range(2):
            w = jnp.broadcast_to(lag_ref[pl.ds(2 * hp + e, 1), :], (MAX_LEN, MAX_LEN))
            table = pltpu.roll(w, 0, 1, stride=1, stride_axis=0)
            bias_s[e] = jnp.where(col >= row, table, masked_score)
        for s in range(count):
            valid = index < len_ref[s]
            window = pl.ds(starts[s], MAX_LEN)
            q = qh_s[s, :, cols]
            k = kh_s[s, :, cols]
            v = vh_s[s, :, cols]
            lse = other_half(lh_s[s, :, cols])
            dm = jnp.where(valid, dm_s[hp, window, :], 0.0).astype(bf16)
            dd = other_half(jnp.where(valid, dd_s[hp, window, :], 0.0))
            dq = dk = dv = None
            for e in range(2):
                score = dot_nt(ones_beside(k, lane, e), augment(q, lse, lane, e)) + bias_s[e]
                p = jnp.exp(score)
                back = dot_nt(ones_beside(v, lane, e), augment(dm, dd, lane, e))
                grad = p * back
                if s == 0:
                    acc_s[e] = grad
                else:
                    acc_s[e] += grad
                ds = grad.astype(bf16)
                mine = (lane < HEAD) if e == 0 else (lane >= HEAD)
                dv_e = dot(p.astype(bf16), jnp.where(mine, dm, 0))
                dk_e = dot(ds, jnp.where(mine, q, 0))
                dq_e = dot_tn(ds, jnp.where(mine, k, 0))
                dq, dk, dv = (dq_e, dk_e, dv_e) if e == 0 else (dq + dq_e, dk + dk_e, dv + dv_e)
            dq_s[hp, window, :] = dq
            dk_s[hp, window, :] = dk
            dv_s[hp, window, :] = dv
        for e in range(2):
            gl_ref[pl.ds(2 * hp + e, 1), :] = diagonal_sums(acc_s.at[e])
        return carry

    lax.fori_loop(0, PAIRS, pair, 0, unroll=2)
    for w, (src, out) in enumerate(((dq_s, dq_ref), (dk_s, dk_ref), (dv_s, dv_ref))):
        join_pairs(out, src, rows)
        for cb in col_blocks():
            put_gradient(keep_ref, send_ref, core_ref, w, cb, dot_tn(n1_ref[...], out[:, cb]))


def hidden_back(core_ref, g1_ref, hid_ref, gain1_ref, dq_ref, dk_ref, dv_ref, gg2_ref, gg3_ref,
                gl_ref, um_ref, uo_ref, gh_ref, small_ref, dn_s, small_s, w_s, sem):
    copies = weight_copies(core_ref, um_ref, uo_ref, w_s, sem)
    for copy in copies:
        copy.start()
    for copy in copies:
        copy.wait()
    rows = g1_ref.shape[0]
    for cb in col_blocks():
        dn_s[:, cb] = (dot_nt(dq_ref[...], w_s[0, cb, :]) + dot_nt(dk_ref[...], w_s[1, cb, :])
                       + dot_nt(dv_ref[...], w_s[2, cb, :]))
    total = jnp.zeros((1, D), f32)
    for rb in row_blocks(rows):
        part, pulled = norm_back(dn_s[rb, :], hid_ref[rb, :].astype(f32), gain1_ref[...])
        gh_ref[rb, :] = g1_ref[rb, :] + part
        total = total + jnp.sum(pulled, axis=0, keepdims=True)
    small_s[...] = jnp.zeros(small_s.shape, f32)
    small_s[0:1, :] = total
    small_s[1:2, :] = gg2_ref[...]
    small_s[2:3, :] = gg3_ref[...]
    small_s[3:3 + HEADS, 0:MAX_LEN] = gl_ref[...]
    small_ref[...] = small_s[...].astype(bf16)


def bucket_table():
    lags = np.arange(MAX_LEN)
    exact = BUCKETS // 2
    bucket = np.minimum(lags, exact)
    for step in range(1, exact):
        edge = math.ceil(exact * (MAX_DIST / exact) ** (step / exact))
        bucket = bucket + (lags >= edge)
    return (bucket[None, :] == np.arange(BUCKETS)[:, None]).astype(np.float32)


def shape(dims, kind):
    return jax.ShapeDtypeStruct(dims, kind)


def call(kernel, name, micros, grant, outs, ins, scratch, **extra):
    return pl.pallas_call(
        kernel,
        out_shape=list(outs),
        name=name,
        scratch_shapes=scratch,
        cost_estimate=pl.CostEstimate(
            flops=int(micros * 1e9), bytes_accessed=1 << 20, transcendentals=0),
        compiler_params=pltpu.CompilerParams(vmem_limit_bytes=grant << 20),
        **extra,
    )(*ins)


def whole(array_shape):
    zeros = (0,) * len(array_shape)
    return pl.BlockSpec(array_shape, lambda s: zeros)


class Routes:
    def __init__(self):
        self.parts = lax.axis_size("dp")
        self.shards = lax.axis_size("fsdp")
        self.dp = lax.axis_index("dp")
        self.z = lax.axis_index("fsdp")
        self.core = self.dp & 1
        bits = list(range(1, self.parts.bit_length() - 1))
        self.steps = list(zip(bits, bits[::-1]))

    def permute(self, value, partner):
        pairs = []
        for dp in range(self.parts):
            for z in range(self.shards):
                to_dp, to_z = partner(dp, z)
                pairs.append((dp * self.shards + z, to_dp * self.shards + to_z))
        return lax.ppermute(value, ("dp", "fsdp"), pairs)

    def swap_core(self, value):
        return self.permute(value, lambda dp, z: (dp ^ 1, z))

    def swap(self, value, step):
        return self.permute(value, lambda dp, z: (dp ^ (1 << step[dp & 1]), z))

    def shift(self, value, by):
        return self.permute(value, lambda dp, z: (dp, (z + by) % self.shards))

    def bit(self, step):
        return jnp.where(self.core == 0, (self.dp >> step[0]) & 1, (self.dp >> step[1]) & 1)

    def piece_index(self):
        index = self.core
        for step in self.steps:
            index = 2 * index + self.bit(step)
        return index

    def shift_all(self, own):
        return [own] + [self.shift(own, by) for by in range(1, self.shards)]

    def stack_shards(self, got):
        return jnp.stack([
            lax.select_n((self.z - z) % self.shards, *got) for z in range(self.shards)])

    def collect(self, piece):
        for step in reversed(self.steps):
            piece = self.join(piece, self.swap(piece, step), step)
        return piece, self.swap_core(piece)

    def join(self, piece, got, step):
        return jnp.where(self.bit(step) == 0, jnp.concatenate([piece, got], 1),
                         jnp.concatenate([got, piece], 1))

    def halve(self, total, step):
        size = total.shape[1] // 2
        bit = self.bit(step)
        send = lax.dynamic_slice_in_dim(total, (1 - bit) * size, size, 1)
        keep = lax.dynamic_slice_in_dim(total, bit * size, size, 1)
        return keep, self.swap(send, step)

    def send_shards(self, total):
        parts = [lax.dynamic_index_in_dim(total, self.z, 0, keepdims=False)]
        for by in range(1, self.shards):
            chunk = lax.dynamic_index_in_dim(total, (self.z + by) % self.shards, 0, keepdims=False)
            parts.append(self.shift(chunk, by))
        return parts


def add(left, right):
    return (left.astype(f32) + right.astype(f32)).astype(bf16)


HALVES = (4, 2, D // 4, D)
WEIGHTS = [pltpu.VMEM((4, D, D), bf16), pltpu.SemaphoreType.DMA((8,))]
SQUARE = pltpu.VMEM((2, MAX_LEN, MAX_LEN), f32)
LINE = whole((1, D))
ENC_BLOCK = pl.BlockSpec((ENC_LEN, D), lambda s: (s, 0))
SEQ_BLOCK = pl.BlockSpec((1, MAX_LEN, D), lambda s: (s, 0, 0))


def scratch_of(rows):
    wide = pltpu.VMEM((PAIRS, rows + MAX_LEN, 128), f32)
    return wide, pltpu.VMEM((rows, D), bf16), pltpu.VMEM((rows, D), f32)


def run_self_forward(lengths, core, hidden, gain1, gain2, turned, u_self):
    rows = hidden.shape[0]
    heads = (lengths.shape[0], MAX_LEN, D)
    wide, low, flat = scratch_of(rows)
    return call(
        self_forward, "self_forward", 21, 40,
        (shape((rows, D), bf16), shape(heads, bf16), shape(heads, bf16), shape(heads, bf16),
         shape(heads, f32), shape((rows, D), bf16), shape((rows, D), f32), shape((rows, D), bf16)),
        (lengths, core, hidden, gain1, gain2, turned, *u_self),
        [wide, wide, wide, wide, SQUARE] + WEIGHTS,
        in_specs=[SMEM] * 2 + [VMEM] * 4 + [ANY] * 2, out_specs=[VMEM] * 8)


def run_cross_forward(lengths, core, n2, h1, gain3, encoded, u_cross):
    rows = n2.shape[0]
    count = lengths.shape[0]
    heads = (count, MAX_LEN, D)
    wide, low, flat = scratch_of(rows)
    full = whole((rows, D))
    return call(
        cross_forward, "cross_forward", 34, 60,
        (shape(encoded.shape, bf16), shape(encoded.shape, bf16), shape(heads, bf16),
         shape(heads, f32), shape((rows, D), bf16), shape((rows, D), f32), shape((rows, D), bf16)),
        (lengths, core, n2, h1, gain3, encoded, *u_cross),
        [wide, wide] + WEIGHTS,
        grid=(count,),
        in_specs=[SMEM] * 2 + [full, full, LINE, ENC_BLOCK, ANY, ANY],
        out_specs=[ENC_BLOCK, ENC_BLOCK, SEQ_BLOCK, SEQ_BLOCK, full, full, full])


def run_feed_forward(lengths, group_ids, group_steps, group_weights, tags, mask, out_grad, n3, h2,
                     gain3, u_ffn):
    rows = n3.shape[0]
    quarter = D // 4
    wide, low, flat = scratch_of(rows)
    full = whole((rows, D))
    column = whole((rows, 1))
    x_block = pl.BlockSpec((4, 1, quarter, D), lambda g: (0, g, 0, 0))
    r_block = pl.BlockSpec((1, 4, quarter, D), lambda g: (g, 1, 0, 0))
    return call(
        feed_forward, "feed_forward", 32, 60,
        (shape((rows, D), bf16), shape((8, 4, quarter, D), bf16),
         shape((rows, D), f32), shape((1, D), f32)),
        (lengths, group_ids, group_steps, group_weights, tags, mask, out_grad, n3, h2, gain3,
         u_ffn, u_ffn),
        [low, flat, flat, low, low, pltpu.VMEM((8, 4, quarter, D), bf16),
         pltpu.SemaphoreType.DMA((8,))],
        grid=(4,),
        in_specs=[SMEM] * 4 + [column, column, full, full, full, LINE, x_block, r_block],
        out_specs=[full, ANY, full, LINE])


def run_cross_backward(lengths, g2, crossed, cq, lse, ck, cv, encoded, n2, h1, gain2, core,
                       u_cross):
    rows = g2.shape[0]
    count = lengths.shape[0]
    wide, low, flat = scratch_of(rows)
    full = whole((rows, D))
    return call(
        cross_backward, "cross_backward", 42, 60,
        (shape(encoded.shape, bf16), shape(encoded.shape, bf16), shape(HALVES, bf16),
         shape(HALVES, bf16), shape((rows, D), f32), shape((1, D), f32)),
        (lengths, g2, crossed, cq, lse, ck, cv, encoded, n2, h1, gain2, core, *u_cross),
        [wide, wide, wide, pltpu.VMEM(encoded.shape, bf16), pltpu.VMEM(encoded.shape, bf16),
         low, low, flat, pltpu.VMEM(encoded.shape, bf16), low, flat,
         pltpu.SemaphoreType.DMA((11,))] + WEIGHTS,
        grid=(count,),
        in_specs=[SMEM, full, full, SEQ_BLOCK, SEQ_BLOCK, ENC_BLOCK, ENC_BLOCK, ANY, ANY,
                  ANY, LINE, SMEM, ANY, ANY],
        out_specs=[ANY, ANY, whole(HALVES), whole(HALVES), full, LINE])


def run_self_backward(lengths, g1, mixed, q, k, v, lse, n1, by_lag, core, u_self):
    rows = g1.shape[0]
    wide, low, flat = scratch_of(rows)
    return call(
        self_backward, "self_backward", 28, 60,
        (shape((rows, D), bf16), shape((rows, D), bf16), shape((rows, D), bf16),
         shape(HALVES, bf16), shape(HALVES, bf16), shape((HEADS, MAX_LEN), f32)),
        (lengths, g1, mixed, q, k, v, lse, n1, by_lag, core, *u_self),
        [wide, wide, wide, wide, wide, low, SQUARE, SQUARE]
        + [pltpu.VMEM(value.shape, value.dtype) for value in (q, k, v, lse)]
        + [pltpu.SemaphoreType.DMA((4,))] + WEIGHTS,
        in_specs=[SMEM, VMEM, VMEM, ANY, ANY, ANY, ANY, VMEM, VMEM, SMEM, ANY, ANY], out_specs=[VMEM] * 6)


def run_hidden_back(core, g1, hidden, gain1, dq, dk, dv, gg2, gg3, grad_lag, u_self):
    rows = g1.shape[0]
    wide, low, flat = scratch_of(rows)
    return call(
        hidden_back, "hidden_back", 8, 24,
        (shape((rows, D), f32), shape((SMALL, D), bf16)),
        (core, g1, hidden, gain1, dq, dk, dv, gg2, gg3, grad_lag, *u_self),
        [flat, pltpu.VMEM((SMALL, D), f32)] + WEIGHTS,
        in_specs=[SMEM] + [VMEM] * 9 + [ANY] * 2, out_specs=[VMEM] * 2)


def run_encoded_back(core, dck, dcv, u_cross):
    return call(
        encoded_back, "encoded_back", 10, 20,
        (shape(dck.shape, f32),),
        (core, dck, dcv, *u_cross),
        WEIGHTS,
        grid=(dck.shape[0] // ENC_LEN,),
        in_specs=[SMEM, ENC_BLOCK, ENC_BLOCK, ANY, ANY], out_specs=[ENC_BLOCK])


def add_all(parts):
    total = parts[0].astype(f32)
    for part in parts[1:]:
        total = total + part.astype(f32)
    return total.astype(bf16)


def tie(value, *after):
    return lax.optimization_barrier((value, *after))[0]


def tie_all(values, *after):
    return lax.optimization_barrier((*values, *after))[:len(values)]


def per_device(
    hidden, encoded, out_grad, lengths, group_ids, id_tags, loss_mask, group_steps, group_weights,
    gain_self, gain_cross, gain_ffn, rel_bias,
    query_weight, key_weight, value_weight, output_weight,
    cross_query, cross_key, cross_value, cross_output, expand_weight, reduce_weight,
):
    rows = hidden.shape[0]
    count = lengths.shape[0]
    quarter = D // 4
    routes = Routes()
    core = routes.core.reshape(1)
    size = D // routes.parts

    def piece_of(parts, index, extent):
        return lax.dynamic_slice_in_dim(jnp.concatenate(parts, 0), index * extent, extent, 0)

    small = jnp.concatenate([gain_self, gain_cross, gain_ffn, rel_bias.reshape(-1)])
    small_row = jnp.pad(small[None], ((0, 15), (0, D - small.shape[0])))
    own = piece_of([query_weight, key_weight, value_weight, output_weight],
                   routes.piece_index(), size)
    first = lax.all_gather(jnp.concatenate([own, small_row], 0)[None], "fsdp", axis=0, tiled=True)
    small = first[:, size, :small.shape[0]].astype(f32)
    cross_own = piece_of([cross_query, cross_key, cross_value, cross_output],
                         routes.piece_index(), size)
    self_piece = first[:, :size]
    cross_got = routes.shift_all(tie(cross_own, first))
    for step in routes.steps[:0:-1]:
        self_piece = routes.join(self_piece, routes.swap(self_piece, step), step)
    start_ffn = self_piece
    cross_piece = routes.stack_shards(tie_all(cross_got, self_piece))
    for step in routes.steps[:0:-1]:
        cross_piece = routes.join(cross_piece, routes.swap(cross_piece, step), step)
    step = routes.steps[0]
    self_piece = routes.join(self_piece, tie(routes.swap(self_piece, step), cross_piece), step)
    self_other = routes.swap_core(self_piece)
    cross_last = routes.swap(cross_piece, routes.steps[0])
    u_self = [half.reshape(HALVES) for half in (self_piece, self_other)]
    ratio = routes.parts // 8
    slot, offset = routes.dp // ratio, (routes.dp % ratio) * (quarter // ratio)
    own = jnp.where(
        slot < 4,
        lax.dynamic_slice(expand_weight, (offset, jnp.minimum(slot, 3) * D), (quarter // ratio, D)),
        lax.dynamic_slice_in_dim(
            reduce_weight, jnp.maximum(slot - 4, 0) * quarter + offset, quarter // ratio, 0))
    u_ffn = lax.all_gather(tie(own, start_ffn), ("fsdp", "dp"), axis=0, tiled=True)
    u_ffn = u_ffn.reshape(4, 8, quarter, D)

    gain1 = small[:, 0:quarter].reshape(1, D)
    gain2 = small[:, quarter:2 * quarter].reshape(1, D)
    gain3 = small[:, 2 * quarter:3 * quarter].reshape(1, D)
    rel = small[:, 3 * quarter:].reshape(HEADS, BUCKETS)
    table = bucket_table()
    by_lag = jnp.dot(rel, jnp.asarray(table), precision=lax.Precision.HIGHEST)
    turned = jnp.dot(
        rel, jnp.asarray(table[:, (-np.arange(MAX_LEN)) % MAX_LEN]), precision=lax.Precision.HIGHEST)

    n1, q, k, v, lse, mixed, h1, n2 = run_self_forward(
        lengths, core, hidden, gain1, gain2, turned, u_self)
    cross_piece = routes.join(cross_piece, tie(cross_last, n2), routes.steps[0])
    u_cross = [half.reshape(HALVES) for half in (cross_piece, routes.swap_core(cross_piece))]
    ck, cv, cq, cross_lse, crossed, h2, n3 = run_cross_forward(
        lengths, core, n2, h1, gain3, encoded, u_cross)
    layer_output, grad_ffn, g2, gg3 = run_feed_forward(
        lengths, group_ids, group_steps, group_weights, id_tags[:, None], loss_mask[:, None],
        out_grad, n3, h2, gain3, u_ffn)
    if routes.parts > 8:
        grad_ffn = grad_ffn.reshape(8, 4, routes.parts // 8, -1, D).swapaxes(1, 2)
    ffn_piece = lax.psum_scatter(
        grad_ffn.reshape(-1, D), "dp", scatter_dimension=0, tiled=True)

    dck, dcv, keep, send, g1, gg2 = run_cross_backward(
        lengths, g2, crossed, cq, cross_lse, ck, cv, encoded, n2, h1, gain2, core, u_cross)
    first_step, later_steps = routes.steps[0], routes.steps[1:]
    half = (4, D // 2, D)
    got = routes.swap_core(send.reshape(half))
    (grad_encoded,) = run_encoded_back(core, tie(dck, g1), dcv, u_cross)
    cross_total = add(keep.reshape(half), tie(got, grad_encoded))
    cross_keep, cross_got = routes.halve(cross_total, first_step)

    ffn_half = ffn_piece
    ffn_piece = lax.psum_scatter(ffn_piece, "fsdp", scatter_dimension=0, tiled=True)
    ffn = lax.all_gather(ffn_piece, "dp", axis=0, tiled=True).astype(f32)

    dq, dk, dv, keep, send, grad_lag = run_self_backward(
        lengths, tie(g1, cross_total), mixed, q, k, v, lse, n1, by_lag, core, u_self)
    cross_total = add(cross_keep, tie(cross_got, dq))
    got = routes.swap_core(tie(send, cross_total, ffn_half).reshape(half))
    for step in later_steps:
        cross_keep, cross_got = routes.halve(cross_total, step)
        if step is not later_steps[-1]:
            cross_total = add(cross_keep, cross_got)
    self_total = add(keep.reshape(half), tie(got, ffn_half))
    self_keep, self_got = routes.halve(self_total, first_step)

    grad_hidden, small = run_hidden_back(
        core, g1, hidden, gain1, tie(dq, self_total), dk, dv, gg2, gg3, grad_lag, u_self)
    cross_total = add(cross_keep, tie(cross_got, grad_hidden))
    self_total = add(self_keep, tie(self_got, grad_hidden, cross_total, ffn_piece))
    cross_parts = routes.send_shards(tie(cross_total, self_total))
    for step in later_steps:
        self_keep, self_got = routes.halve(self_total, step)
        if step is not later_steps[-1]:
            self_total = add(self_keep, self_got)
    self_total = add(self_keep, self_got)
    self_parts = routes.send_shards(jnp.concatenate(
        [self_total, jnp.broadcast_to(small[None], (4, SMALL, D))], axis=1))
    piece = jnp.concatenate(
        [add_all(self_parts), add_all(tie_all(cross_parts, self_total))], axis=0)

    mine, other = routes.collect(piece[None])
    mine = mine.reshape(routes.parts // 2, 2 * size + SMALL, D)
    other = other.reshape(routes.parts // 2, 2 * size + SMALL, D)
    small = jnp.sum(mine[:, size:size + SMALL].astype(f32), 0) + jnp.sum(
        other[:, size:size + SMALL].astype(f32), 0)
    gains = lax.dynamic_slice_in_dim(small[0:3], routes.z * quarter, quarter, 1)
    lag = lax.dynamic_slice_in_dim(small[3:3 + HEADS, :MAX_LEN], routes.z * (HEADS // 4), HEADS // 4, 0)
    grad_rel = lax.dot_general(
        lag, jnp.asarray(table), (((1,), (1,)), ((), ())), precision=lax.Precision.HIGHEST)

    def weight_grads(first):
        own = [value[:, first:first + size].reshape(2, quarter, D) for value in (mine, other)]
        lows = jnp.where(routes.core == 0, own[0], own[1]).astype(f32)
        highs = jnp.where(routes.core == 0, own[1], own[0]).astype(f32)
        return lows[0], lows[1], highs[0], highs[1]

    return (
        layer_output,
        grad_hidden,
        grad_encoded,
        gains[0],
        gains[1],
        gains[2],
        grad_rel,
        *weight_grads(0),
        *weight_grads(size + SMALL),
        jnp.concatenate([ffn[g * quarter:(g + 1) * quarter] for g in range(4)], axis=1),
        ffn[D:],
    )


def solution(mesh):
    rows = P(("dp", "fsdp"), None)
    flat = P(("dp", "fsdp"))
    shard = P("fsdp", None)
    line = P("fsdp")
    return jax.shard_map(
        per_device,
        mesh=mesh,
        in_specs=(rows, rows, rows, flat, flat, flat, flat, P(), P(), line, line, line) + (shard,) * 11,
        out_specs=(rows, rows, rows, line, line, line) + (shard,) * 11,
        check_vma=False,
    )
```

```python
from functools import partial
import math

import jax
import jax.numpy as jnp
import numpy as np
from jax import lax
from jax.experimental import pallas as pl
from jax.experimental.pallas import tpu as pltpu
from jax.sharding import PartitionSpec as P

HEADS = 12
HEAD = 64
PAIRS = 6
BUCKETS = 32
MAX_DIST = 128
ENC_LEN = 512
MAX_LEN = 256
GROUPS = 3
HORIZON = 10000
D = 768
COLS = 768
SMALL = 16

f32 = jnp.float32
bf16 = jnp.bfloat16
epsilon = 1e-06
masked_score = -1000000000.0

VMEM = pl.BlockSpec(memory_space=pltpu.VMEM)
SMEM = pl.BlockSpec(memory_space=pltpu.SMEM)
ANY = pl.BlockSpec(memory_space=pl.ANY)


def dot(left, right):
    return jnp.dot(left, right, preferred_element_type=f32)


def dot_nt(left, right):
    return lax.dot_general(left, right, (((1,), (1,)), ((), ())), preferred_element_type=f32)


def dot_tn(left, right):
    return lax.dot_general(left, right, (((0,), (0,)), ((), ())), preferred_element_type=f32)


def rounded(value):
    return value.astype(bf16).astype(f32)


def row_scale(rows):
    return lax.rsqrt(jnp.mean(rows * rows, axis=-1, keepdims=True) + epsilon)


def row_blocks(rows):
    return [slice(r, r + 128) for r in range(0, rows, 128)]


def col_blocks(width=D):
    return [slice(c, c + COLS) for c in range(0, width, COLS)]


def starts_of(len_ref):
    starts = [0]
    for s in range(3):
        starts.append(starts[-1] + len_ref[s])
    return starts


def norm_back(grad, rows, gain):
    r = row_scale(rows)
    pulled = gain * grad
    inner = jnp.mean(pulled * rows, axis=-1, keepdims=True)
    return r * pulled - rows * (r * r * r * inner), grad * rows * r


def split_three(value):
    high = value.astype(bf16)
    rest = value - high.astype(f32)
    mid = rest.astype(bf16)
    return high, mid, (rest - mid.astype(f32)).astype(bf16)


def weight_copies(core_ref, mine_ref, other_ref, w_s, sem):
    core = core_ref[0]
    quarter = D // 4
    copies = []
    for h, ref in enumerate((mine_ref, other_ref)):
        first = 2 * core if h == 0 else 2 * (1 - core)
        for z in range(4):
            copies.append(pltpu.make_async_copy(
                ref.at[z], w_s.at[pl.ds(first, 2), pl.ds(z * quarter, quarter), :],
                sem.at[4 * h + z]))
    return copies


def put_gradient(keep_ref, send_ref, core_ref, index, cb, value):
    value = value.astype(bf16).reshape(4, D // 4, COLS)
    stays = core_ref[0] == index // 2

    @pl.when(stays)
    def _():
        keep_ref[:, index % 2, :, cb] = value

    @pl.when(jnp.logical_not(stays))
    def _():
        send_ref[:, index % 2, :, cb] = value


def put_pairs(dst, cb, value):
    first = cb.start // 128
    for part in range(COLS // 128):
        dst[first + part, 0:value.shape[0], :] = value[:, part * 128:part * 128 + 128]


def clear_tail(dst, rows):
    dst[:, rows:, :] = jnp.zeros((PAIRS, dst.shape[1] - rows, 128), f32)


def join_pairs(dst, src, rows):
    for hp in range(PAIRS):
        dst[:, hp * 128:hp * 128 + 128] = src[hp, 0:rows, :].astype(dst.dtype)


def by_length(length, sizes, body):
    below = 0
    for size in sizes:
        fits = length > below if size == sizes[-1] else (length > below) & (length <= size)
        pl.when(fits)(lambda size=size: body(size))
        below = size


def clear_rows(ref, s, first):
    if first < MAX_LEN:
        ref[s, first:, :] = jnp.zeros((MAX_LEN - first, D), ref.dtype)


def start_of(len_ref, s):
    start = 0
    for t in range(3):
        start = start + jnp.where(s > t, len_ref[t], 0)
    return start


def lane_index(rows):
    return lax.broadcasted_iota(jnp.int32, (rows, 128), 1)


def self_forward(len_ref, core_ref, hid_ref, gain1_ref, gain2_ref, lag_ref, um_ref, uo_ref,
                 n1_ref, q_ref, k_ref, v_ref, lse_ref, mixed_ref, h1_ref, n2_ref,
                 q_s, k_s, v_s, m_s, bias_s, w_s, sem):
    copies = weight_copies(core_ref, um_ref, uo_ref, w_s, sem)
    for copy in copies:
        copy.start()
    rows = hid_ref.shape[0]
    count = q_ref.shape[0]
    for rb in row_blocks(rows):
        x = hid_ref[rb, :].astype(f32)
        n1_ref[rb, :] = (x * row_scale(x) * gain1_ref[...]).astype(bf16)
    for copy in copies:
        copy.wait()
    for w, dst in enumerate((q_s, k_s, v_s)):
        for cb in col_blocks():
            put_pairs(dst, cb, rounded(dot(n1_ref[...], w_s[w, :, cb])))
        clear_tail(dst, rows)
    starts = starts_of(len_ref)
    row = lax.broadcasted_iota(jnp.int32, (MAX_LEN, MAX_LEN), 0)
    col = lax.broadcasted_iota(jnp.int32, (MAX_LEN, MAX_LEN), 1)
    lane = lane_index(MAX_LEN)
    even = lane < HEAD

    def pair(hp, carry):
        cols = pl.ds(pl.multiple_of(hp * 128, 128), 128)
        for e in range(2):
            w = jnp.broadcast_to(lag_ref[pl.ds(2 * hp + e, 1), :], (MAX_LEN, MAX_LEN))
            table = pltpu.roll(w, 0, 1, stride=1, stride_axis=0)
            bias_s[e] = jnp.where(row >= col, table, masked_score)
        for s in range(count):
            window = pl.ds(starts[s], MAX_LEN)
            q = q_s[hp, window, :].astype(bf16)
            k = k_s[hp, window, :].astype(bf16)
            v = v_s[hp, window, :].astype(bf16)
            q_ref[s, :, cols] = q
            k_ref[s, :, cols] = k
            v_ref[s, :, cols] = v
            res, tops = [], []
            for e in range(2):
                mine = even if e == 0 else ~even
                score = dot_nt(jnp.where(mine, q, 0), k) + bias_s[e]
                top = jnp.max(score, axis=-1, keepdims=True)
                p = jnp.exp(score - top).astype(bf16)
                res.append(dot(p, jnp.where(mine, v, 1)))
                tops.append(top)
            num = jnp.where(even, res[0], res[1])
            den = jnp.where(even, pltpu.roll(res[0], HEAD, 1), pltpu.roll(res[1], HEAD, 1))
            lse_ref[s, :, cols] = jnp.where(even, tops[0], tops[1]) + jnp.log(den)
            m_s[hp, window, :] = num / den
        return carry

    lax.fori_loop(0, PAIRS, pair, 0, unroll=2)
    join_pairs(mixed_ref, m_s, rows)
    for cb in col_blocks():
        h1_ref[:, cb] = hid_ref[:, cb].astype(f32) + dot(mixed_ref[...], w_s[3, :, cb])
    for rb in row_blocks(rows):
        x = h1_ref[rb, :]
        n2_ref[rb, :] = (x * row_scale(x) * gain2_ref[...]).astype(bf16)


def cross_forward(len_ref, core_ref, n2_ref, h1_ref, gain3_ref, enc_ref, um_ref, uo_ref,
                  ck_ref, cv_ref, cq_ref, lse_ref, crossed_ref, h2_ref, n3_ref,
                  q_s, m_s, w_s, sem):
    s = pl.program_id(0)
    rows = n2_ref.shape[0]
    count = pl.num_programs(0)

    @pl.when(s == 0)
    def _():
        copies = weight_copies(core_ref, um_ref, uo_ref, w_s, sem)
        for copy in copies:
            copy.start()
        for copy in copies:
            copy.wait()
        for cb in col_blocks():
            put_pairs(q_s, cb, rounded(dot(n2_ref[...], w_s[0, :, cb])))
        clear_tail(q_s, rows)

    for cb in col_blocks():
        ck_ref[:, cb] = dot(enc_ref[...], w_s[1, :, cb]).astype(bf16)
        cv_ref[:, cb] = dot(enc_ref[...], w_s[2, :, cb]).astype(bf16)
    start = start_of(len_ref, s)
    even_v = lane_index(ENC_LEN) < HEAD

    def attend(size):
        window = pl.ds(start, size)
        even = lane_index(size) < HEAD
        clear_rows(cq_ref, 0, size)
        clear_rows(lse_ref, 0, size)

        def pair(hp, carry):
            cols = pl.ds(pl.multiple_of(hp * 128, 128), 128)
            q = q_s[hp, window, :].astype(bf16)
            cq_ref[0, 0:size, cols] = q
            k = ck_ref[:, cols]
            v = cv_ref[:, cols]
            res, tops = [], []
            for e in range(2):
                mine = even if e == 0 else ~even
                mine_v = even_v if e == 0 else ~even_v
                score = dot_nt(jnp.where(mine, q, 0), k)
                top = jnp.max(score, axis=-1, keepdims=True)
                p = jnp.exp(score - top).astype(bf16)
                res.append(dot(p, jnp.where(mine_v, v, 1)))
                tops.append(top)
            num = jnp.where(even, res[0], res[1])
            den = jnp.where(even, pltpu.roll(res[0], HEAD, 1), pltpu.roll(res[1], HEAD, 1))
            lse_ref[0, 0:size, cols] = jnp.where(even, tops[0], tops[1]) + jnp.log(den)
            m_s[hp, window, :] = num / den
            return carry

        lax.fori_loop(0, PAIRS, pair, 0, unroll=2)

    by_length(len_ref[s], (64, 128, 192, 256), attend)

    @pl.when(s == count - 1)
    def _():
        join_pairs(crossed_ref, m_s, rows)
        for cb in col_blocks():
            h2_ref[:, cb] = h1_ref[:, cb] + dot(crossed_ref[...], w_s[3, :, cb])
        for rb in row_blocks(rows):
            x = h2_ref[rb, :]
            n3_ref[rb, :] = (x * row_scale(x) * gain3_ref[...]).astype(bf16)


def gelu_parts(x):
    decay = jnp.exp(-0.5 * (x * x))
    t = 1.0 / (1.0 + jnp.abs(x) * (0.3275911 / math.sqrt(2.0)))
    poly = t * (0.5 * 0.254829592 + t * (-0.5 * 0.284496736 + t * (
        0.5 * 1.421413741 + t * (-0.5 * 1.453152027 + t * (0.5 * 1.061405429)))))
    tail = poly * decay
    below = jnp.where(x >= 0, 1.0 - tail, tail)
    return x * below, below + x * decay * (1.0 / math.sqrt(2.0 * math.pi))


def feed_forward(len_ref, group_ref, step_ref, weight_ref, tags_ref, mask_ref, og_ref, n3_ref,
                 h2_ref, gain3_ref, x_ref, r_ref,
                 out_ref, gu_ref, g2_ref, gg_ref,
                 scaled_s, out_s, dn_s, act_s, de_s, gu_s, sem):
    g = pl.program_id(0)
    count = 4

    def copies(g):
        return (pltpu.make_async_copy(gu_s.at[g], gu_ref.at[g], sem.at[g]),
                pltpu.make_async_copy(
                    gu_s.at[pl.ds(4, 4), g], gu_ref.at[pl.ds(4, 4), g], sem.at[count + g]))

    rows = n3_ref.shape[0]

    def token_weight(rb):
        index = lax.broadcasted_iota(jnp.int32, (128, 1), 0) + rb.start
        scale = jnp.zeros((128, 1), f32)
        tagged = jnp.zeros((128, 1), jnp.int32)
        start = 0
        for s in range(4):
            group = group_ref[s]
            factor = jnp.float32(0.0)
            for k in range(GROUPS):
                value = weight_ref[k].astype(f32) * 0.25 * (
                    1.0 - step_ref[k].astype(f32) * (1.0 / (2.0 * HORIZON)))
                factor = jnp.where(group == k, value, factor)
            inside = index >= start
            scale = jnp.where(inside, factor, scale)
            tagged = jnp.where(inside, jnp.where(group == 1, 1, 0), tagged)
            start = start + len_ref[s]
        counted = jnp.where(tagged == 1, tags_ref[rb, :], mask_ref[rb, :]).astype(f32)
        return scale * (0.25 + 0.75 * counted)

    @pl.when(g == 0)
    def _():
        for rb in row_blocks(rows):
            scaled = og_ref[rb, :].astype(f32) * token_weight(rb)
            g2_ref[rb, :] = scaled
            scaled_s[rb, :] = scaled.astype(bf16)
        out_s[...] = h2_ref[...]
        dn_s[...] = jnp.zeros(dn_s.shape, f32)

    for cb in col_blocks():
        expanded = dot(n3_ref[...], x_ref[:, 0, :, cb].reshape(D, COLS))
        act, slope = gelu_parts(expanded)
        act_s[:, cb] = act.astype(bf16)
        back = dot_nt(scaled_s[...], r_ref[0].reshape(D, D)[cb, :])
        de_s[:, cb] = (back * slope).astype(bf16)
    for cb in col_blocks():
        out_s[:, cb] += dot(act_s[...], r_ref[0, :, :, cb].reshape(D, COLS))
        gx = dot_tn(n3_ref[...], de_s[:, cb]).astype(bf16)
        gr = dot_tn(act_s[...], scaled_s[:, cb]).astype(bf16)
        gu_s[g, :, :, cb] = gx.reshape(4, D // 4, COLS)
        for part in range(4):
            gu_s[4 + part, g, :, cb] = gr[part * (D // 4):(part + 1) * (D // 4), :]
    for copy in copies(g):
        copy.start()
    full = x_ref[:, 0].reshape(D, D)
    for cb in col_blocks():
        dn_s[:, cb] += dot_nt(de_s[...], full[cb, :])

    @pl.when(g == pl.num_programs(0) - 1)
    def _():
        total = jnp.zeros((1, D), f32)
        for rb in row_blocks(rows):
            out_ref[rb, :] = out_s[rb, :].astype(bf16)
            part, pulled = norm_back(dn_s[rb, :], h2_ref[rb, :], gain3_ref[...])
            g2_ref[rb, :] += part
            total = total + jnp.sum(pulled, axis=0, keepdims=True)
        gg_ref[...] = total
        for step in range(count):
            for copy in copies(step):
                copy.wait()


def head_sums(product):
    a = (lax.broadcasted_iota(jnp.int32, (256, 128), 0) & 127) < HEAD
    b = lax.broadcasted_iota(jnp.int32, (256, 128), 1) < HEAD
    ones = (a == b).astype(bf16)
    high = product.astype(bf16)
    rest = (product - high.astype(f32)).astype(bf16)
    return dot(jnp.concatenate([high, rest], axis=1), ones)


def augment(base, minus, lane, e):
    mine = (lane < HEAD) if e == 0 else (lane >= HEAD)
    spot = HEAD if e == 0 else 0
    high, mid, rest = split_three(-minus)
    extra = jnp.where(lane == spot, high, jnp.where(lane == spot + 1, mid, jnp.where(
        lane == spot + 2, rest, jnp.zeros_like(high))))
    return jnp.where(mine, base, extra)


def ones_beside(base, lane, e):
    mine = (lane < HEAD) if e == 0 else (lane >= HEAD)
    return jnp.where(mine, base, 1)


def other_half(value):
    return pltpu.roll(value, HEAD, 1)


def cross_backward(len_ref, g2_ref, crossed_ref, cq_ref, lse_ref, ck_ref, cv_ref, enc_ref, n2_ref,
                   h1_ref, gain2_ref, core_ref, um_ref, uo_ref,
                   dk_ref, dv_ref, keep_ref, send_ref, g1_ref, gg_ref,
                   dm_s, dd_s, dq_s, dk_s, dv_s, b2_s, dml_s, dn_s, enc_s, n2_s, h1_s, late,
                   w_s, sem):
    s = pl.program_id(0)
    rows = g2_ref.shape[0]
    early = [pltpu.make_async_copy(src, dst, late.at[i])
             for i, (src, dst) in enumerate(((enc_ref, enc_s), (n2_ref, n2_s), (h1_ref, h1_s)))]

    def results(s):
        part = pl.ds(pl.multiple_of(s * ENC_LEN, ENC_LEN), ENC_LEN)
        return [pltpu.make_async_copy(src.at[part], dst.at[part], late.at[3 + 4 * i + s])
                for i, (src, dst) in enumerate(((dk_s, dk_ref), (dv_s, dv_ref)))]

    @pl.when(s == 0)
    def _():
        copies = weight_copies(core_ref, um_ref, uo_ref, w_s, sem)
        for copy in copies:
            copy.start()
        b2_s[...] = g2_ref[...].astype(bf16)
        for cb in col_blocks():
            put_gradient(keep_ref, send_ref, core_ref, 3, cb,
                         dot_tn(crossed_ref[...], b2_s[:, cb]))
        for copy in copies:
            copy.wait()
        for cb in col_blocks():
            put_pairs(dm_s, cb, rounded(dot_nt(b2_s[...], w_s[3, cb, :])))
        for copy in early:
            copy.start()
        clear_tail(dm_s, rows)
        clear_tail(dd_s, rows)
        for hp in range(PAIRS):
            cols = slice(hp * 128, hp * 128 + 128)
            dd_s[hp, 0:rows, :] = head_sums(dm_s[hp, 0:rows, :] * crossed_ref[:, cols].astype(f32))

    start = 0
    length = len_ref[0]
    for t in range(3):
        start = start + jnp.where(s > t, len_ref[t], 0)
        length = jnp.where(s == t + 1, len_ref[t + 1], length)
    lane = lane_index(MAX_LEN)
    lane_k = lane_index(ENC_LEN)
    valid = lax.broadcasted_iota(jnp.int32, (MAX_LEN, 128), 0) < length
    window = pl.ds(start, MAX_LEN)
    part = pl.ds(pl.multiple_of(s * ENC_LEN, ENC_LEN), ENC_LEN)

    def pair(hp, carry):
        cols = pl.ds(pl.multiple_of(hp * 128, 128), 128)
        q = cq_ref[0, :, cols]
        k = ck_ref[:, cols]
        v = cv_ref[:, cols]
        lse = other_half(lse_ref[0, :, cols])
        dm = jnp.where(valid, dm_s[hp, window, :], 0.0).astype(bf16)
        dd = other_half(jnp.where(valid, dd_s[hp, window, :], 0.0))
        dq = dk = dv = None
        for e in range(2):
            score = dot_nt(ones_beside(k, lane_k, e), augment(q, lse, lane, e))
            p = jnp.exp(score)
            back = dot_nt(ones_beside(v, lane_k, e), augment(dm, dd, lane, e))
            ds = (p * back).astype(bf16)
            mine = (lane < HEAD) if e == 0 else (lane >= HEAD)
            mine_k = (lane_k < HEAD) if e == 0 else (lane_k >= HEAD)
            dv_e = dot(p.astype(bf16), jnp.where(mine, dm, 0))
            dk_e = dot(ds, jnp.where(mine, q, 0))
            dq_e = dot_tn(ds, jnp.where(mine_k, k, 0))
            dq, dk, dv = (dq_e, dk_e, dv_e) if e == 0 else (dq + dq_e, dk + dk_e, dv + dv_e)
        dq_s[hp, window, :] = dq
        dk_s[part, cols] = dk.astype(bf16)
        dv_s[part, cols] = dv.astype(bf16)
        return carry

    lax.fori_loop(0, PAIRS, pair, 0, unroll=2)
    for copy in results(s):
        copy.start()

    @pl.when(s == pl.num_programs(0) - 1)
    def _():
        join_pairs(dml_s, dq_s, rows)
        for copy in early:
            copy.wait()
        for cb in col_blocks():
            put_gradient(keep_ref, send_ref, core_ref, 0, cb, dot_tn(n2_s[...], dml_s[:, cb]))
            put_gradient(keep_ref, send_ref, core_ref, 1, cb, dot_tn(enc_s[...], dk_s[:, cb]))
            put_gradient(keep_ref, send_ref, core_ref, 2, cb, dot_tn(enc_s[...], dv_s[:, cb]))
            dn_s[:, cb] = dot_nt(dml_s[...], w_s[0, cb, :])
        total = jnp.zeros((1, D), f32)
        for rb in row_blocks(rows):
            part, pulled = norm_back(dn_s[rb, :], h1_s[rb, :], gain2_ref[...])
            g1_ref[rb, :] = g2_ref[rb, :] + part
            total = total + jnp.sum(pulled, axis=0, keepdims=True)
        gg_ref[...] = total
        for step in range(4):
            for copy in results(step):
                copy.wait()


def encoded_back(core_ref, dk_ref, dv_ref, um_ref, uo_ref, *refs):
    ge_ref, w_s, sem = refs[-3:]
    @pl.when(pl.program_id(0) == 0)
    def _():
        copies = weight_copies(core_ref, um_ref, uo_ref, w_s, sem)
        for copy in copies:
            copy.start()
        for copy in copies:
            copy.wait()

    for cb in col_blocks():
        ge_ref[:, cb] = dot_nt(dk_ref[...], w_s[1, cb, :]) + dot_nt(dv_ref[...], w_s[2, cb, :])


def diagonal_sums(ref):
    total = ref[0:8, :]
    for r in range(8, MAX_LEN, 8):
        total = total + pltpu.roll(ref[r:r + 8, :], MAX_LEN - r, 1)
    row = lax.broadcasted_iota(jnp.int32, (8, MAX_LEN), 0)
    for bit in (1, 2, 4):
        total = jnp.where((row & bit) != 0, pltpu.roll(total, MAX_LEN - bit, 1), total)
    return jnp.sum(total, axis=0, keepdims=True)


def self_backward(len_ref, g1_ref, mixed_ref, q_ref, k_ref, v_ref, lse_ref, n1_ref,
                  lag_ref, core_ref, um_ref, uo_ref,
                  dq_ref, dk_ref, dv_ref, keep_ref, send_ref, gl_ref,
                  dm_s, dd_s, dq_s, dk_s, dv_s, b1_s, bias_s, acc_s, qh_s, kh_s, vh_s, lh_s, late,
                  w_s, sem):
    early = [pltpu.make_async_copy(src, dst, late.at[i]) for i, (src, dst) in enumerate(
        ((q_ref, qh_s), (k_ref, kh_s), (v_ref, vh_s), (lse_ref, lh_s)))]
    copies = weight_copies(core_ref, um_ref, uo_ref, w_s, sem)
    for copy in copies:
        copy.start()
    for copy in early:
        copy.start()
    rows = g1_ref.shape[0]
    count = q_ref.shape[0]
    b1_s[...] = g1_ref[...].astype(bf16)
    for cb in col_blocks():
        put_gradient(keep_ref, send_ref, core_ref, 3, cb, dot_tn(mixed_ref[...], b1_s[:, cb]))
    for copy in copies:
        copy.wait()
    for cb in col_blocks():
        put_pairs(dm_s, cb, rounded(dot_nt(b1_s[...], w_s[3, cb, :])))
    clear_tail(dm_s, rows)
    clear_tail(dd_s, rows)
    for hp in range(PAIRS):
        cols = slice(hp * 128, hp * 128 + 128)
        dd_s[hp, 0:rows, :] = head_sums(dm_s[hp, 0:rows, :] * mixed_ref[:, cols].astype(f32))
    starts = starts_of(len_ref)
    row = lax.broadcasted_iota(jnp.int32, (MAX_LEN, MAX_LEN), 0)
    col = lax.broadcasted_iota(jnp.int32, (MAX_LEN, MAX_LEN), 1)
    lane = lane_index(MAX_LEN)
    index = lax.broadcasted_iota(jnp.int32, (MAX_LEN, 128), 0)

    for copy in early:
        copy.wait()

    def pair(hp, carry):
        cols = pl.ds(pl.multiple_of(hp * 128, 128), 128)
        for e in range(2):
            w = jnp.broadcast_to(lag_ref[pl.ds(2 * hp + e, 1), :], (MAX_LEN, MAX_LEN))
            table = pltpu.roll(w, 0, 1, stride=1, stride_axis=0)
            bias_s[e] = jnp.where(col >= row, table, masked_score)
        for s in range(count):
            valid = index < len_ref[s]
            window = pl.ds(starts[s], MAX_LEN)
            q = qh_s[s, :, cols]
            k = kh_s[s, :, cols]
            v = vh_s[s, :, cols]
            lse = other_half(lh_s[s, :, cols])
            dm = jnp.where(valid, dm_s[hp, window, :], 0.0).astype(bf16)
            dd = other_half(jnp.where(valid, dd_s[hp, window, :], 0.0))
            dq = dk = dv = None
            for e in range(2):
                score = dot_nt(ones_beside(k, lane, e), augment(q, lse, lane, e)) + bias_s[e]
                p = jnp.exp(score)
                back = dot_nt(ones_beside(v, lane, e), augment(dm, dd, lane, e))
                grad = p * back
                if s == 0:
                    acc_s[e] = grad
                else:
                    acc_s[e] += grad
                ds = grad.astype(bf16)
                mine = (lane < HEAD) if e == 0 else (lane >= HEAD)
                dv_e = dot(p.astype(bf16), jnp.where(mine, dm, 0))
                dk_e = dot(ds, jnp.where(mine, q, 0))
                dq_e = dot_tn(ds, jnp.where(mine, k, 0))
                dq, dk, dv = (dq_e, dk_e, dv_e) if e == 0 else (dq + dq_e, dk + dk_e, dv + dv_e)
            dq_s[hp, window, :] = dq
            dk_s[hp, window, :] = dk
            dv_s[hp, window, :] = dv
        for e in range(2):
            gl_ref[pl.ds(2 * hp + e, 1), :] = diagonal_sums(acc_s.at[e])
        return carry

    lax.fori_loop(0, PAIRS, pair, 0, unroll=2)
    for w, (src, out) in enumerate(((dq_s, dq_ref), (dk_s, dk_ref), (dv_s, dv_ref))):
        join_pairs(out, src, rows)
        for cb in col_blocks():
            put_gradient(keep_ref, send_ref, core_ref, w, cb, dot_tn(n1_ref[...], out[:, cb]))


def hidden_back(core_ref, g1_ref, hid_ref, gain1_ref, dq_ref, dk_ref, dv_ref, gg2_ref, gg3_ref,
                gl_ref, um_ref, uo_ref, gh_ref, small_ref, dn_s, small_s, w_s, sem):
    copies = weight_copies(core_ref, um_ref, uo_ref, w_s, sem)
    for copy in copies:
        copy.start()
    for copy in copies:
        copy.wait()
    rows = g1_ref.shape[0]
    for cb in col_blocks():
        dn_s[:, cb] = (dot_nt(dq_ref[...], w_s[0, cb, :]) + dot_nt(dk_ref[...], w_s[1, cb, :])
                       + dot_nt(dv_ref[...], w_s[2, cb, :]))
    total = jnp.zeros((1, D), f32)
    for rb in row_blocks(rows):
        part, pulled = norm_back(dn_s[rb, :], hid_ref[rb, :].astype(f32), gain1_ref[...])
        gh_ref[rb, :] = g1_ref[rb, :] + part
        total = total + jnp.sum(pulled, axis=0, keepdims=True)
    small_s[...] = jnp.zeros(small_s.shape, f32)
    small_s[0:1, :] = total
    small_s[1:2, :] = gg2_ref[...]
    small_s[2:3, :] = gg3_ref[...]
    small_s[3:3 + HEADS, 0:MAX_LEN] = gl_ref[...]
    small_ref[...] = small_s[...].astype(bf16)


def bucket_table():
    lags = np.arange(MAX_LEN)
    exact = BUCKETS // 2
    bucket = np.minimum(lags, exact)
    for step in range(1, exact):
        edge = math.ceil(exact * (MAX_DIST / exact) ** (step / exact))
        bucket = bucket + (lags >= edge)
    return (bucket[None, :] == np.arange(BUCKETS)[:, None]).astype(np.float32)


def shape(dims, kind):
    return jax.ShapeDtypeStruct(dims, kind)


def call(kernel, name, micros, grant, outs, ins, scratch, **extra):
    return pl.pallas_call(
        kernel,
        out_shape=list(outs),
        name=name,
        scratch_shapes=scratch,
        cost_estimate=pl.CostEstimate(
            flops=int(micros * 1e9), bytes_accessed=1 << 20, transcendentals=0),
        compiler_params=pltpu.CompilerParams(vmem_limit_bytes=grant << 20),
        **extra,
    )(*ins)


def whole(array_shape):
    zeros = (0,) * len(array_shape)
    return pl.BlockSpec(array_shape, lambda s: zeros)


class Routes:
    def __init__(self):
        self.parts = lax.axis_size("dp")
        self.shards = lax.axis_size("fsdp")
        self.dp = lax.axis_index("dp")
        self.z = lax.axis_index("fsdp")
        self.core = self.dp & 1
        bits = list(range(1, self.parts.bit_length() - 1))
        self.steps = list(zip(bits, bits[::-1]))

    def permute(self, value, partner):
        pairs = []
        for dp in range(self.parts):
            for z in range(self.shards):
                to_dp, to_z = partner(dp, z)
                pairs.append((dp * self.shards + z, to_dp * self.shards + to_z))
        return lax.ppermute(value, ("dp", "fsdp"), pairs)

    def swap_core(self, value):
        return self.permute(value, lambda dp, z: (dp ^ 1, z))

    def swap(self, value, step):
        return self.permute(value, lambda dp, z: (dp ^ (1 << step[dp & 1]), z))

    def shift(self, value, by):
        return self.permute(value, lambda dp, z: (dp, (z + by) % self.shards))

    def bit(self, step):
        return jnp.where(self.core == 0, (self.dp >> step[0]) & 1, (self.dp >> step[1]) & 1)

    def piece_index(self):
        index = self.core
        for step in self.steps:
            index = 2 * index + self.bit(step)
        return index

    def shift_all(self, own):
        return [own] + [self.shift(own, by) for by in range(1, self.shards)]

    def stack_shards(self, got):
        return jnp.stack([
            lax.select_n((self.z - z) % self.shards, *got) for z in range(self.shards)])

    def collect(self, piece):
        for step in reversed(self.steps):
            piece = self.join(piece, self.swap(piece, step), step)
        return piece, self.swap_core(piece)

    def join(self, piece, got, step):
        return jnp.where(self.bit(step) == 0, jnp.concatenate([piece, got], 1),
                         jnp.concatenate([got, piece], 1))

    def halve(self, total, step):
        size = total.shape[1] // 2
        bit = self.bit(step)
        send = lax.dynamic_slice_in_dim(total, (1 - bit) * size, size, 1)
        keep = lax.dynamic_slice_in_dim(total, bit * size, size, 1)
        return keep, self.swap(send, step)

    def send_shards(self, total):
        parts = [lax.dynamic_index_in_dim(total, self.z, 0, keepdims=False)]
        for by in range(1, self.shards):
            chunk = lax.dynamic_index_in_dim(total, (self.z + by) % self.shards, 0, keepdims=False)
            parts.append(self.shift(chunk, by))
        return parts


def add(left, right):
    return (left.astype(f32) + right.astype(f32)).astype(bf16)


HALVES = (4, 2, D // 4, D)
WEIGHTS = [pltpu.VMEM((4, D, D), bf16), pltpu.SemaphoreType.DMA((8,))]
SQUARE = pltpu.VMEM((2, MAX_LEN, MAX_LEN), f32)
LINE = whole((1, D))
ENC_BLOCK = pl.BlockSpec((ENC_LEN, D), lambda s: (s, 0))
SEQ_BLOCK = pl.BlockSpec((1, MAX_LEN, D), lambda s: (s, 0, 0))


def scratch_of(rows):
    wide = pltpu.VMEM((PAIRS, rows + MAX_LEN, 128), f32)
    return wide, pltpu.VMEM((rows, D), bf16), pltpu.VMEM((rows, D), f32)


def run_self_forward(lengths, core, hidden, gain1, gain2, turned, u_self):
    rows = hidden.shape[0]
    heads = (lengths.shape[0], MAX_LEN, D)
    wide, low, flat = scratch_of(rows)
    return call(
        self_forward, "self_forward", 21, 60,
        (shape((rows, D), bf16), shape(heads, bf16), shape(heads, bf16), shape(heads, bf16),
         shape(heads, f32), shape((rows, D), bf16), shape((rows, D), f32), shape((rows, D), bf16)),
        (lengths, core, hidden, gain1, gain2, turned, *u_self),
        [wide, wide, wide, wide, SQUARE] + WEIGHTS,
        in_specs=[SMEM] * 2 + [VMEM] * 4 + [ANY] * 2, out_specs=[VMEM] * 8)


def run_cross_forward(lengths, core, n2, h1, gain3, encoded, u_cross):
    rows = n2.shape[0]
    count = lengths.shape[0]
    heads = (count, MAX_LEN, D)
    wide, low, flat = scratch_of(rows)
    full = whole((rows, D))
    return call(
        cross_forward, "cross_forward", 34, 60,
        (shape(encoded.shape, bf16), shape(encoded.shape, bf16), shape(heads, bf16),
         shape(heads, f32), shape((rows, D), bf16), shape((rows, D), f32), shape((rows, D), bf16)),
        (lengths, core, n2, h1, gain3, encoded, *u_cross),
        [wide, wide] + WEIGHTS,
        grid=(count,),
        in_specs=[SMEM] * 2 + [full, full, LINE, ENC_BLOCK, ANY, ANY],
        out_specs=[ENC_BLOCK, ENC_BLOCK, SEQ_BLOCK, SEQ_BLOCK, full, full, full])


def run_feed_forward(lengths, group_ids, group_steps, group_weights, tags, mask, out_grad, n3, h2,
                     gain3, u_ffn):
    rows = n3.shape[0]
    quarter = D // 4
    wide, low, flat = scratch_of(rows)
    full = whole((rows, D))
    column = whole((rows, 1))
    x_block = pl.BlockSpec((4, 1, quarter, D), lambda g: (0, g, 0, 0))
    r_block = pl.BlockSpec((1, 4, quarter, D), lambda g: (g, 1, 0, 0))
    return call(
        feed_forward, "feed_forward", 32, 60,
        (shape((rows, D), bf16), shape((8, 4, quarter, D), bf16),
         shape((rows, D), f32), shape((1, D), f32)),
        (lengths, group_ids, group_steps, group_weights, tags, mask, out_grad, n3, h2, gain3,
         u_ffn, u_ffn),
        [low, flat, flat, low, low, pltpu.VMEM((8, 4, quarter, D), bf16),
         pltpu.SemaphoreType.DMA((8,))],
        grid=(4,),
        in_specs=[SMEM] * 4 + [column, column, full, full, full, LINE, x_block, r_block],
        out_specs=[full, ANY, full, LINE])


def run_cross_backward(lengths, g2, crossed, cq, lse, ck, cv, encoded, n2, h1, gain2, core,
                       u_cross):
    rows = g2.shape[0]
    count = lengths.shape[0]
    wide, low, flat = scratch_of(rows)
    full = whole((rows, D))
    return call(
        cross_backward, "cross_backward", 42, 60,
        (shape(encoded.shape, bf16), shape(encoded.shape, bf16), shape(HALVES, bf16),
         shape(HALVES, bf16), shape((rows, D), f32), shape((1, D), f32)),
        (lengths, g2, crossed, cq, lse, ck, cv, encoded, n2, h1, gain2, core, *u_cross),
        [wide, wide, wide, pltpu.VMEM(encoded.shape, bf16), pltpu.VMEM(encoded.shape, bf16),
         low, low, flat, pltpu.VMEM(encoded.shape, bf16), low, flat,
         pltpu.SemaphoreType.DMA((11,))] + WEIGHTS,
        grid=(count,),
        in_specs=[SMEM, full, full, SEQ_BLOCK, SEQ_BLOCK, ENC_BLOCK, ENC_BLOCK, ANY, ANY,
                  ANY, LINE, SMEM, ANY, ANY],
        out_specs=[ANY, ANY, whole(HALVES), whole(HALVES), full, LINE])


def run_self_backward(lengths, g1, mixed, q, k, v, lse, n1, by_lag, core, u_self):
    rows = g1.shape[0]
    wide, low, flat = scratch_of(rows)
    return call(
        self_backward, "self_backward", 28, 60,
        (shape((rows, D), bf16), shape((rows, D), bf16), shape((rows, D), bf16),
         shape(HALVES, bf16), shape(HALVES, bf16), shape((HEADS, MAX_LEN), f32)),
        (lengths, g1, mixed, q, k, v, lse, n1, by_lag, core, *u_self),
        [wide, wide, wide, wide, wide, low, SQUARE, SQUARE]
        + [pltpu.VMEM(value.shape, value.dtype) for value in (q, k, v, lse)]
        + [pltpu.SemaphoreType.DMA((4,))] + WEIGHTS,
        in_specs=[SMEM, VMEM, VMEM, ANY, ANY, ANY, ANY, VMEM, VMEM, SMEM, ANY, ANY], out_specs=[VMEM] * 6)


def run_hidden_back(core, g1, hidden, gain1, dq, dk, dv, gg2, gg3, grad_lag, u_self):
    rows = g1.shape[0]
    wide, low, flat = scratch_of(rows)
    return call(
        hidden_back, "hidden_back", 8, 60,
        (shape((rows, D), f32), shape((SMALL, D), bf16)),
        (core, g1, hidden, gain1, dq, dk, dv, gg2, gg3, grad_lag, *u_self),
        [flat, pltpu.VMEM((SMALL, D), f32)] + WEIGHTS,
        in_specs=[SMEM] + [VMEM] * 9 + [ANY] * 2, out_specs=[VMEM] * 2)


def run_encoded_back(core, dck, dcv, u_cross, before=None):
    half = dck.shape[0] // ENC_LEN // 2
    first = 0 if before is None else half
    block = pl.BlockSpec((ENC_LEN, D), lambda s: (s + first, 0))
    more = () if before is None else (before,)
    return call(
        encoded_back, "encoded_back", 6, 60,
        (shape(dck.shape, f32),),
        (core, dck, dcv, *u_cross, *more),
        WEIGHTS,
        grid=(half,),
        input_output_aliases={} if before is None else {5: 0},
        in_specs=[SMEM, block, block, ANY, ANY] + [ANY] * len(more), out_specs=[block])


def add_all(parts):
    total = parts[0].astype(f32)
    for part in parts[1:]:
        total = total + part.astype(f32)
    return total.astype(bf16)


def tie(value, *after):
    return lax.optimization_barrier((value, *after))[0]


def tie_all(values, *after):
    return lax.optimization_barrier((*values, *after))[:len(values)]


def per_device(
    hidden, encoded, out_grad, lengths, group_ids, id_tags, loss_mask, group_steps, group_weights,
    gain_self, gain_cross, gain_ffn, rel_bias,
    query_weight, key_weight, value_weight, output_weight,
    cross_query, cross_key, cross_value, cross_output, expand_weight, reduce_weight,
):
    rows = hidden.shape[0]
    count = lengths.shape[0]
    quarter = D // 4
    routes = Routes()
    core = routes.core.reshape(1)
    size = D // routes.parts

    def piece_of(parts, index, extent):
        return lax.dynamic_slice_in_dim(jnp.concatenate(parts, 0), index * extent, extent, 0)

    small = jnp.concatenate([gain_self, gain_cross, gain_ffn, rel_bias.reshape(-1)])
    small_row = jnp.pad(small[None], ((0, 15), (0, D - small.shape[0])))
    own = piece_of([query_weight, key_weight, value_weight, output_weight],
                   routes.piece_index(), size)
    first = lax.all_gather(jnp.concatenate([own, small_row], 0)[None], "fsdp", axis=0, tiled=True)
    small = first[:, size, :small.shape[0]].astype(f32)
    cross_own = piece_of([cross_query, cross_key, cross_value, cross_output],
                         routes.piece_index(), size)
    self_piece = first[:, :size]
    cross_got = routes.shift_all(tie(cross_own, first))
    for step in routes.steps[:0:-1]:
        self_piece = routes.join(self_piece, routes.swap(self_piece, step), step)
    start_ffn = self_piece
    cross_piece = routes.stack_shards(tie_all(cross_got, self_piece))
    for step in routes.steps[:0:-1]:
        cross_piece = routes.join(cross_piece, routes.swap(cross_piece, step), step)
    step = routes.steps[0]
    self_piece = routes.join(self_piece, tie(routes.swap(self_piece, step), cross_piece), step)
    self_other = routes.swap_core(self_piece)
    cross_last = routes.swap(cross_piece, routes.steps[0])
    u_self = [half.reshape(HALVES) for half in (self_piece, self_other)]
    ratio = routes.parts // 8
    slot, offset = routes.dp // ratio, (routes.dp % ratio) * (quarter // ratio)
    own = jnp.where(
        slot < 4,
        lax.dynamic_slice(expand_weight, (offset, jnp.minimum(slot, 3) * D), (quarter // ratio, D)),
        lax.dynamic_slice_in_dim(
            reduce_weight, jnp.maximum(slot - 4, 0) * quarter + offset, quarter // ratio, 0))
    u_ffn = lax.all_gather(tie(own, start_ffn), ("fsdp", "dp"), axis=0, tiled=True)
    u_ffn = u_ffn.reshape(4, 8, quarter, D)

    gain1 = small[:, 0:quarter].reshape(1, D)
    gain2 = small[:, quarter:2 * quarter].reshape(1, D)
    gain3 = small[:, 2 * quarter:3 * quarter].reshape(1, D)
    rel = small[:, 3 * quarter:].reshape(HEADS, BUCKETS)
    table = bucket_table()
    by_lag = jnp.dot(rel, jnp.asarray(table), precision=lax.Precision.HIGHEST)
    turned = jnp.dot(
        rel, jnp.asarray(table[:, (-np.arange(MAX_LEN)) % MAX_LEN]), precision=lax.Precision.HIGHEST)

    n1, q, k, v, lse, mixed, h1, n2 = run_self_forward(
        lengths, core, hidden, gain1, gain2, turned, u_self)
    cross_piece = routes.join(cross_piece, tie(cross_last, n2), routes.steps[0])
    u_cross = [half.reshape(HALVES) for half in (cross_piece, routes.swap_core(cross_piece))]
    ck, cv, cq, cross_lse, crossed, h2, n3 = run_cross_forward(
        lengths, core, n2, h1, gain3, encoded, u_cross)
    layer_output, grad_ffn, g2, gg3 = run_feed_forward(
        lengths, group_ids, group_steps, group_weights, id_tags[:, None], loss_mask[:, None],
        out_grad, n3, h2, gain3, u_ffn)
    if routes.parts > 8:
        grad_ffn = grad_ffn.reshape(8, 4, routes.parts // 8, -1, D).swapaxes(1, 2)
    ffn_piece = lax.psum_scatter(
        grad_ffn.reshape(-1, D), "dp", scatter_dimension=0, tiled=True)

    dck, dcv, keep, send, g1, gg2 = run_cross_backward(
        lengths, g2, crossed, cq, cross_lse, ck, cv, encoded, n2, h1, gain2, core, u_cross)
    first_step, later_steps = routes.steps[0], routes.steps[1:]
    half = (4, D // 2, D)
    got = routes.swap_core(send.reshape(half))
    (grad_encoded,) = run_encoded_back(core, tie(dck, g1), dcv, u_cross)
    cross_total = add(keep.reshape(half), tie(got, grad_encoded))
    cross_keep, cross_got = routes.halve(cross_total, first_step)

    ffn_half = ffn_piece
    ffn_piece = lax.psum_scatter(ffn_piece, "fsdp", scatter_dimension=0, tiled=True)
    ffn = lax.all_gather(ffn_piece, "dp", axis=0, tiled=True).astype(f32)

    dq, dk, dv, keep, send, grad_lag = run_self_backward(
        lengths, tie(g1, cross_total), mixed, q, k, v, lse, n1, by_lag, core, u_self)
    cross_total = add(cross_keep, tie(cross_got, dq))
    got = routes.swap_core(tie(send, cross_total, ffn_half).reshape(half))
    for step in later_steps:
        cross_keep, cross_got = routes.halve(cross_total, step)
        if step is not later_steps[-1]:
            cross_total = add(cross_keep, cross_got)
    self_total = add(keep.reshape(half), tie(got, ffn_half))
    self_keep, self_got = routes.halve(self_total, first_step)

    grad_hidden, small = run_hidden_back(
        core, g1, hidden, gain1, tie(dq, self_total), dk, dv, gg2, gg3, grad_lag, u_self)
    cross_total = add(cross_keep, tie(cross_got, grad_hidden))
    self_total = add(self_keep, tie(self_got, grad_hidden, cross_total, ffn_piece))
    first_total = self_total
    cross_parts = routes.send_shards(tie(cross_total, self_total))
    for step in later_steps:
        self_keep, self_got = routes.halve(self_total, step)
        if step is not later_steps[-1]:
            self_total = add(self_keep, self_got)
    (grad_encoded,) = run_encoded_back(
        core, tie(dck, first_total), dcv, u_cross, grad_encoded)
    self_total = add(self_keep, tie(self_got, grad_encoded))
    self_parts = routes.send_shards(jnp.concatenate(
        [self_total, jnp.broadcast_to(small[None], (4, SMALL, D))], axis=1))
    piece = jnp.concatenate(
        [add_all(self_parts), add_all(tie_all(cross_parts, self_total))], axis=0)

    mine, other = routes.collect(piece[None])
    mine = mine.reshape(routes.parts // 2, 2 * size + SMALL, D)
    other = other.reshape(routes.parts // 2, 2 * size + SMALL, D)
    small = jnp.sum(mine[:, size:size + SMALL].astype(f32), 0) + jnp.sum(
        other[:, size:size + SMALL].astype(f32), 0)
    gains = lax.dynamic_slice_in_dim(small[0:3], routes.z * quarter, quarter, 1)
    lag = lax.dynamic_slice_in_dim(small[3:3 + HEADS, :MAX_LEN], routes.z * (HEADS // 4), HEADS // 4, 0)
    grad_rel = lax.dot_general(
        lag, jnp.asarray(table), (((1,), (1,)), ((), ())), precision=lax.Precision.HIGHEST)

    def weight_grads(first):
        own = [value[:, first:first + size].reshape(2, quarter, D) for value in (mine, other)]
        lows = jnp.where(routes.core == 0, own[0], own[1]).astype(f32)
        highs = jnp.where(routes.core == 0, own[1], own[0]).astype(f32)
        return lows[0], lows[1], highs[0], highs[1]

    return (
        layer_output,
        grad_hidden,
        grad_encoded,
        gains[0],
        gains[1],
        gains[2],
        grad_rel,
        *weight_grads(0),
        *weight_grads(size + SMALL),
        jnp.concatenate([ffn[g * quarter:(g + 1) * quarter] for g in range(4)], axis=1),
        ffn[D:],
    )


def solution(mesh):
    rows = P(("dp", "fsdp"), None)
    flat = P(("dp", "fsdp"))
    shard = P("fsdp", None)
    line = P("fsdp")
    return jax.shard_map(
        per_device,
        mesh=mesh,
        in_specs=(rows, rows, rows, flat, flat, flat, flat, P(), P(), line, line, line) + (shard,) * 11,
        out_specs=(rows, rows, rows, line, line, line) + (shard,) * 11,
        check_vma=False,
    )
```

```python
from functools import partial
import math

import jax
import jax.numpy as jnp
import numpy as np
from jax import lax
from jax.experimental import pallas as pl
from jax.experimental.pallas import tpu as pltpu
from jax.sharding import PartitionSpec as P

HEADS = 12
HEAD = 64
PAIRS = 6
BUCKETS = 32
MAX_DIST = 128
ENC_LEN = 512
MAX_LEN = 256
GROUPS = 3
HORIZON = 10000
D = 768
COLS = 768
SMALL = 16

f32 = jnp.float32
bf16 = jnp.bfloat16
epsilon = 1e-06
masked_score = -1000000000.0

VMEM = pl.BlockSpec(memory_space=pltpu.VMEM)
SMEM = pl.BlockSpec(memory_space=pltpu.SMEM)
ANY = pl.BlockSpec(memory_space=pl.ANY)


def dot(left, right):
    return jnp.dot(left, right, preferred_element_type=f32)


def dot_nt(left, right):
    return lax.dot_general(left, right, (((1,), (1,)), ((), ())), preferred_element_type=f32)


def dot_tn(left, right):
    return lax.dot_general(left, right, (((0,), (0,)), ((), ())), preferred_element_type=f32)


def rounded(value):
    return value.astype(bf16).astype(f32)


def row_scale(rows):
    return lax.rsqrt(jnp.mean(rows * rows, axis=-1, keepdims=True) + epsilon)


def row_blocks(rows):
    return [slice(r, r + 128) for r in range(0, rows, 128)]


def col_blocks(width=D):
    return [slice(c, c + COLS) for c in range(0, width, COLS)]


def starts_of(len_ref):
    starts = [0]
    for s in range(3):
        starts.append(starts[-1] + len_ref[s])
    return starts


def norm_back(grad, rows, gain):
    r = row_scale(rows)
    pulled = gain * grad
    inner = jnp.mean(pulled * rows, axis=-1, keepdims=True)
    return r * pulled - rows * (r * r * r * inner), grad * rows * r


def split_three(value):
    high = value.astype(bf16)
    rest = value - high.astype(f32)
    mid = rest.astype(bf16)
    return high, mid, (rest - mid.astype(f32)).astype(bf16)


def weight_copies(core_ref, mine_ref, other_ref, w_s, sem):
    core = core_ref[0]
    quarter = D // 4
    copies = []
    for h, ref in enumerate((mine_ref, other_ref)):
        first = 2 * core if h == 0 else 2 * (1 - core)
        for z in range(4):
            copies.append(pltpu.make_async_copy(
                ref.at[z], w_s.at[pl.ds(first, 2), pl.ds(z * quarter, quarter), :],
                sem.at[4 * h + z]))
    return copies


def put_gradient(keep_ref, send_ref, core_ref, index, cb, value):
    value = value.astype(bf16).reshape(4, D // 4, COLS)
    stays = core_ref[0] == index // 2

    @pl.when(stays)
    def _():
        keep_ref[:, index % 2, :, cb] = value

    @pl.when(jnp.logical_not(stays))
    def _():
        send_ref[:, index % 2, :, cb] = value


def put_pairs(dst, cb, value):
    first = cb.start // 128
    for part in range(COLS // 128):
        dst[first + part, 0:value.shape[0], :] = value[:, part * 128:part * 128 + 128]


def clear_tail(dst, rows):
    dst[:, rows:, :] = jnp.zeros((PAIRS, dst.shape[1] - rows, 128), f32)


def join_pairs(dst, src, rows):
    for hp in range(PAIRS):
        dst[:, hp * 128:hp * 128 + 128] = src[hp, 0:rows, :].astype(dst.dtype)


def by_length(length, sizes, body):
    below = 0
    for size in sizes:
        fits = length > below if size == sizes[-1] else (length > below) & (length <= size)
        pl.when(fits)(lambda size=size: body(size))
        below = size


def clear_rows(ref, s, first):
    if first < MAX_LEN:
        ref[s, first:, :] = jnp.zeros((MAX_LEN - first, D), ref.dtype)


def start_of(len_ref, s):
    start = 0
    for t in range(3):
        start = start + jnp.where(s > t, len_ref[t], 0)
    return start


def lane_index(rows):
    return lax.broadcasted_iota(jnp.int32, (rows, 128), 1)


def self_forward(len_ref, core_ref, hid_ref, gain1_ref, gain2_ref, lag_ref, um_ref, uo_ref,
                 n1_ref, q_ref, k_ref, v_ref, lse_ref, mixed_ref, h1_ref, n2_ref,
                 q_s, k_s, v_s, m_s, bias_s, w_s, sem):
    copies = weight_copies(core_ref, um_ref, uo_ref, w_s, sem)
    for copy in copies:
        copy.start()
    rows = hid_ref.shape[0]
    count = q_ref.shape[0]
    for rb in row_blocks(rows):
        x = hid_ref[rb, :].astype(f32)
        n1_ref[rb, :] = (x * row_scale(x) * gain1_ref[...]).astype(bf16)
    for copy in copies:
        copy.wait()
    for w, dst in enumerate((q_s, k_s, v_s)):
        for cb in col_blocks():
            put_pairs(dst, cb, rounded(dot(n1_ref[...], w_s[w, :, cb])))
        clear_tail(dst, rows)
    starts = starts_of(len_ref)
    row = lax.broadcasted_iota(jnp.int32, (MAX_LEN, MAX_LEN), 0)
    col = lax.broadcasted_iota(jnp.int32, (MAX_LEN, MAX_LEN), 1)
    lane = lane_index(MAX_LEN)
    even = lane < HEAD

    def pair(hp, carry):
        cols = pl.ds(pl.multiple_of(hp * 128, 128), 128)
        for e in range(2):
            w = jnp.broadcast_to(lag_ref[pl.ds(2 * hp + e, 1), :], (MAX_LEN, MAX_LEN))
            table = pltpu.roll(w, 0, 1, stride=1, stride_axis=0)
            bias_s[e] = jnp.where(row >= col, table, masked_score)
        for s in range(count):
            window = pl.ds(starts[s], MAX_LEN)
            q = q_s[hp, window, :].astype(bf16)
            k = k_s[hp, window, :].astype(bf16)
            v = v_s[hp, window, :].astype(bf16)
            q_ref[s, :, cols] = q
            k_ref[s, :, cols] = k
            v_ref[s, :, cols] = v
            res, tops = [], []
            for e in range(2):
                mine = even if e == 0 else ~even
                score = dot_nt(jnp.where(mine, q, 0), k) + bias_s[e]
                top = jnp.max(score, axis=-1, keepdims=True)
                p = jnp.exp(score - top).astype(bf16)
                res.append(dot(p, jnp.where(mine, v, 1)))
                tops.append(top)
            num = jnp.where(even, res[0], res[1])
            den = jnp.where(even, pltpu.roll(res[0], HEAD, 1), pltpu.roll(res[1], HEAD, 1))
            lse_ref[s, :, cols] = jnp.where(even, tops[0], tops[1]) + jnp.log(den)
            m_s[hp, window, :] = num / den
        return carry

    lax.fori_loop(0, PAIRS, pair, 0, unroll=2)
    join_pairs(mixed_ref, m_s, rows)
    for cb in col_blocks():
        h1_ref[:, cb] = hid_ref[:, cb].astype(f32) + dot(mixed_ref[...], w_s[3, :, cb])
    for rb in row_blocks(rows):
        x = h1_ref[rb, :]
        n2_ref[rb, :] = (x * row_scale(x) * gain2_ref[...]).astype(bf16)


def cross_forward(len_ref, core_ref, n2_ref, h1_ref, gain3_ref, enc_ref, um_ref, uo_ref,
                  ck_ref, cv_ref, cq_ref, lse_ref, crossed_ref, h2_ref, n3_ref,
                  q_s, m_s, w_s, sem):
    s = pl.program_id(0)
    rows = n2_ref.shape[0]
    count = pl.num_programs(0)

    @pl.when(s == 0)
    def _():
        copies = weight_copies(core_ref, um_ref, uo_ref, w_s, sem)
        for copy in copies:
            copy.start()
        for copy in copies:
            copy.wait()
        for cb in col_blocks():
            put_pairs(q_s, cb, rounded(dot(n2_ref[...], w_s[0, :, cb])))
        clear_tail(q_s, rows)

    for cb in col_blocks():
        ck_ref[:, cb] = dot(enc_ref[...], w_s[1, :, cb]).astype(bf16)
        cv_ref[:, cb] = dot(enc_ref[...], w_s[2, :, cb]).astype(bf16)
    start = start_of(len_ref, s)
    even_v = lane_index(ENC_LEN) < HEAD

    def attend(size):
        window = pl.ds(start, size)
        even = lane_index(size) < HEAD
        clear_rows(cq_ref, 0, size)
        clear_rows(lse_ref, 0, size)

        def pair(hp, carry):
            cols = pl.ds(pl.multiple_of(hp * 128, 128), 128)
            q = q_s[hp, window, :].astype(bf16)
            cq_ref[0, 0:size, cols] = q
            k = ck_ref[:, cols]
            v = cv_ref[:, cols]
            res, tops = [], []
            for e in range(2):
                mine = even if e == 0 else ~even
                mine_v = even_v if e == 0 else ~even_v
                score = dot_nt(jnp.where(mine, q, 0), k)
                top = jnp.max(score, axis=-1, keepdims=True)
                p = jnp.exp(score - top).astype(bf16)
                res.append(dot(p, jnp.where(mine_v, v, 1)))
                tops.append(top)
            num = jnp.where(even, res[0], res[1])
            den = jnp.where(even, pltpu.roll(res[0], HEAD, 1), pltpu.roll(res[1], HEAD, 1))
            lse_ref[0, 0:size, cols] = jnp.where(even, tops[0], tops[1]) + jnp.log(den)
            m_s[hp, window, :] = num / den
            return carry

        lax.fori_loop(0, PAIRS, pair, 0, unroll=2)

    by_length(len_ref[s], (64, 128, 192, 256), attend)

    @pl.when(s == count - 1)
    def _():
        join_pairs(crossed_ref, m_s, rows)
        for cb in col_blocks():
            h2_ref[:, cb] = h1_ref[:, cb] + dot(crossed_ref[...], w_s[3, :, cb])
        for rb in row_blocks(rows):
            x = h2_ref[rb, :]
            n3_ref[rb, :] = (x * row_scale(x) * gain3_ref[...]).astype(bf16)


def gelu_parts(x):
    decay = jnp.exp(-0.5 * (x * x))
    t = 1.0 / (1.0 + jnp.abs(x) * (0.3275911 / math.sqrt(2.0)))
    poly = t * (0.5 * 0.254829592 + t * (-0.5 * 0.284496736 + t * (
        0.5 * 1.421413741 + t * (-0.5 * 1.453152027 + t * (0.5 * 1.061405429)))))
    tail = poly * decay
    below = jnp.where(x >= 0, 1.0 - tail, tail)
    return x * below, below + x * decay * (1.0 / math.sqrt(2.0 * math.pi))


def feed_forward(len_ref, group_ref, step_ref, weight_ref, tags_ref, mask_ref, og_ref, n3_ref,
                 h2_ref, gain3_ref, x_ref, r_ref,
                 out_ref, gu_ref, g2_ref, gg_ref,
                 scaled_s, out_s, dn_s, act_s, de_s, gu_s, sem):
    g = pl.program_id(0)
    count = 4

    def copies(g):
        return (pltpu.make_async_copy(gu_s.at[g], gu_ref.at[g], sem.at[g]),
                pltpu.make_async_copy(
                    gu_s.at[pl.ds(4, 4), g], gu_ref.at[pl.ds(4, 4), g], sem.at[count + g]))

    rows = n3_ref.shape[0]

    def token_weight(rb):
        index = lax.broadcasted_iota(jnp.int32, (128, 1), 0) + rb.start
        scale = jnp.zeros((128, 1), f32)
        tagged = jnp.zeros((128, 1), jnp.int32)
        start = 0
        for s in range(4):
            group = group_ref[s]
            factor = jnp.float32(0.0)
            for k in range(GROUPS):
                value = weight_ref[k].astype(f32) * 0.25 * (
                    1.0 - step_ref[k].astype(f32) * (1.0 / (2.0 * HORIZON)))
                factor = jnp.where(group == k, value, factor)
            inside = index >= start
            scale = jnp.where(inside, factor, scale)
            tagged = jnp.where(inside, jnp.where(group == 1, 1, 0), tagged)
            start = start + len_ref[s]
        counted = jnp.where(tagged == 1, tags_ref[rb, :], mask_ref[rb, :]).astype(f32)
        return scale * (0.25 + 0.75 * counted)

    @pl.when(g == 0)
    def _():
        for rb in row_blocks(rows):
            scaled = og_ref[rb, :].astype(f32) * token_weight(rb)
            g2_ref[rb, :] = scaled
            scaled_s[rb, :] = scaled.astype(bf16)
        out_s[...] = h2_ref[...]
        dn_s[...] = jnp.zeros(dn_s.shape, f32)

    for cb in col_blocks():
        expanded = dot(n3_ref[...], x_ref[:, 0, :, cb].reshape(D, COLS))
        act, slope = gelu_parts(expanded)
        act_s[:, cb] = act.astype(bf16)
        back = dot_nt(scaled_s[...], r_ref[0].reshape(D, D)[cb, :])
        de_s[:, cb] = (back * slope).astype(bf16)
    for cb in col_blocks():
        out_s[:, cb] += dot(act_s[...], r_ref[0, :, :, cb].reshape(D, COLS))
        gx = dot_tn(n3_ref[...], de_s[:, cb]).astype(bf16)
        gr = dot_tn(act_s[...], scaled_s[:, cb]).astype(bf16)
        gu_s[g, :, :, cb] = gx.reshape(4, D // 4, COLS)
        for part in range(4):
            gu_s[4 + part, g, :, cb] = gr[part * (D // 4):(part + 1) * (D // 4), :]
    for copy in copies(g):
        copy.start()
    full = x_ref[:, 0].reshape(D, D)
    for cb in col_blocks():
        dn_s[:, cb] += dot_nt(de_s[...], full[cb, :])

    @pl.when(g == pl.num_programs(0) - 1)
    def _():
        total = jnp.zeros((1, D), f32)
        for rb in row_blocks(rows):
            out_ref[rb, :] = out_s[rb, :].astype(bf16)
            part, pulled = norm_back(dn_s[rb, :], h2_ref[rb, :], gain3_ref[...])
            g2_ref[rb, :] += part
            total = total + jnp.sum(pulled, axis=0, keepdims=True)
        gg_ref[...] = total
        for step in range(count):
            for copy in copies(step):
                copy.wait()


def head_sums(product):
    a = (lax.broadcasted_iota(jnp.int32, (256, 128), 0) & 127) < HEAD
    b = lax.broadcasted_iota(jnp.int32, (256, 128), 1) < HEAD
    ones = (a == b).astype(bf16)
    high = product.astype(bf16)
    rest = (product - high.astype(f32)).astype(bf16)
    return dot(jnp.concatenate([high, rest], axis=1), ones)


def augment(base, minus, lane, e):
    mine = (lane < HEAD) if e == 0 else (lane >= HEAD)
    spot = HEAD if e == 0 else 0
    high, mid, rest = split_three(-minus)
    extra = jnp.where(lane == spot, high, jnp.where(lane == spot + 1, mid, jnp.where(
        lane == spot + 2, rest, jnp.zeros_like(high))))
    return jnp.where(mine, base, extra)


def ones_beside(base, lane, e):
    mine = (lane < HEAD) if e == 0 else (lane >= HEAD)
    return jnp.where(mine, base, 1)


def other_half(value):
    return pltpu.roll(value, HEAD, 1)


def cross_backward(len_ref, g2_ref, crossed_ref, cq_ref, lse_ref, ck_ref, cv_ref, enc_ref, n2_ref,
                   h1_ref, gain2_ref, core_ref, um_ref, uo_ref,
                   dk_ref, dv_ref, keep_ref, send_ref, g1_ref, gg_ref,
                   dm_s, dd_s, dq_s, dk_s, dv_s, b2_s, dml_s, dn_s, enc_s, n2_s, h1_s, late,
                   w_s, sem):
    s = pl.program_id(0)
    rows = g2_ref.shape[0]
    early = [pltpu.make_async_copy(src, dst, late.at[i])
             for i, (src, dst) in enumerate(((enc_ref, enc_s), (n2_ref, n2_s), (h1_ref, h1_s)))]

    def results(s):
        part = pl.ds(pl.multiple_of(s * ENC_LEN, ENC_LEN), ENC_LEN)
        return [pltpu.make_async_copy(src.at[part], dst.at[part], late.at[3 + 4 * i + s])
                for i, (src, dst) in enumerate(((dk_s, dk_ref), (dv_s, dv_ref)))]

    @pl.when(s == 0)
    def _():
        copies = weight_copies(core_ref, um_ref, uo_ref, w_s, sem)
        for copy in copies:
            copy.start()
        b2_s[...] = g2_ref[...].astype(bf16)
        for cb in col_blocks():
            put_gradient(keep_ref, send_ref, core_ref, 3, cb,
                         dot_tn(crossed_ref[...], b2_s[:, cb]))
        for copy in copies:
            copy.wait()
        for cb in col_blocks():
            put_pairs(dm_s, cb, rounded(dot_nt(b2_s[...], w_s[3, cb, :])))
        for copy in early:
            copy.start()
        clear_tail(dm_s, rows)
        clear_tail(dd_s, rows)
        for hp in range(PAIRS):
            cols = slice(hp * 128, hp * 128 + 128)
            dd_s[hp, 0:rows, :] = head_sums(dm_s[hp, 0:rows, :] * crossed_ref[:, cols].astype(f32))

    start = 0
    length = len_ref[0]
    for t in range(3):
        start = start + jnp.where(s > t, len_ref[t], 0)
        length = jnp.where(s == t + 1, len_ref[t + 1], length)
    lane = lane_index(MAX_LEN)
    lane_k = lane_index(ENC_LEN)
    valid = lax.broadcasted_iota(jnp.int32, (MAX_LEN, 128), 0) < length
    window = pl.ds(start, MAX_LEN)
    part = pl.ds(pl.multiple_of(s * ENC_LEN, ENC_LEN), ENC_LEN)

    def pair(hp, carry):
        cols = pl.ds(pl.multiple_of(hp * 128, 128), 128)
        q = cq_ref[0, :, cols]
        k = ck_ref[:, cols]
        v = cv_ref[:, cols]
        lse = other_half(lse_ref[0, :, cols])
        dm = jnp.where(valid, dm_s[hp, window, :], 0.0).astype(bf16)
        dd = other_half(jnp.where(valid, dd_s[hp, window, :], 0.0))
        dq = dk = dv = None
        for e in range(2):
            score = dot_nt(ones_beside(k, lane_k, e), augment(q, lse, lane, e))
            p = jnp.exp(score)
            back = dot_nt(ones_beside(v, lane_k, e), augment(dm, dd, lane, e))
            ds = (p * back).astype(bf16)
            mine = (lane < HEAD) if e == 0 else (lane >= HEAD)
            mine_k = (lane_k < HEAD) if e == 0 else (lane_k >= HEAD)
            dv_e = dot(p.astype(bf16), jnp.where(mine, dm, 0))
            dk_e = dot(ds, jnp.where(mine, q, 0))
            dq_e = dot_tn(ds, jnp.where(mine_k, k, 0))
            dq, dk, dv = (dq_e, dk_e, dv_e) if e == 0 else (dq + dq_e, dk + dk_e, dv + dv_e)
        dq_s[hp, window, :] = dq
        dk_s[part, cols] = dk.astype(bf16)
        dv_s[part, cols] = dv.astype(bf16)
        return carry

    lax.fori_loop(0, PAIRS, pair, 0, unroll=2)
    for copy in results(s):
        copy.start()

    @pl.when(s == pl.num_programs(0) - 1)
    def _():
        join_pairs(dml_s, dq_s, rows)
        for copy in early:
            copy.wait()
        for cb in col_blocks():
            put_gradient(keep_ref, send_ref, core_ref, 0, cb, dot_tn(n2_s[...], dml_s[:, cb]))
            put_gradient(keep_ref, send_ref, core_ref, 1, cb, dot_tn(enc_s[...], dk_s[:, cb]))
            put_gradient(keep_ref, send_ref, core_ref, 2, cb, dot_tn(enc_s[...], dv_s[:, cb]))
            dn_s[:, cb] = dot_nt(dml_s[...], w_s[0, cb, :])
        total = jnp.zeros((1, D), f32)
        for rb in row_blocks(rows):
            part, pulled = norm_back(dn_s[rb, :], h1_s[rb, :], gain2_ref[...])
            g1_ref[rb, :] = g2_ref[rb, :] + part
            total = total + jnp.sum(pulled, axis=0, keepdims=True)
        gg_ref[...] = total
        for step in range(4):
            for copy in results(step):
                copy.wait()


def encoded_back(core_ref, dk_ref, dv_ref, um_ref, uo_ref, *refs):
    ge_ref, w_s, sem = refs[-3:]
    @pl.when(pl.program_id(0) == 0)
    def _():
        copies = weight_copies(core_ref, um_ref, uo_ref, w_s, sem)
        for copy in copies:
            copy.start()
        for copy in copies:
            copy.wait()

    for cb in col_blocks():
        ge_ref[:, cb] = dot_nt(dk_ref[...], w_s[1, cb, :]) + dot_nt(dv_ref[...], w_s[2, cb, :])


def diagonal_sums(ref):
    total = ref[0:8, :]
    for r in range(8, MAX_LEN, 8):
        total = total + pltpu.roll(ref[r:r + 8, :], MAX_LEN - r, 1)
    row = lax.broadcasted_iota(jnp.int32, (8, MAX_LEN), 0)
    for bit in (1, 2, 4):
        total = jnp.where((row & bit) != 0, pltpu.roll(total, MAX_LEN - bit, 1), total)
    return jnp.sum(total, axis=0, keepdims=True)


def self_backward(len_ref, g1_ref, mixed_ref, q_ref, k_ref, v_ref, lse_ref, n1_ref,
                  lag_ref, core_ref, um_ref, uo_ref,
                  dq_ref, dk_ref, dv_ref, keep_ref, send_ref, gl_ref,
                  dm_s, dd_s, dq_s, dk_s, dv_s, b1_s, bias_s, acc_s, qh_s, kh_s, vh_s, lh_s, late,
                  w_s, sem):
    early = [pltpu.make_async_copy(src, dst, late.at[i]) for i, (src, dst) in enumerate(
        ((q_ref, qh_s), (k_ref, kh_s), (v_ref, vh_s), (lse_ref, lh_s)))]
    copies = weight_copies(core_ref, um_ref, uo_ref, w_s, sem)
    for copy in copies:
        copy.start()
    for copy in early:
        copy.start()
    rows = g1_ref.shape[0]
    count = q_ref.shape[0]
    b1_s[...] = g1_ref[...].astype(bf16)
    for cb in col_blocks():
        put_gradient(keep_ref, send_ref, core_ref, 3, cb, dot_tn(mixed_ref[...], b1_s[:, cb]))
    for copy in copies:
        copy.wait()
    for cb in col_blocks():
        put_pairs(dm_s, cb, rounded(dot_nt(b1_s[...], w_s[3, cb, :])))
    clear_tail(dm_s, rows)
    clear_tail(dd_s, rows)
    for hp in range(PAIRS):
        cols = slice(hp * 128, hp * 128 + 128)
        dd_s[hp, 0:rows, :] = head_sums(dm_s[hp, 0:rows, :] * mixed_ref[:, cols].astype(f32))
    starts = starts_of(len_ref)
    row = lax.broadcasted_iota(jnp.int32, (MAX_LEN, MAX_LEN), 0)
    col = lax.broadcasted_iota(jnp.int32, (MAX_LEN, MAX_LEN), 1)
    lane = lane_index(MAX_LEN)
    index = lax.broadcasted_iota(jnp.int32, (MAX_LEN, 128), 0)

    for copy in early:
        copy.wait()

    def pair(hp, carry):
        cols = pl.ds(pl.multiple_of(hp * 128, 128), 128)
        for e in range(2):
            w = jnp.broadcast_to(lag_ref[pl.ds(2 * hp + e, 1), :], (MAX_LEN, MAX_LEN))
            table = pltpu.roll(w, 0, 1, stride=1, stride_axis=0)
            bias_s[e] = jnp.where(col >= row, table, masked_score)
        for s in range(count):
            valid = index < len_ref[s]
            window = pl.ds(starts[s], MAX_LEN)
            q = qh_s[s, :, cols]
            k = kh_s[s, :, cols]
            v = vh_s[s, :, cols]
            lse = other_half(lh_s[s, :, cols])
            dm = jnp.where(valid, dm_s[hp, window, :], 0.0).astype(bf16)
            dd = other_half(jnp.where(valid, dd_s[hp, window, :], 0.0))
            dq = dk = dv = None
            for e in range(2):
                score = dot_nt(ones_beside(k, lane, e), augment(q, lse, lane, e)) + bias_s[e]
                p = jnp.exp(score)
                back = dot_nt(ones_beside(v, lane, e), augment(dm, dd, lane, e))
                grad = p * back
                if s == 0:
                    acc_s[e] = grad
                else:
                    acc_s[e] += grad
                ds = grad.astype(bf16)
                mine = (lane < HEAD) if e == 0 else (lane >= HEAD)
                dv_e = dot(p.astype(bf16), jnp.where(mine, dm, 0))
                dk_e = dot(ds, jnp.where(mine, q, 0))
                dq_e = dot_tn(ds, jnp.where(mine, k, 0))
                dq, dk, dv = (dq_e, dk_e, dv_e) if e == 0 else (dq + dq_e, dk + dk_e, dv + dv_e)
            dq_s[hp, window, :] = dq
            dk_s[hp, window, :] = dk
            dv_s[hp, window, :] = dv
        for e in range(2):
            gl_ref[pl.ds(2 * hp + e, 1), :] = diagonal_sums(acc_s.at[e])
        return carry

    lax.fori_loop(0, PAIRS, pair, 0, unroll=2)
    for w, (src, out) in enumerate(((dq_s, dq_ref), (dk_s, dk_ref), (dv_s, dv_ref))):
        join_pairs(out, src, rows)
        for cb in col_blocks():
            put_gradient(keep_ref, send_ref, core_ref, w, cb, dot_tn(n1_ref[...], out[:, cb]))


def hidden_back(core_ref, g1_ref, hid_ref, gain1_ref, dq_ref, dk_ref, dv_ref, gg2_ref, gg3_ref,
                gl_ref, um_ref, uo_ref, gh_ref, small_ref, dn_s, small_s, w_s, sem):
    copies = weight_copies(core_ref, um_ref, uo_ref, w_s, sem)
    for copy in copies:
        copy.start()
    for copy in copies:
        copy.wait()
    rows = g1_ref.shape[0]
    for cb in col_blocks():
        dn_s[:, cb] = (dot_nt(dq_ref[...], w_s[0, cb, :]) + dot_nt(dk_ref[...], w_s[1, cb, :])
                       + dot_nt(dv_ref[...], w_s[2, cb, :]))
    total = jnp.zeros((1, D), f32)
    for rb in row_blocks(rows):
        part, pulled = norm_back(dn_s[rb, :], hid_ref[rb, :].astype(f32), gain1_ref[...])
        gh_ref[rb, :] = g1_ref[rb, :] + part
        total = total + jnp.sum(pulled, axis=0, keepdims=True)
    small_s[...] = jnp.zeros(small_s.shape, f32)
    small_s[0:1, :] = total
    small_s[1:2, :] = gg2_ref[...]
    small_s[2:3, :] = gg3_ref[...]
    small_s[3:3 + HEADS, 0:MAX_LEN] = gl_ref[...]
    small_ref[...] = small_s[...].astype(bf16)


def bucket_table():
    lags = np.arange(MAX_LEN)
    exact = BUCKETS // 2
    bucket = np.minimum(lags, exact)
    for step in range(1, exact):
        edge = math.ceil(exact * (MAX_DIST / exact) ** (step / exact))
        bucket = bucket + (lags >= edge)
    return (bucket[None, :] == np.arange(BUCKETS)[:, None]).astype(np.float32)


def shape(dims, kind):
    return jax.ShapeDtypeStruct(dims, kind)


def call(kernel, name, micros, grant, outs, ins, scratch, **extra):
    return pl.pallas_call(
        kernel,
        out_shape=list(outs),
        name=name,
        scratch_shapes=scratch,
        cost_estimate=pl.CostEstimate(
            flops=int(micros * 1e9), bytes_accessed=1 << 20, transcendentals=0),
        compiler_params=pltpu.CompilerParams(vmem_limit_bytes=grant << 20),
        **extra,
    )(*ins)


def whole(array_shape):
    zeros = (0,) * len(array_shape)
    return pl.BlockSpec(array_shape, lambda s: zeros)


class Routes:
    def __init__(self):
        self.parts = lax.axis_size("dp")
        self.shards = lax.axis_size("fsdp")
        self.dp = lax.axis_index("dp")
        self.z = lax.axis_index("fsdp")
        self.core = self.dp & 1
        bits = list(range(1, self.parts.bit_length() - 1))
        self.steps = list(zip(bits, bits[::-1]))

    def permute(self, value, partner):
        pairs = []
        for dp in range(self.parts):
            for z in range(self.shards):
                to_dp, to_z = partner(dp, z)
                pairs.append((dp * self.shards + z, to_dp * self.shards + to_z))
        return lax.ppermute(value, ("dp", "fsdp"), pairs)

    def swap_core(self, value):
        return self.permute(value, lambda dp, z: (dp ^ 1, z))

    def swap(self, value, step):
        return self.permute(value, lambda dp, z: (dp ^ (1 << step[dp & 1]), z))

    def shift(self, value, by):
        return self.permute(value, lambda dp, z: (dp, (z + by) % self.shards))

    def bit(self, step):
        return jnp.where(self.core == 0, (self.dp >> step[0]) & 1, (self.dp >> step[1]) & 1)

    def piece_index(self):
        index = self.core
        for step in self.steps:
            index = 2 * index + self.bit(step)
        return index

    def shift_all(self, own):
        return [own] + [self.shift(own, by) for by in range(1, self.shards)]

    def stack_shards(self, got):
        return jnp.stack([
            lax.select_n((self.z - z) % self.shards, *got) for z in range(self.shards)])

    def collect(self, piece):
        for step in reversed(self.steps):
            piece = self.join(piece, self.swap(piece, step), step)
        return piece, self.swap_core(piece)

    def join(self, piece, got, step):
        return jnp.where(self.bit(step) == 0, jnp.concatenate([piece, got], 1),
                         jnp.concatenate([got, piece], 1))

    def halve(self, total, step):
        size = total.shape[1] // 2
        bit = self.bit(step)
        send = lax.dynamic_slice_in_dim(total, (1 - bit) * size, size, 1)
        keep = lax.dynamic_slice_in_dim(total, bit * size, size, 1)
        return keep, self.swap(send, step)

    def send_shards(self, total):
        parts = [lax.dynamic_index_in_dim(total, self.z, 0, keepdims=False)]
        for by in range(1, self.shards):
            chunk = lax.dynamic_index_in_dim(total, (self.z + by) % self.shards, 0, keepdims=False)
            parts.append(self.shift(chunk, by))
        return parts


def add(left, right):
    return (left.astype(f32) + right.astype(f32)).astype(bf16)


HALVES = (4, 2, D // 4, D)
WEIGHTS = [pltpu.VMEM((4, D, D), bf16), pltpu.SemaphoreType.DMA((8,))]
SQUARE = pltpu.VMEM((2, MAX_LEN, MAX_LEN), f32)
LINE = whole((1, D))
ENC_BLOCK = pl.BlockSpec((ENC_LEN, D), lambda s: (s, 0))
SEQ_BLOCK = pl.BlockSpec((1, MAX_LEN, D), lambda s: (s, 0, 0))


def scratch_of(rows):
    wide = pltpu.VMEM((PAIRS, rows + MAX_LEN, 128), f32)
    return wide, pltpu.VMEM((rows, D), bf16), pltpu.VMEM((rows, D), f32)


def run_self_forward(lengths, core, hidden, gain1, gain2, turned, u_self):
    rows = hidden.shape[0]
    heads = (lengths.shape[0], MAX_LEN, D)
    wide, low, flat = scratch_of(rows)
    return call(
        self_forward, "self_forward", 21, 60,
        (shape((rows, D), bf16), shape(heads, bf16), shape(heads, bf16), shape(heads, bf16),
         shape(heads, f32), shape((rows, D), bf16), shape((rows, D), f32), shape((rows, D), bf16)),
        (lengths, core, hidden, gain1, gain2, turned, *u_self),
        [wide, wide, wide, wide, SQUARE] + WEIGHTS,
        in_specs=[SMEM] * 2 + [VMEM] * 4 + [ANY] * 2, out_specs=[VMEM] * 8)


def run_cross_forward(lengths, core, n2, h1, gain3, encoded, u_cross):
    rows = n2.shape[0]
    count = lengths.shape[0]
    heads = (count, MAX_LEN, D)
    wide, low, flat = scratch_of(rows)
    full = whole((rows, D))
    return call(
        cross_forward, "cross_forward", 34, 60,
        (shape(encoded.shape, bf16), shape(encoded.shape, bf16), shape(heads, bf16),
         shape(heads, f32), shape((rows, D), bf16), shape((rows, D), f32), shape((rows, D), bf16)),
        (lengths, core, n2, h1, gain3, encoded, *u_cross),
        [wide, wide] + WEIGHTS,
        grid=(count,),
        in_specs=[SMEM] * 2 + [full, full, LINE, ENC_BLOCK, ANY, ANY],
        out_specs=[ENC_BLOCK, ENC_BLOCK, SEQ_BLOCK, SEQ_BLOCK, full, full, full])


def run_feed_forward(lengths, group_ids, group_steps, group_weights, tags, mask, out_grad, n3, h2,
                     gain3, u_ffn):
    rows = n3.shape[0]
    quarter = D // 4
    wide, low, flat = scratch_of(rows)
    full = whole((rows, D))
    column = whole((rows, 1))
    x_block = pl.BlockSpec((4, 1, quarter, D), lambda g: (0, g, 0, 0))
    r_block = pl.BlockSpec((1, 4, quarter, D), lambda g: (g, 1, 0, 0))
    return call(
        feed_forward, "feed_forward", 32, 60,
        (shape((rows, D), bf16), shape((8, 4, quarter, D), bf16),
         shape((rows, D), f32), shape((1, D), f32)),
        (lengths, group_ids, group_steps, group_weights, tags, mask, out_grad, n3, h2, gain3,
         u_ffn, u_ffn),
        [low, flat, flat, low, low, pltpu.VMEM((8, 4, quarter, D), bf16),
         pltpu.SemaphoreType.DMA((8,))],
        grid=(4,),
        in_specs=[SMEM] * 4 + [column, column, full, full, full, LINE, x_block, r_block],
        out_specs=[full, ANY, full, LINE])


def run_cross_backward(lengths, g2, crossed, cq, lse, ck, cv, encoded, n2, h1, gain2, core,
                       u_cross):
    rows = g2.shape[0]
    count = lengths.shape[0]
    wide, low, flat = scratch_of(rows)
    full = whole((rows, D))
    return call(
        cross_backward, "cross_backward", 42, 60,
        (shape(encoded.shape, bf16), shape(encoded.shape, bf16), shape(HALVES, bf16),
         shape(HALVES, bf16), shape((rows, D), f32), shape((1, D), f32)),
        (lengths, g2, crossed, cq, lse, ck, cv, encoded, n2, h1, gain2, core, *u_cross),
        [wide, wide, wide, pltpu.VMEM(encoded.shape, bf16), pltpu.VMEM(encoded.shape, bf16),
         low, low, flat, pltpu.VMEM(encoded.shape, bf16), low, flat,
         pltpu.SemaphoreType.DMA((11,))] + WEIGHTS,
        grid=(count,),
        in_specs=[SMEM, full, full, SEQ_BLOCK, SEQ_BLOCK, ENC_BLOCK, ENC_BLOCK, ANY, ANY,
                  ANY, LINE, SMEM, ANY, ANY],
        out_specs=[ANY, ANY, whole(HALVES), whole(HALVES), full, LINE])


def run_self_backward(lengths, g1, mixed, q, k, v, lse, n1, by_lag, core, u_self):
    rows = g1.shape[0]
    wide, low, flat = scratch_of(rows)
    return call(
        self_backward, "self_backward", 28, 60,
        (shape((rows, D), bf16), shape((rows, D), bf16), shape((rows, D), bf16),
         shape(HALVES, bf16), shape(HALVES, bf16), shape((HEADS, MAX_LEN), f32)),
        (lengths, g1, mixed, q, k, v, lse, n1, by_lag, core, *u_self),
        [wide, wide, wide, wide, wide, low, SQUARE, SQUARE]
        + [pltpu.VMEM(value.shape, value.dtype) for value in (q, k, v, lse)]
        + [pltpu.SemaphoreType.DMA((4,))] + WEIGHTS,
        in_specs=[SMEM, VMEM, VMEM, ANY, ANY, ANY, ANY, VMEM, VMEM, SMEM, ANY, ANY], out_specs=[VMEM] * 6)


def run_hidden_back(core, g1, hidden, gain1, dq, dk, dv, gg2, gg3, grad_lag, u_self):
    rows = g1.shape[0]
    wide, low, flat = scratch_of(rows)
    return call(
        hidden_back, "hidden_back", 8, 60,
        (shape((rows, D), f32), shape((SMALL, D), bf16)),
        (core, g1, hidden, gain1, dq, dk, dv, gg2, gg3, grad_lag, *u_self),
        [flat, pltpu.VMEM((SMALL, D), f32)] + WEIGHTS,
        in_specs=[SMEM] + [VMEM] * 9 + [ANY] * 2, out_specs=[VMEM] * 2)


def run_encoded_back(core, dck, dcv, u_cross, before=None):
    half = dck.shape[0] // ENC_LEN // 2
    first = 0 if before is None else half
    block = pl.BlockSpec((ENC_LEN, D), lambda s: (s + first, 0))
    more = () if before is None else (before,)
    return call(
        encoded_back, "encoded_back", 6, 60,
        (shape(dck.shape, f32),),
        (core, dck, dcv, *u_cross, *more),
        WEIGHTS,
        grid=(half,),
        input_output_aliases={} if before is None else {5: 0},
        in_specs=[SMEM, block, block, ANY, ANY] + [ANY] * len(more), out_specs=[block])


def add_all(parts):
    total = parts[0].astype(f32)
    for part in parts[1:]:
        total = total + part.astype(f32)
    return total.astype(bf16)


def tie(value, *after):
    return lax.optimization_barrier((value, *after))[0]


def tie_all(values, *after):
    return lax.optimization_barrier((*values, *after))[:len(values)]


def per_device(
    hidden, encoded, out_grad, lengths, group_ids, id_tags, loss_mask, group_steps, group_weights,
    gain_self, gain_cross, gain_ffn, rel_bias,
    query_weight, key_weight, value_weight, output_weight,
    cross_query, cross_key, cross_value, cross_output, expand_weight, reduce_weight,
):
    rows = hidden.shape[0]
    count = lengths.shape[0]
    quarter = D // 4
    routes = Routes()
    core = routes.core.reshape(1)
    size = D // routes.parts

    def piece_of(parts, index, extent):
        return lax.dynamic_slice_in_dim(jnp.concatenate(parts, 0), index * extent, extent, 0)

    small = jnp.concatenate([gain_self, gain_cross, gain_ffn, rel_bias.reshape(-1)])
    small_row = jnp.pad(small[None], ((0, 15), (0, D - small.shape[0])))
    own = piece_of([query_weight, key_weight, value_weight, output_weight],
                   routes.piece_index(), size)
    first = lax.all_gather(jnp.concatenate([own, small_row], 0)[None], "fsdp", axis=0, tiled=True)
    small = first[:, size, :small.shape[0]].astype(f32)
    cross_own = piece_of([cross_query, cross_key, cross_value, cross_output],
                         routes.piece_index(), size)
    self_piece = first[:, :size]
    cross_got = routes.shift_all(tie(cross_own, first))
    for step in routes.steps[:0:-1]:
        self_piece = routes.join(self_piece, routes.swap(self_piece, step), step)
    start_ffn = first
    cross_piece = routes.stack_shards(tie_all(cross_got, self_piece))
    for step in routes.steps[:0:-1]:
        cross_piece = routes.join(cross_piece, routes.swap(cross_piece, step), step)
    step = routes.steps[0]
    self_piece = routes.join(self_piece, tie(routes.swap(self_piece, step), cross_piece), step)
    self_other = routes.swap_core(self_piece)
    cross_last = routes.swap(cross_piece, routes.steps[0])
    u_self = [half.reshape(HALVES) for half in (self_piece, self_other)]
    ratio = routes.parts // 8
    slot, offset = routes.dp // ratio, (routes.dp % ratio) * (quarter // ratio)
    own = jnp.where(
        slot < 4,
        lax.dynamic_slice(expand_weight, (offset, jnp.minimum(slot, 3) * D), (quarter // ratio, D)),
        lax.dynamic_slice_in_dim(
            reduce_weight, jnp.maximum(slot - 4, 0) * quarter + offset, quarter // ratio, 0))
    u_ffn = lax.all_gather(tie(own, start_ffn), ("fsdp", "dp"), axis=0, tiled=True)
    u_ffn = u_ffn.reshape(4, 8, quarter, D)

    gain1 = small[:, 0:quarter].reshape(1, D)
    gain2 = small[:, quarter:2 * quarter].reshape(1, D)
    gain3 = small[:, 2 * quarter:3 * quarter].reshape(1, D)
    rel = small[:, 3 * quarter:].reshape(HEADS, BUCKETS)
    table = bucket_table()
    by_lag = jnp.dot(rel, jnp.asarray(table), precision=lax.Precision.HIGHEST)
    turned = jnp.dot(
        rel, jnp.asarray(table[:, (-np.arange(MAX_LEN)) % MAX_LEN]), precision=lax.Precision.HIGHEST)

    n1, q, k, v, lse, mixed, h1, n2 = run_self_forward(
        lengths, core, hidden, gain1, gain2, turned, u_self)
    cross_piece = routes.join(cross_piece, tie(cross_last, n2), routes.steps[0])
    u_cross = [half.reshape(HALVES) for half in (cross_piece, routes.swap_core(cross_piece))]
    ck, cv, cq, cross_lse, crossed, h2, n3 = run_cross_forward(
        lengths, core, n2, h1, gain3, encoded, u_cross)
    layer_output, grad_ffn, g2, gg3 = run_feed_forward(
        lengths, group_ids, group_steps, group_weights, id_tags[:, None], loss_mask[:, None],
        out_grad, n3, h2, gain3, u_ffn)
    if routes.parts > 8:
        grad_ffn = grad_ffn.reshape(8, 4, routes.parts // 8, -1, D).swapaxes(1, 2)
    ffn_piece = lax.psum_scatter(
        grad_ffn.reshape(-1, D), "dp", scatter_dimension=0, tiled=True)

    dck, dcv, keep, send, g1, gg2 = run_cross_backward(
        lengths, g2, crossed, cq, cross_lse, ck, cv, encoded, n2, h1, gain2, core, u_cross)
    first_step, later_steps = routes.steps[0], routes.steps[1:]
    half = (4, D // 2, D)
    got = routes.swap_core(send.reshape(half))
    (grad_encoded,) = run_encoded_back(core, tie(dck, g1), dcv, u_cross)
    cross_total = add(keep.reshape(half), tie(got, grad_encoded))
    cross_keep, cross_got = routes.halve(cross_total, first_step)

    ffn_half = ffn_piece
    ffn_piece = lax.psum_scatter(ffn_piece, "fsdp", scatter_dimension=0, tiled=True)
    ffn = lax.all_gather(ffn_piece, "dp", axis=0, tiled=True).astype(f32)

    dq, dk, dv, keep, send, grad_lag = run_self_backward(
        lengths, tie(g1, cross_total), mixed, q, k, v, lse, n1, by_lag, core, u_self)
    cross_total = add(cross_keep, tie(cross_got, dq))
    got = routes.swap_core(tie(send, cross_total, ffn_half).reshape(half))
    for step in later_steps:
        cross_keep, cross_got = routes.halve(cross_total, step)
        if step is not later_steps[-1]:
            cross_total = add(cross_keep, cross_got)
    self_total = add(keep.reshape(half), tie(got, ffn_half))
    self_keep, self_got = routes.halve(self_total, first_step)

    grad_hidden, small = run_hidden_back(
        core, g1, hidden, gain1, tie(dq, self_total), dk, dv, gg2, gg3, grad_lag, u_self)
    cross_total = add(cross_keep, tie(cross_got, grad_hidden))
    self_total = add(self_keep, tie(self_got, grad_hidden, cross_total, ffn_piece))
    first_total = self_total
    cross_parts = routes.send_shards(tie(cross_total, self_total))
    for step in later_steps:
        self_keep, self_got = routes.halve(self_total, step)
        if step is not later_steps[-1]:
            self_total = add(self_keep, self_got)
    (grad_encoded,) = run_encoded_back(
        core, tie(dck, first_total), dcv, u_cross, grad_encoded)
    self_total = add(self_keep, tie(self_got, grad_encoded))
    self_parts = routes.send_shards(jnp.concatenate(
        [self_total, jnp.broadcast_to(small[None], (4, SMALL, D))], axis=1))
    piece = jnp.concatenate(
        [add_all(self_parts), add_all(tie_all(cross_parts, self_total))], axis=0)

    mine, other = routes.collect(piece[None])
    mine = mine.reshape(routes.parts // 2, 2 * size + SMALL, D)
    other = other.reshape(routes.parts // 2, 2 * size + SMALL, D)
    small = jnp.sum(mine[:, size:size + SMALL].astype(f32), 0) + jnp.sum(
        other[:, size:size + SMALL].astype(f32), 0)
    gains = lax.dynamic_slice_in_dim(small[0:3], routes.z * quarter, quarter, 1)
    lag = lax.dynamic_slice_in_dim(small[3:3 + HEADS, :MAX_LEN], routes.z * (HEADS // 4), HEADS // 4, 0)
    grad_rel = lax.dot_general(
        lag, jnp.asarray(table), (((1,), (1,)), ((), ())), precision=lax.Precision.HIGHEST)

    def weight_grads(first):
        own = [value[:, first:first + size].reshape(2, quarter, D) for value in (mine, other)]
        lows = jnp.where(routes.core == 0, own[0], own[1]).astype(f32)
        highs = jnp.where(routes.core == 0, own[1], own[0]).astype(f32)
        return lows[0], lows[1], highs[0], highs[1]

    return (
        layer_output,
        grad_hidden,
        grad_encoded,
        gains[0],
        gains[1],
        gains[2],
        grad_rel,
        *weight_grads(0),
        *weight_grads(size + SMALL),
        jnp.concatenate([ffn[g * quarter:(g + 1) * quarter] for g in range(4)], axis=1),
        ffn[D:],
    )


def solution(mesh):
    rows = P(("dp", "fsdp"), None)
    flat = P(("dp", "fsdp"))
    shard = P("fsdp", None)
    line = P("fsdp")
    return jax.shard_map(
        per_device,
        mesh=mesh,
        in_specs=(rows, rows, rows, flat, flat, flat, flat, P(), P(), line, line, line) + (shard,) * 11,
        out_specs=(rows, rows, rows, line, line, line) + (shard,) * 11,
        check_vma=False,
    )
```
